512 devices in a mesh: tm: 128 (over z, y, core), plane: 4 (over x).
Axes of the slice: x: 4, y: 8, z: 8, core: 2. Of those that a mesh axis runs over, the one named last changes fastest.
Arguments:
- source: float32 [128, 16, 256, 256], P('tm', 'plane'), may hold values from -6 to 6
- potential: float32 [16, 256, 256], P('plane'), may hold values from 0.1 to 10
- level_shift: float32 [4], replicated, may hold values from 0.5 to 16
Outputs:
- result: float32 [128, 16, 256, 256], P('tm', 'plane')
The draws below stay inside these ranges and needn't reach their ends.
All inputs are finite; a program needn't handle non-finite values.
Results may differ from the reference program's by a relative error of at most 0.00002.
Values sent between devices are 32-bit elements; how exact they have to be, the bound alone decides.
A program may use at most 192 MiB of HBM per device.

```python
import math
import jax
import jax.numpy as jnp
from jax import lax

NY = 256
NZ = 256
CB = 8
NT = 128
NX = 16


def block_scale(rng, dims, cuts, low, largest):
    level, own = 1.0, jax.random.fold_in(rng, 6)
    for axis_at, blocks in cuts:
        steps = jnp.exp(jax.random.uniform(jax.random.fold_in(own, axis_at), (blocks,), jnp.float32, low / len(cuts), largest / len(cuts)))
        level = level * jnp.repeat(steps, dims[axis_at] // blocks).reshape([-1 if axis == axis_at else 1 for axis in range(len(dims))])
    return level


def scatter_about(rng, extent, deviation, limit, split=(), held_as=jnp.bfloat16):
    gain = block_scale(rng, extent, split, -0.22, 0.18) if split else 1.0
    drawn = jax.random.normal(rng, extent, jnp.float32) * deviation * gain
    return jnp.minimum(jnp.maximum(drawn, -limit), limit).astype(held_as)


def setup_inputs(seed: int = 0) -> dict:
    streams_of = jax.random.split(jax.random.key(seed), 4)
    return {
        "source": scatter_about(streams_of[0], (NT, NX, NY, NZ), 1.0, 6.0, ((0, 128), (1, 4)), jnp.float32),
        "potential": jnp.clip(jnp.exp(math.log(10.0) - 4.6051702 * jax.random.uniform(streams_of[1], (NX, NY, NZ), jnp.float32) ** block_scale(streams_of[1], (NX, NY, NZ), ((0, 4),), -0.2, 0.2)), 0.1, 10.0),
        "level_shift": jnp.clip(jnp.exp(jax.random.uniform(streams_of[2], (4,), jnp.float32, math.log(0.5), math.log(16.0))), 0.5, 16.0),
    }


OMEGA = 0.8
INV_ROOT = 1.0 / math.sqrt(2.0)

def haar_level(values, level):
    count = values.shape[0]
    stride = 1 << level
    grouped = values.reshape((count // (2 * stride), 2, stride) + values.shape[1:])
    lower = grouped[:, 0]
    upper = grouped[:, 1]
    mixed_low = (lower + upper) * INV_ROOT
    mixed_up = (lower - upper) * INV_ROOT
    leading = (jnp.arange(stride) == 0).reshape((1, stride) + (1,) * (values.ndim - 1))
    lower = jnp.where(leading, mixed_low, lower)
    upper = jnp.where(leading, mixed_up, upper)
    return jnp.stack([lower, upper], axis=1).reshape(values.shape)

def neighbours(extended):
    inner = extended[1:-1]
    padded = jnp.pad(inner, ((0, 0), (1, 1), (1, 1)))
    total = extended[2:] + extended[:-2]
    total = total + padded[:, 2:, 1:-1] + padded[:, :-2, 1:-1]
    return total + padded[:, 1:-1, 2:] + padded[:, 1:-1, :-2]

def block_sum(field):
    planes, rows, cols = field.shape
    return field.reshape(planes, rows // CB, CB, cols // CB, CB).sum(axis=(0, 2, 4))

def coarse_fix(coarse_rem, coarse_pot, shift_now, planes_all):
    coarse_diag = coarse_pot + shift_now * (CB * CB * planes_all) + 2.0 * CB * CB + 4.0 * CB * planes_all
    coarse_one = coarse_rem / coarse_diag
    padded = jnp.pad(coarse_one, 1)
    beside_all = padded[2:, 1:-1] + padded[:-2, 1:-1] + padded[1:-1, 2:] + padded[1:-1, :-2]
    applied = coarse_diag * coarse_one - CB * planes_all * beside_all
    return coarse_one + (coarse_rem - applied) / coarse_diag

def prolong(coarse):
    rows, cols = coarse.shape
    return jnp.broadcast_to(coarse[:, None, :, None], (rows, CB, cols, CB)).reshape(rows * CB, cols * CB)

def level_of(position):
    return (position % 2 == 0).astype(jnp.int32) + (position % 4 == 0).astype(jnp.int32) + (position % 8 == 0).astype(jnp.int32)

def reference(source, potential, level_shift):
    waves = source
    for level in range(3):
        waves = haar_level(waves, level)
    level_id = level_of(jnp.arange(NT, dtype=jnp.int32))
    shifts_all = jnp.take(level_shift, level_id)
    coarse_pot = block_sum(potential)
    flat_pad = ((1, 1), (0, 0), (0, 0))

    def solve_one(item):
        wave_src, shift_now = item
        diagonal = 6.0 + potential + shift_now
        first_pass = OMEGA * wave_src / diagonal
        second_pass = first_pass + OMEGA * (wave_src - (diagonal * first_pass - neighbours(jnp.pad(first_pass, flat_pad)))) / diagonal
        remainder = wave_src - (diagonal * second_pass - neighbours(jnp.pad(second_pass, flat_pad)))
        correction = coarse_fix(block_sum(remainder), coarse_pot, shift_now, NX)
        return second_pass + prolong(correction)[None]
    result = lax.map(solve_one, (waves, shifts_all))
    for level in (2, 1, 0):
        result = haar_level(result, level)
    return result
```

```python
import math

import jax
import jax.numpy as jnp
from jax import lax
from jax.experimental import pallas as pl
from jax.experimental.pallas import tpu as pltpu
from jax.sharding import PartitionSpec as P

F32 = jnp.float32
MESH = pl.DeviceIdType.MESH
ROOT = 1.0 / math.sqrt(2.0)
OMEGA = 0.8
PLANES = (0, 3, 1, 2)
SLOT = {plane: slot for slot, plane in enumerate(PLANES)}
LEVELS = (3, 1, 2, 1)


def dot(a, b):
    return jnp.dot(a, b, precision=lax.Precision.HIGHEST, preferred_element_type=F32)


def iota(shape, dim):
    return lax.broadcasted_iota(jnp.int32, shape, dim)


def ones_where(mask):
    return jnp.where(mask, 1.0, 0.0).astype(F32)


def beside_yz(ext):
    rows = ext.shape[0] - 16
    mid = ext[8 : 8 + rows]
    up = pltpu.roll(ext, 1, 0)[8 : 8 + rows]
    down = pltpu.roll(ext, rows + 15, 0)[8 : 8 + rows]
    col = iota(mid.shape, 1)
    left = jnp.where(col == 0, 0.0, pltpu.roll(mid, 1, 1))
    right = jnp.where(col == 255, 0.0, pltpu.roll(mid, 255, 1))
    return mid, (up + down) + (left + right)


def kernel(
    shift_ref, source, potential, out,
    own, other, pot, s_buf, fd, sd, strip, rs, rstrip, fs, r_s, r_strip, hd, hs, sb, bk,
    t_d, x_d, t_s, x_s, pot_all, coarse, coarse_x, total, tr, dr, xs, xd, mine, yours,
    l_sem, p_sem, s0, r0, sy, ry, st, rt, sxd, rxd, sxs, rxs, sp, rp, sc, rc, sg, rg, sdp, rdp, sbk, rbk, so, ro, lo,
):
    t, x = lax.axis_index("tm"), lax.axis_index("plane")
    e = t % 8
    base = t - e
    k, c = e % 2, e // 2
    partner = t + 1 - 2 * k
    chips = [(c + m) % 4 for m in (1, 2, 3)]
    x_peers = [(x + m) % 4 for m in (1, 2, 3)]
    group = [base + (e + m) % 8 for m in range(1, 8)]

    barrier = pltpu.get_barrier_semaphore()
    for peer in group:
        pl.semaphore_signal(barrier, inc=1, device_id=(peer, x), device_id_type=MESH)
    for peer in x_peers:
        pl.semaphore_signal(barrier, inc=1, device_id=(t, peer), device_id_type=MESH)

    rows_from = pl.multiple_of(120 * k, 8)
    rows_to = pl.multiple_of(8 - 8 * k, 8)
    loads = []
    for slot, plane in enumerate(PLANES):
        load = pltpu.make_async_copy(
            source.at[0, plane, pl.ds(rows_from, 136), :],
            own.at[slot, pl.ds(rows_to, 136), :],
            l_sem.at[slot],
        )
        load.start()
        loads.append(load)
    pot_loads = []
    for slot, plane in enumerate(PLANES):
        load = pltpu.make_async_copy(
            potential.at[plane, pl.ds(rows_from, 136), :],
            pot.at[slot, pl.ds(rows_to, 136), :],
            p_sem.at[slot],
        )
        load.start()
        pot_loads.append(load)
    blank = pl.multiple_of(136 * k, 8)
    for slot in range(4):
        own[slot, pl.ds(blank, 8), :] = jnp.zeros((8, 256), F32)
        other[slot, pl.ds(blank, 8), :] = jnp.zeros((8, 256), F32)
        pot[slot, pl.ds(blank, 8), :] = jnp.zeros((8, 256), F32)

    pl.semaphore_wait(barrier, 10)

    def remote(src, dst, send, recv, where):
        return pltpu.make_async_remote_copy(
            src_ref=src, dst_ref=dst, send_sem=send, recv_sem=recv, device_id=where, device_id_type=MESH
        )

    their_from = pl.multiple_of(120 - 120 * k, 8)
    their_to = pl.multiple_of(8 * k, 8)
    swaps = []
    for slot, plane in enumerate(PLANES):
        copy = remote(
            source.at[0, plane, pl.ds(their_from, 136), :],
            other.at[slot, pl.ds(their_to, 136), :],
            s0.at[slot], r0.at[slot], (partner, x),
        )
        copy.start()
        swaps.append(copy)

    lifts, strips = [], []
    for part in range(2):
        for slot in (2 * part, 2 * part + 1):
            loads[slot].wait()
            swaps[slot].wait_recv()
            s_buf[slot] = (own[slot] + other[slot]) * ROOT
        if part == 1:
            for q in range(4):
                for slot in range(4):
                    strip[q, slot : slot + 1, :] = s_buf[slot, 7 + 32 * q : 8 + 32 * q, :]
                    strip[q, 4 + slot : 5 + slot, :] = s_buf[slot, 40 + 32 * q : 41 + 32 * q, :]
            for m, chip in enumerate(chips):
                copy = remote(strip.at[chip], rstrip.at[c], st.at[m], rt.at[m], (base + 2 * chip + k, x))
                copy.start()
                strips.append(copy)
        for m, chip in enumerate(chips):
            copy = remote(
                s_buf.at[2 * part : 2 * part + 2, pl.ds(pl.multiple_of(8 + 32 * chip, 8), 32), :],
                rs.at[c, 2 * part : 2 * part + 2],
                sy.at[3 * part + m], ry.at[3 * part + m], (base + 2 * chip + k, x),
            )
            copy.start()
            lifts.append(copy)

    sign = (1 - 2 * k).astype(F32)
    scale = ROOT * sign
    shift_0 = shift_ref[0]
    for slot in range(4):
        pot_loads[slot].wait()
        fd[slot] = (own[slot] - other[slot]) * scale * (OMEGA / (6.0 + pot[slot] + shift_0))
    halo_d = [
        remote(fd.at[0, 8:136, :], hd.at[1], sxd.at[0], rxd.at[0], (t, (x + 3) % 4)),
        remote(fd.at[1, 8:136, :], hd.at[0], sxd.at[1], rxd.at[1], (t, (x + 1) % 4)),
    ]
    for copy in halo_d:
        copy.start()

    lane_block = ones_where(iota((256, 128), 0) // 8 == iota((256, 128), 1) % 32)
    row_block = ones_where(iota((24, 144), 1) // 8 == iota((24, 144), 0))
    pot_sum = pot[0] + pot[1] + pot[2] + pot[3]
    pot_all[0] = dot(row_block, dot(pot_sum, lane_block))
    pots = []
    for m, peer in enumerate(x_peers):
        copy = remote(pot_all.at[0], pot_all.at[m + 1], sp.at[m], rp.at[m], (t, peer))
        copy.start()
        pots.append(copy)

    quarter = pl.multiple_of(8 + 32 * c, 8)
    for slot in range(4):
        here = 6.0 + pot[slot, pl.ds(quarter, 32), :]
        for level in (1, 2, 3):
            r_s[level - 1, slot] = OMEGA / (here + shift_ref[level])
        rs[c, slot] = s_buf[slot, pl.ds(quarter, 32), :]
        above = pot[slot, pl.ds(pl.multiple_of(32 * c, 8), 8), :]
        below = pot[slot, pl.ds(pl.multiple_of(40 + 32 * c, 8), 8), :]
        for level in (1, 2, 3):
            r_strip[level - 1, slot : slot + 1, :] = OMEGA / (6.0 + above[7:8] + shift_ref[level])
            r_strip[level - 1, 4 + slot : 5 + slot, :] = OMEGA / (6.0 + below[0:1] + shift_ref[level])
    rstrip[c] = strip[c]

    keep_low, keep_high = ones_where(x > 0), ones_where(x < 3)
    edge_low, edge_high = 1.0 - keep_low, 1.0 - keep_high
    for copy in halo_d:
        copy.wait_recv()

    def odd_rows(step, _):
        at = pl.multiple_of(32 * step, 8)
        mids = {}
        summed = jnp.zeros((32, 256), F32)
        waves = jnp.zeros((32, 256), F32)
        edges = jnp.zeros((32, 256), F32)
        center = pl.ds(pl.multiple_of(at + 8, 8), 32)
        for plane in range(4):
            slot = SLOT[plane]
            mid, beside = beside_yz(fd[slot, pl.ds(at, 48), :])
            if plane > 0:
                low = fd[SLOT[plane - 1], center, :]
            else:
                low = hd[0, pl.ds(at, 32), :] * keep_low
            if plane < 3:
                high = fd[SLOT[plane + 1], center, :]
            else:
                high = hd[1, pl.ds(at, 32), :] * keep_high
            diagonal = 6.0 + pot[slot, center, :] + shift_0
            second = 1.2 * mid + (OMEGA / diagonal) * (beside + (low + high))
            sd[slot, pl.ds(at, 32), :] = second
            q = second - OMEGA * mid
            summed = summed + q
            waves = waves + (own[slot, center, :] - other[slot, center, :])
            if plane == 0:
                edges = edges + q * edge_low
            if plane == 3:
                edges = edges + q * edge_high
        t_d[pl.ds(at, 32), :] = summed
        x_d[pl.ds(at, 32), :] = (0.04 * scale) * waves - edges
        return 0

    lax.fori_loop(0, 4, odd_rows, 0)

    in_block = iota((256, 128), 0) // 8 == iota((256, 128), 1)
    z_at, z_block = iota((256, 128), 0), iota((256, 128), 1)
    block = ones_where(in_block)
    around = (
        2.0 * block
        + ones_where((z_at + 7) // 8 == z_block + 1)
        + ones_where((z_at + 1) // 8 == z_block)
    )
    around = jnp.where(z_block < 32, around, 0.0)
    y_at, y_row = iota((24, 128), 1), iota((24, 128), 0)
    odd_in = ones_where((y_at // 8 + 1 == y_row))
    odd_beside = ones_where((y_at + 7) // 8 == y_row) + ones_where((y_at + 1) // 8 + 1 == y_row)
    t_now = t_d[...]
    coarse[8:32, :] = dot(odd_in, dot(x_d[...], block) + dot(t_now, around)) + dot(odd_beside, dot(t_now, block))

    def even_first(slot):
        s_0, s_1, s_2, s_3 = (rs[i, slot] for i in range(4))
        u_a, u_b = (s_0 + s_1) * ROOT, (s_2 + s_3) * ROOT
        waves = ((u_a + u_b) * ROOT, (s_0 - s_1) * ROOT, (u_a - u_b) * ROOT, (s_2 - s_3) * ROOT)
        for j in range(4):
            fs[j, slot, 8:40, :] = waves[j] * r_s[LEVELS[j] - 1, slot]
            if slot == 0:
                x_s[j] = waves[j]
            else:
                x_s[j] += waves[j]

    for m in range(3):
        lifts[m].wait_recv()
    even_first(0)
    even_first(1)
    halo_s = [
        remote(fs.at[:, 0, 8:40, :], hs.at[1], sxs.at[0], rxs.at[0], (t, (x + 3) % 4)),
        remote(fs.at[:, 1, 8:40, :], hs.at[0], sxs.at[1], rxs.at[1], (t, (x + 1) % 4)),
    ]
    for copy in halo_s:
        copy.start()
    for copy in strips:
        copy.wait_recv()
    s_0, s_1, s_2, s_3 = (rstrip[i] for i in range(4))
    u_a, u_b = (s_0 + s_1) * ROOT, (s_2 + s_3) * ROOT
    rims = ((u_a + u_b) * ROOT, (s_0 - s_1) * ROOT, (u_a - u_b) * ROOT, (s_2 - s_3) * ROOT)
    for j in range(4):
        rim = rims[j] * r_strip[LEVELS[j] - 1]
        for slot in range(4):
            fs[j, slot, 7:8, :] = rim[slot : slot + 1]
            fs[j, slot, 40:41, :] = rim[4 + slot : 5 + slot]
    for m in range(3):
        lifts[3 + m].wait_recv()
    even_first(2)
    even_first(3)

    def even_second(slot):
        plane = PLANES[slot]
        seconds = []
        for j in range(4):
            mid, beside = beside_yz(fs[j, slot])
            if plane > 0:
                low = fs[j, SLOT[plane - 1], 8:40, :]
            else:
                low = hs[0, j] * keep_low
            if plane < 3:
                high = fs[j, SLOT[plane + 1], 8:40, :]
            else:
                high = hs[1, j] * keep_high
            second = 1.2 * mid + r_s[LEVELS[j] - 1, slot] * (beside + (low + high))
            q = second - OMEGA * mid
            if slot == 2:
                t_s[j] = q
                x_s[j] = 0.04 * x_s[j]
            else:
                t_s[j] += q
            if plane == 0:
                x_s[j] -= q * edge_low
            if plane == 3:
                x_s[j] -= q * edge_high
            seconds.append(second)
        u_a, u_b = (seconds[0] + seconds[2]) * ROOT, (seconds[0] - seconds[2]) * ROOT
        sb[0, slot] = (u_a + seconds[1]) * ROOT
        sb[1, slot] = (u_a - seconds[1]) * ROOT
        sb[2, slot] = (u_b + seconds[3]) * ROOT
        sb[3, slot] = (u_b - seconds[3]) * ROOT

    backs = {}
    own_rows = pl.ds(pl.multiple_of(32 * c, 8), 32)
    for part in (1, 0):
        if part == 0:
            for copy in halo_s:
                copy.wait_recv()
        even_second(2 * part)
        even_second(2 * part + 1)
        for m, chip in enumerate(chips):
            copy = remote(
                sb.at[chip, 2 * part : 2 * part + 2],
                bk.at[2 * part : 2 * part + 2, own_rows, :],
                sbk.at[3 * part + m], rbk.at[3 * part + m], (base + 2 * chip + k, x),
            )
            copy.start()
            backs[part, m] = copy
    for slot in range(4):
        bk[slot, own_rows, :] = sb[c, slot]

    y_at, y_row = iota((32, 128), 1), iota((32, 128), 0)
    same = y_at // 32 == y_row // 8
    y_at, y_row = y_at % 32, y_row % 8
    even_in = ones_where(same & (y_at // 8 + 1 == y_row))
    even_beside = ones_where(same & ((y_at + 7) // 8 == y_row)) + ones_where(same & ((y_at + 1) // 8 + 1 == y_row))
    t_now = t_s[...].reshape(128, 256)
    sums = dot(even_in, dot(x_s[...].reshape(128, 256), block) + dot(t_now, around)) + dot(even_beside, dot(t_now, block))
    packed = sums[0:8]
    for j in (1, 2, 3):
        packed = packed + pltpu.roll(sums[8 * j : 8 * j + 8], 32 * j, 1)
    coarse[0:8, :] = packed
    reduces = []
    for m, peer in enumerate(x_peers):
        copy = remote(coarse, coarse_x.at[m], sc.at[m], rc.at[m], (t, peer))
        copy.start()
        reduces.append(copy)
    for copy in pots:
        copy.wait_recv()
    for copy in reduces:
        copy.wait_recv()
    total[...] = (coarse[...] + coarse_x[0]) + (coarse_x[1] + coarse_x[2])
    gathers = []
    for m, peer in enumerate(group):
        copy = remote(total.at[0:8, :], tr.at[e], sg.at[m], rg.at[m], (peer, x))
        copy.start()
        gathers.append(copy)
    pair = remote(total.at[8:32, :], dr, sdp, rdp, (partner, x))
    pair.start()
    tr[e] = total[0:8, :]
    coarse_pot = (pot_all[0] + pot_all[1]) + (pot_all[2] + pot_all[3])
    for copy in gathers:
        copy.wait_recv()
    pair.wait_recv()

    row, col = iota((24, 64), 0), iota((24, 64), 1)
    sender, r = col // 8, col % 8
    where = 16 * (sender % 2) + 4 * (sender // 2) - 1 + r
    pick = ones_where((r < 6) & (where >= 0) & (where < 32) & (where == 16 * k - 1 + row))
    even_rem = dot(pick, tr[...].reshape(64, 128))
    row, col = iota((24, 24), 0), iota((24, 24), 1)
    where = 16 * (1 - k) - 1 + col
    pick = ones_where((col < 18) & (where >= 0) & (where < 32) & (where == 16 * k - 1 + row))
    row = iota((24, 128), 0)
    lane = iota((24, 128), 1)
    inside = (row < 18) & (16 * k - 1 + row >= 0) & (16 * k - 1 + row < 32)
    odd_rem = jnp.where(inside, total[8:32, :], 0.0) + dot(pick, dr[...])
    coef = lane // 32
    shifts = jnp.where(
        coef == 0, shift_ref[3], jnp.where(coef == 2, shift_ref[2], shift_ref[1])
    )

    def coarse_fix(rem, shift):
        diag = coarse_pot + shift * 1024.0 + 640.0
        one = rem / diag
        up, down = pltpu.roll(one, 1, 0), pltpu.roll(one, 23, 0)
        left = jnp.where(lane % 32 == 0, 0.0, pltpu.roll(one, 1, 1))
        right = jnp.where(lane % 32 == 31, 0.0, pltpu.roll(one, 127, 1))
        applied = diag * one - 128.0 * ((up + down) + (left + right))
        return one + (rem - applied) / diag

    half = jnp.where(coef == 2, jnp.where(c < 2, 0.5, -0.5), 0.5)
    detail = jnp.where(coef == 1, jnp.where(c == 0, ROOT, jnp.where(c == 1, -ROOT, 0.0)), 0.0)
    detail = detail + jnp.where(coef == 3, jnp.where(c == 2, ROOT, jnp.where(c == 3, -ROOT, 0.0)), 0.0)
    weight = jnp.where(coef % 2 == 0, half, detail)
    even_fix = coarse_fix(even_rem, shifts) * weight
    odd_fix = jnp.where(lane < 32, coarse_fix(odd_rem, shift_0), 0.0)
    widen = ones_where(iota((128, 256), 0) % 32 == iota((128, 256), 1) // 8)
    heighten = ones_where(iota((128, 24), 0) // 8 + 1 == iota((128, 24), 1))
    xs[...] = dot(heighten, dot(even_fix, widen))
    xd[...] = dot(heighten, dot(odd_fix, widen)) * sign

    half_rows = pl.ds(pl.multiple_of(128 * k, 8), 128)
    sends, stores = [], []
    for part in (1, 0):
        for m in range(3):
            backs[part, m].wait_recv()
        for slot in (2 * part, 2 * part + 1):
            even = bk[slot] + xs[...]
            odd = sd[slot] * sign + xd[...]
            yours[slot] = (even - odd) * ROOT
            there = out.at[0, PLANES[slot], half_rows, :]
            copy = remote(yours.at[slot], there, so.at[slot], ro.at[slot], (partner, x))
            copy.start()
            sends.append(copy)
            mine[slot] = (even + odd) * ROOT
            copy = pltpu.make_async_copy(mine.at[slot], there, lo.at[slot])
            copy.start()
            stores.append(copy)

    for copy in swaps + lifts + strips + halo_d + halo_s + pots + reduces + gathers + [pair] + list(backs.values()):
        copy.wait_send()
    for copy in sends + stores:
        copy.wait()


def shards(source, potential, level_shift):
    dma = pltpu.SemaphoreType.DMA
    vmem = lambda *shape: pltpu.VMEM(shape, F32)
    scratch = dict(
        own=vmem(4, 144, 256), other=vmem(4, 144, 256), pot=vmem(4, 144, 256), s_buf=vmem(4, 144, 256),
        fd=vmem(4, 144, 256), sd=vmem(4, 128, 256), strip=vmem(4, 8, 256), rs=vmem(4, 4, 32, 256),
        rstrip=vmem(4, 8, 256), fs=vmem(4, 4, 48, 256), r_s=vmem(3, 4, 32, 256), r_strip=vmem(3, 8, 256),
        hd=vmem(2, 128, 256), hs=vmem(2, 4, 32, 256), sb=vmem(4, 4, 32, 256), bk=vmem(4, 128, 256),
        t_d=vmem(128, 256), x_d=vmem(128, 256), t_s=vmem(4, 32, 256), x_s=vmem(4, 32, 256),
        pot_all=vmem(4, 24, 128), coarse=vmem(32, 128), coarse_x=vmem(3, 32, 128), total=vmem(32, 128),
        tr=vmem(8, 8, 128), dr=vmem(24, 128), xs=vmem(128, 256), xd=vmem(128, 256),
        mine=vmem(4, 128, 256), yours=vmem(4, 128, 256),
        l_sem=dma((4,)), p_sem=dma((4,)), s0=dma((4,)), r0=dma((4,)), sy=dma((6,)), ry=dma((6,)),
        st=dma((3,)), rt=dma((3,)), sxd=dma((2,)), rxd=dma((2,)), sxs=dma((2,)), rxs=dma((2,)),
        sp=dma((3,)), rp=dma((3,)), sc=dma((3,)), rc=dma((3,)), sg=dma((7,)), rg=dma((7,)),
        sdp=dma(()), rdp=dma(()), sbk=dma((6,)), rbk=dma((6,)), so=dma((4,)), ro=dma((4,)), lo=dma((4,)),
    )
    return pl.pallas_call(
        kernel,
        out_shape=jax.ShapeDtypeStruct(source.shape, F32),
        in_specs=[
            pl.BlockSpec(memory_space=pltpu.SMEM),
            pl.BlockSpec(memory_space=pl.ANY),
            pl.BlockSpec(memory_space=pl.ANY),
        ],
        out_specs=pl.BlockSpec(memory_space=pl.ANY),
        scratch_shapes=list(scratch.values()),
        compiler_params=pltpu.CompilerParams(
            collective_id=0, has_side_effects=True, vmem_limit_bytes=40 * 2**20
        ),
        name="space_time_apply",
    )(level_shift, source, potential)


def solution(mesh):
    in_specs = (P("tm", "plane", None, None), P("plane", None, None), P())
    out_specs = P("tm", "plane", None, None)
    return jax.shard_map(shards, mesh=mesh, in_specs=in_specs, out_specs=out_specs, check_vma=False)
```

```python
import math

import jax
import jax.numpy as jnp
from jax import lax
from jax.experimental import pallas as pl
from jax.experimental.pallas import tpu as pltpu
from jax.sharding import PartitionSpec as P

F32 = jnp.float32
MESH = pl.DeviceIdType.MESH
ROOT = 1.0 / math.sqrt(2.0)
OMEGA = 0.8
PLANES = (0, 3, 1, 2)
SLOT = {plane: slot for slot, plane in enumerate(PLANES)}


def dot(a, b):
    return jnp.dot(a, b, precision=lax.Precision.HIGHEST, preferred_element_type=F32)


def iota(shape, dim):
    return lax.broadcasted_iota(jnp.int32, shape, dim)


def ones_where(mask):
    return jnp.where(mask, 1.0, 0.0).astype(F32)


def beside_yz(ext):
    rows = ext.shape[0] - 16
    mid = ext[8 : 8 + rows]
    up = pltpu.roll(ext, 1, 0)[8 : 8 + rows]
    down = pltpu.roll(ext, rows + 15, 0)[8 : 8 + rows]
    col = iota(mid.shape, 1)
    left = jnp.where(col == 0, 0.0, pltpu.roll(mid, 1, 1))
    right = jnp.where(col == 255, 0.0, pltpu.roll(mid, 255, 1))
    return mid, (up + down) + (left + right)


def kernel(
    shift_hbm, source, potential, out,
    shift_ref, own, other, pot, s_buf, rd, fd, sd, strip, nb, nstrip, u_buf, fv, rv, sv, ustrip, nu, nustrip, fu, ru,
    hd, hv, hu, ub, give, bk, gives, t_d, x_d, t_v, x_v, t_u, x_u, pot_all, coarse, coarse_x, total, tr, pick,
    xs, xd, mine, yours,
    h_sem, l_sem, p_sem, s0, r0, s1, r1, s2, r2, st, rt, su, ru_sem, sx, rx, sp, rp, sc, rc, sg, rg,
    sb2, rb2, sb1, rb1, so, ro, lo,
):
    t, x = lax.axis_index("tm"), lax.axis_index("plane")
    e = t % 8
    k, c = e % 2, e // 2
    b, p = c % 2, c // 2
    partner = t + 1 - 2 * k
    near = t + 2 - 4 * b
    far = t + 4 - 8 * p
    x_peers = [(x + m) % 4 for m in (1, 2, 3)]
    group = [t - e + (e + m) % 8 for m in range(1, 8)]

    barrier = pltpu.get_barrier_semaphore()
    for peer in group:
        pl.semaphore_signal(barrier, inc=1, device_id=(peer, x), device_id_type=MESH)
    for peer in x_peers:
        pl.semaphore_signal(barrier, inc=1, device_id=(t, peer), device_id_type=MESH)

    def rows(start, count):
        return pl.ds(pl.multiple_of(start, 8), count)

    def remote(src, dst, send, recv, where):
        copy = pltpu.make_async_remote_copy(
            src_ref=src, dst_ref=dst, send_sem=send, recv_sem=recv, device_id=where, device_id_type=MESH
        )
        copy.start()
        return copy

    def local(src, dst, sem):
        copy = pltpu.make_async_copy(src, dst, sem)
        copy.start()
        return copy

    loads = [
        local(source.at[0, plane, rows(120 * k, 136), :], own.at[slot, rows(8 - 8 * k, 136), :], l_sem.at[slot])
        for slot, plane in enumerate(PLANES)
    ]
    shift_load = local(shift_hbm, shift_ref, h_sem)
    pot_loads = [
        local(potential.at[plane, rows(120 * k, 136), :], pot.at[slot, rows(8 - 8 * k, 136), :], p_sem.at[slot])
        for slot, plane in enumerate(PLANES)
    ]
    for slot in range(4):
        for ref in (own, other, pot):
            ref[slot, rows(136 * k, 8), :] = jnp.zeros((8, 256), F32)

    pl.semaphore_wait(barrier, 10)

    swaps = [
        remote(
            source.at[0, plane, rows(120 - 120 * k, 136), :], other.at[slot, rows(8 * k, 136), :],
            s0.at[slot], r0.at[slot], (partner, x),
        )
        for slot, plane in enumerate(PLANES)
    ]

    firsts = []
    for slot in range(4):
        loads[slot].wait()
        swaps[slot].wait_recv()
        s_buf[slot] = (own[slot] + other[slot]) * ROOT
        if slot == 3:
            for q in range(2):
                for i in range(4):
                    strip[q, i : i + 1, :] = s_buf[i, 7 + 64 * q : 8 + 64 * q, :]
                    strip[q, 4 + i : 5 + i, :] = s_buf[i, 72 + 64 * q : 73 + 64 * q, :]
            strip_1 = remote(strip.at[1 - b], nstrip, st, rt, (near, x))
        firsts.append(
            remote(s_buf.at[slot, rows(72 - 64 * b, 64), :], nb.at[slot], s1.at[slot], r1.at[slot], (near, x))
        )

    sign = (1 - 2 * k).astype(F32)
    near_sign = (1 - 2 * b).astype(F32)
    far_sign = (1 - 2 * p).astype(F32)
    scale = ROOT * sign
    keep_low, keep_high = ones_where(x > 0), ones_where(x < 3)
    edge_low, edge_high = 1.0 - keep_low, 1.0 - keep_high
    shift_load.wait()
    shift_0 = shift_ref[0]
    for slot in range(4):
        pot_loads[slot].wait()
        rd[slot] = OMEGA / (6.0 + pot[slot] + shift_0)
        fd[slot] = (own[slot] - other[slot]) * scale * rd[slot]
    below, above = (t, (x + 3) % 4), (t, (x + 1) % 4)
    halo_d = [
        remote(fd.at[0, 8:136, :], hd.at[1], sx.at[0], rx.at[0], below),
        remote(fd.at[1, 8:136, :], hd.at[0], sx.at[1], rx.at[1], above),
    ]

    for slot in range(4):
        rv[slot] = OMEGA / (6.0 + pot[slot, rows(64 * b, 80), :] + shift_ref[1])
        here = 6.0 + pot[slot, rows(64 * b + 32 * p, 48), :]
        ru[0, slot] = OMEGA / (here + shift_ref[3])
        ru[1, slot] = OMEGA / (here + shift_ref[2])

    lane_block = ones_where(iota((256, 128), 0) // 8 == iota((256, 128), 1) % 32)
    row_block = ones_where(iota((24, 144), 1) // 8 == iota((24, 144), 0))
    pot_sum = (pot[0] + pot[1]) + (pot[2] + pot[3])
    pot_all[0] = dot(row_block, dot(pot_sum, lane_block))
    pots = [
        remote(pot_all.at[0], pot_all.at[m + 1], sp.at[m], rp.at[m], (t, peer)) for m, peer in enumerate(x_peers)
    ]

    seconds = []
    for slot in range(4):
        firsts[slot].wait_recv()
        here = s_buf[slot, rows(8 + 64 * b, 64), :]
        u_buf[slot, 8:72, :] = (here + nb[slot]) * ROOT
        seconds.append(
            remote(u_buf.at[slot, rows(40 - 32 * p, 32), :], nu.at[slot], s2.at[slot], r2.at[slot], (far, x))
        )
        detail = (here - nb[slot]) * (ROOT * near_sign)
        fv[slot, 8:72, :] = detail * rv[slot, 8:72, :]
        x_v[...] = detail if slot == 0 else x_v[...] + detail
        if slot == 1:
            halo_v = [
                remote(fv.at[0, 8:72, :], hv.at[1], sx.at[2], rx.at[2], below),
                remote(fv.at[1, 8:72, :], hv.at[0], sx.at[3], rx.at[3], above),
            ]
    strip_1.wait_recv()
    here = strip[b]
    sums = (here + nstrip[...]) * ROOT
    details = (here - nstrip[...]) * (ROOT * near_sign)
    for slot in range(4):
        u_buf[slot, 7:8, :] = sums[slot : slot + 1]
        u_buf[slot, 72:73, :] = sums[4 + slot : 5 + slot]
        fv[slot, 7:8, :] = details[slot : slot + 1] * rv[slot, 7:8, :]
        fv[slot, 72:73, :] = details[4 + slot : 5 + slot] * rv[slot, 72:73, :]
    for q in range(2):
        for i in range(4):
            ustrip[q, i : i + 1, :] = u_buf[i, 7 + 32 * q : 8 + 32 * q, :]
            ustrip[q, 4 + i : 5 + i, :] = u_buf[i, 40 + 32 * q : 41 + 32 * q, :]
    strip_2 = remote(ustrip.at[1 - p], nustrip, su, ru_sem, (far, x))

    row, col = iota((24, 192), 0), iota((24, 192), 1)
    sender, r = col // 24, col % 24
    sk, sc_, sb, sp_ = sender % 2, sender // 2, sender // 2 % 2, sender // 4
    wanted = 16 * k - 1 + row
    real = (wanted >= 0) & (wanted < 32) & (row < 18)
    pick[0] = ones_where(real & (r < 6) & (16 * sk + 8 * sb + 4 * sp_ - 1 + r == wanted))
    pick[1] = ones_where(real & (r < 10) & (sp_ == p) & (16 * sk + 8 * sb - 1 + r == wanted))
    pick[2] = ones_where(real & (r < 18) & (sc_ == c) & (16 * sk - 1 + r == wanted))

    z_at, z_block = iota((256, 128), 0), iota((256, 128), 1)
    block = ones_where(z_at // 8 == z_block)
    around = (
        2.0 * block
        + ones_where((z_at + 7) // 8 == z_block + 1)
        + ones_where((z_at + 1) // 8 == z_block)
    )
    around = jnp.where(z_block < 32, around, 0.0)

    def block_sums(fields, outer, out_rows, span, stride):
        shape = (out_rows, fields.shape[0])
        y_at, y_row = iota(shape, 1), iota(shape, 0)
        same = y_at // span == y_row // stride
        y_at, y_row = y_at % span, y_row % stride
        inner = ones_where(same & (y_at // 8 + 1 == y_row))
        beside = ones_where(same & ((y_at + 7) // 8 == y_row)) + ones_where(same & ((y_at + 1) // 8 + 1 == y_row))
        return dot(inner, dot(outer, block) + dot(fields, around)) + dot(beside, dot(fields, block))

    def second_pass(f, weight, low_rim, high_rim, at, order, done):
        center = rows(at + 8, 32)
        total, outer = None, None
        for plane in order:
            slot = SLOT[plane]
            mid, beside = beside_yz(f[slot, rows(at, 48), :])
            low = f[SLOT[plane - 1], center, :] if plane > 0 else low_rim() * keep_low
            high = f[SLOT[plane + 1], center, :] if plane < 3 else high_rim() * keep_high
            second = 1.2 * mid + weight[slot, center, :] * (beside + (low + high))
            done(slot, second)
            q = second - OMEGA * mid
            total = q if total is None else total + q
            if plane in (0, 3):
                rim = q * (edge_low if plane == 0 else edge_high)
                outer = rim if outer is None else outer + rim
        return total, outer

    for copy in halo_d:
        copy.wait_recv()

    def odd_rows(step, _):
        at = 32 * step
        here = rows(at, 32)

        def done(slot, second):
            sd[slot, here, :] = second

        summed, outer = second_pass(
            fd, rd, lambda: hd[0, here, :], lambda: hd[1, here, :], at, range(4), done
        )
        center = rows(at + 8, 32)
        waves = (own[0, center, :] - other[0, center, :]) + (own[1, center, :] - other[1, center, :])
        waves = waves + (own[2, center, :] - other[2, center, :]) + (own[3, center, :] - other[3, center, :])
        t_d[here, :] = summed
        x_d[here, :] = (0.04 * scale) * waves - outer
        return 0

    lax.fori_loop(0, 4, odd_rows, 0)

    for copy in halo_v:
        copy.wait_recv()

    def near_rows(step, _):
        at = 32 * step
        here = rows(at, 32)

        def done(slot, second):
            sv[slot, here, :] = second

        summed, outer = second_pass(
            fv, rv, lambda: hv[0, here, :], lambda: hv[1, here, :], at, range(4), done
        )
        t_v[here, :] = summed
        x_v[here, :] = 0.04 * x_v[here, :] - outer
        return 0

    lax.fori_loop(0, 2, near_rows, 0)
    coarse[...] = pltpu.roll(block_sums(t_d[...], x_d[...], 24, 128, 24), 96, 1) + pltpu.roll(
        block_sums(t_v[...], x_v[...], 24, 64, 24), 64, 1
    )

    for slot in range(4):
        seconds[slot].wait_recv()
        here = u_buf[slot, rows(8 + 32 * p, 32), :]
        low, high = (here + nu[slot]) * ROOT, (here - nu[slot]) * (ROOT * far_sign)
        fu[0, slot, 8:40, :] = low * ru[0, slot, 8:40, :]
        fu[1, slot, 8:40, :] = high * ru[1, slot, 8:40, :]
        x_u[0] = low if slot == 0 else x_u[0] + low
        x_u[1] = high if slot == 0 else x_u[1] + high
        if slot == 1:
            halo_u = [
                remote(fu.at[:, 0, 8:40, :], hu.at[1], sx.at[4], rx.at[4], below),
                remote(fu.at[:, 1, 8:40, :], hu.at[0], sx.at[5], rx.at[5], above),
            ]
    strip_2.wait_recv()
    here = ustrip[p]
    low, high = (here + nustrip[...]) * ROOT, (here - nustrip[...]) * (ROOT * far_sign)
    for slot in range(4):
        for j, rim in enumerate((low, high)):
            fu[j, slot, 7:8, :] = rim[slot : slot + 1] * ru[j, slot, 7:8, :]
            fu[j, slot, 40:41, :] = rim[4 + slot : 5 + slot] * ru[j, slot, 40:41, :]

    backs_2 = {}
    for planes in ((1,), (2,), (0,), (3,)):
        if planes == (0,):
            for copy in halo_u:
                copy.wait_recv()
        made = []
        for j in range(2):
            summed, outer = second_pass(
                fu.at[j], ru.at[j], lambda j=j: hu[0, j], lambda j=j: hu[1, j], 0, planes,
                lambda slot, second: made.append(second),
            )
            t_u[j] = summed if planes == (1,) else t_u[j] + summed
            x_u[j] = 0.04 * x_u[j] if planes == (1,) else x_u[j]
            if outer is not None:
                x_u[j] = x_u[j] - outer
        slot = SLOT[planes[0]]
        low, high = made[0] * ROOT, made[1] * (ROOT * far_sign)
        give[slot] = low - high
        backs_2[slot] = remote(
            give.at[slot], ub.at[slot, rows(32 * p, 32), :], sb2.at[slot], rb2.at[slot], (far, x)
        )
        ub[slot, rows(32 * p, 32), :] = low + high

    sums = block_sums(t_u[...].reshape(64, 256), x_u[...].reshape(64, 256), 16, 32, 8)
    coarse[0:8, :] = coarse[0:8, :] + (sums[0:8] + pltpu.roll(sums[8:16], 32, 1))
    reduces = [
        remote(coarse, coarse_x.at[m], sc.at[m], rc.at[m], (t, peer)) for m, peer in enumerate(x_peers)
    ]

    backs_1 = {}

    def level_1(slot):
        backs_2[slot].wait_recv()
        low, high = ub[slot] * ROOT, sv[slot] * (ROOT * near_sign)
        gives[slot] = low - high
        backs_1[slot] = remote(
            gives.at[slot], bk.at[slot, rows(64 * b, 64), :], sb1.at[slot], rb1.at[slot], (near, x)
        )
        bk[slot, rows(64 * b, 64), :] = low + high

    level_1(2)
    level_1(3)
    for copy in pots + reduces:
        copy.wait_recv()
    total[...] = (coarse[...] + coarse_x[0]) + (coarse_x[1] + coarse_x[2])
    gathers = [
        remote(total, tr.at[e], sg.at[m], rg.at[m], (peer, x)) for m, peer in enumerate(group)
    ]
    tr[e] = total[...]
    level_1(0)
    level_1(1)
    for copy in gathers:
        copy.wait_recv()

    lane = iota((24, 128), 1)
    coef = lane // 32
    sent = tr[...].reshape(192, 128)
    rem = jnp.where(coef < 2, dot(pick[0], sent), jnp.where(coef == 2, dot(pick[1], sent), dot(pick[2], sent)))
    shift = jnp.where(
        coef == 0, shift_ref[3], jnp.where(coef == 1, shift_ref[2], jnp.where(coef == 2, shift_ref[1], shift_0))
    )
    coarse_pot = (pot_all[0] + pot_all[1]) + (pot_all[2] + pot_all[3])
    diag = coarse_pot + shift * 1024.0 + 640.0
    one = rem / diag
    up, down = pltpu.roll(one, 1, 0), pltpu.roll(one, 23, 0)
    left = jnp.where(lane % 32 == 0, 0.0, pltpu.roll(one, 1, 1))
    right = jnp.where(lane % 32 == 31, 0.0, pltpu.roll(one, 127, 1))
    applied = diag * one - 128.0 * ((up + down) + (left + right))
    fix = one + (rem - applied) / diag
    weight = jnp.where(coef == 0, 0.5, jnp.where(coef == 1, 0.5 * far_sign, ROOT * near_sign))
    widen = ones_where(iota((128, 256), 0) % 32 == iota((128, 256), 1) // 8)
    heighten = ones_where(iota((128, 24), 0) // 8 + 1 == iota((128, 24), 1))
    xs[...] = dot(heighten, dot(jnp.where(coef < 3, fix * weight, 0.0), widen))
    xd[...] = dot(heighten, dot(jnp.where(coef == 3, fix, 0.0), widen)) * sign

    sends, stores = [], []
    for slot in (2, 3, 0, 1):
        backs_1[slot].wait_recv()
        even = bk[slot] + xs[...]
        odd = sd[slot] * sign + xd[...]
        yours[slot] = (even - odd) * ROOT
        there = out.at[0, PLANES[slot], rows(128 * k, 128), :]
        sends.append(remote(yours.at[slot], there, so.at[slot], ro.at[slot], (partner, x)))
        mine[slot] = (even + odd) * ROOT
        stores.append(local(mine.at[slot], there, lo.at[slot]))

    sent_all = swaps + firsts + seconds + [strip_1, strip_2] + halo_d + halo_v + halo_u + pots + reduces + gathers
    for copy in sent_all + list(backs_2.values()) + list(backs_1.values()):
        copy.wait_send()
    for copy in sends + stores:
        copy.wait()


def shards(source, potential, level_shift):
    dma = pltpu.SemaphoreType.DMA
    vmem = lambda *shape: pltpu.VMEM(shape, F32)
    scratch = dict(
        shift_ref=pltpu.SMEM((4,), F32),
        own=vmem(4, 144, 256), other=vmem(4, 144, 256), pot=vmem(4, 144, 256), s_buf=vmem(4, 144, 256),
        rd=vmem(4, 144, 256), fd=vmem(4, 144, 256), sd=vmem(4, 128, 256), strip=vmem(2, 8, 256),
        nb=vmem(4, 64, 256), nstrip=vmem(8, 256), u_buf=vmem(4, 80, 256), fv=vmem(4, 80, 256), rv=vmem(4, 80, 256),
        sv=vmem(4, 64, 256), ustrip=vmem(2, 8, 256), nu=vmem(4, 32, 256), nustrip=vmem(8, 256),
        fu=vmem(2, 4, 48, 256), ru=vmem(2, 4, 48, 256),
        hd=vmem(2, 128, 256), hv=vmem(2, 64, 256), hu=vmem(2, 2, 32, 256),
        ub=vmem(4, 64, 256), give=vmem(4, 32, 256), bk=vmem(4, 128, 256), gives=vmem(4, 64, 256),
        t_d=vmem(128, 256), x_d=vmem(128, 256), t_v=vmem(64, 256), x_v=vmem(64, 256),
        t_u=vmem(2, 32, 256), x_u=vmem(2, 32, 256),
        pot_all=vmem(4, 24, 128), coarse=vmem(24, 128), coarse_x=vmem(3, 24, 128), total=vmem(24, 128),
        tr=vmem(8, 24, 128), pick=vmem(3, 24, 192), xs=vmem(128, 256), xd=vmem(128, 256),
        mine=vmem(4, 128, 256), yours=vmem(4, 128, 256),
        h_sem=dma(()), l_sem=dma((4,)), p_sem=dma((4,)), s0=dma((4,)), r0=dma((4,)), s1=dma((4,)), r1=dma((4,)),
        s2=dma((4,)), r2=dma((4,)), st=dma(()), rt=dma(()), su=dma(()), ru_sem=dma(()), sx=dma((6,)), rx=dma((6,)),
        sp=dma((3,)), rp=dma((3,)), sc=dma((3,)), rc=dma((3,)), sg=dma((7,)), rg=dma((7,)),
        sb2=dma((4,)), rb2=dma((4,)), sb1=dma((4,)), rb1=dma((4,)), so=dma((4,)), ro=dma((4,)), lo=dma((4,)),
    )
    return pl.pallas_call(
        kernel,
        out_shape=jax.ShapeDtypeStruct(source.shape, F32),
        in_specs=[
            pl.BlockSpec(memory_space=pltpu.HBM),
            pl.BlockSpec(memory_space=pltpu.HBM),
            pl.BlockSpec(memory_space=pltpu.HBM),
        ],
        out_specs=pl.BlockSpec(memory_space=pl.ANY),
        scratch_shapes=list(scratch.values()),
        compiler_params=pltpu.CompilerParams(
            collective_id=0, has_side_effects=True, vmem_limit_bytes=105 * 2**19
        ),
        name="space_time_apply",
    )(level_shift, source, potential)


def solution(mesh):
    in_specs = (P("tm", "plane", None, None), P("plane", None, None), P())
    out_specs = P("tm", "plane", None, None)
    return jax.shard_map(shards, mesh=mesh, in_specs=in_specs, out_specs=out_specs, check_vma=False)
```

```python
import math

import jax
import jax.numpy as jnp
from jax import lax
from jax.experimental import pallas as pl
from jax.experimental.pallas import tpu as pltpu
from jax.sharding import PartitionSpec as P

F32 = jnp.float32
MESH = pl.DeviceIdType.MESH
ROOT = 1.0 / math.sqrt(2.0)
OMEGA = 0.8
PLANES = (0, 3, 1, 2)
SLOT = {plane: slot for slot, plane in enumerate(PLANES)}


def dot(a, b):
    return jnp.dot(a, b, precision=lax.Precision.HIGHEST, preferred_element_type=F32)


def iota(shape, dim):
    return lax.broadcasted_iota(jnp.int32, shape, dim)


def ones_where(mask):
    return jnp.where(mask, 1.0, 0.0).astype(F32)


def beside_yz(ext):
    rows = ext.shape[0] - 16
    mid = ext[8 : 8 + rows]
    up = pltpu.roll(ext, 1, 0)[8 : 8 + rows]
    down = pltpu.roll(ext, rows + 15, 0)[8 : 8 + rows]
    col = iota(mid.shape, 1)
    left = jnp.where(col == 0, 0.0, pltpu.roll(mid, 1, 1))
    right = jnp.where(col == 255, 0.0, pltpu.roll(mid, 255, 1))
    return mid, (up + down) + (left + right)


def kernel(
    shift_hbm, source, potential, out, fix_out,
    shift_ref, own, other, pot, pot_other, s_buf, rd, fd, sd, strip, nb, nstrip, u_buf, fv, rv, sv, ustrip, nu, nustrip, fu, ru,
    hd, hv, hu, ub, ub_own, give, bk, gives, t_d, x_d, t_uv, x_uv, pot_all, d_sums, d_x, d_total, d_other, uv_sums, uv_x, uv_total,
    tr, blocks, pick, pick_d, fix_all, mine, yours,
    h_sem, l_sem, p_sem, q_sem, f_sem, s0, r0, s1, r1, s2, r2, st, rt, su, ru_sem, sx, rx, sp, rp, sdx, rdx, sdp, rdp, sc, rc, sg, rg,
    sb2, rb2, sb1, rb1, so, ro, lo,
):
    t, x = lax.axis_index("tm"), lax.axis_index("plane")
    e = t % 8
    k, c = e % 2, e // 2
    b, p = c % 2, c // 2
    partner = t + 1 - 2 * k
    near = t + 2 - 4 * b
    far = t + 4 - 8 * p
    x_peers = [(x + m) % 4 for m in (1, 2, 3)]
    group = [t - e + (e + m) % 8 for m in range(1, 8)]

    barrier = pltpu.get_barrier_semaphore()
    for peer in group:
        pl.semaphore_signal(barrier, inc=1, device_id=(peer, x), device_id_type=MESH)
    for peer in x_peers:
        pl.semaphore_signal(barrier, inc=1, device_id=(t, peer), device_id_type=MESH)

    def rows(start, count):
        return pl.ds(pl.multiple_of(start, 8), count)

    def remote(src, dst, send, recv, where):
        copy = pltpu.make_async_remote_copy(
            src_ref=src, dst_ref=dst, send_sem=send, recv_sem=recv, device_id=where, device_id_type=MESH
        )
        copy.start()
        return copy

    def local(src, dst, sem):
        copy = pltpu.make_async_copy(src, dst, sem)
        copy.start()
        return copy

    loads = [
        local(source.at[0, plane, rows(120 * k, 136), :], own.at[slot, rows(8 - 8 * k, 136), :], l_sem.at[slot])
        for slot, plane in enumerate(PLANES)
    ]
    shift_load = local(shift_hbm, shift_ref, h_sem)
    pot_loads = [
        local(potential.at[plane, rows(120 * k, 136), :], pot.at[slot, rows(8 - 8 * k, 136), :], p_sem.at[slot])
        for slot, plane in enumerate(PLANES)
    ]
    rest_load = local(potential.at[:, rows(128 - 128 * k, 128), :], pot_other, q_sem)
    for slot in range(4):
        for ref in (own, other, pot):
            ref[slot, rows(136 * k, 8), :] = jnp.zeros((8, 256), F32)

    pl.semaphore_wait(barrier, 10)

    swaps = [
        remote(
            source.at[0, plane, rows(120 - 120 * k, 136), :], other.at[slot, rows(8 * k, 136), :],
            s0.at[slot], r0.at[slot], (partner, x),
        )
        for slot, plane in enumerate(PLANES)
    ]

    def to_near(index, q, slots, start=0, count=32):
        at = 32 * q + start
        return remote(
            s_buf.at[slots, rows(72 - 64 * b + at, count), :], nb.at[slots, rows(at, count), :],
            s1.at[index], r1.at[index], (near, x),
        )

    firsts = {}
    for slot in range(4):
        loads[slot].wait()
        swaps[slot].wait_recv()
        s_buf[slot] = (own[slot] + other[slot]) * ROOT
        if slot < 2:
            firsts[slot] = to_near(slot, 1 - p, slot)
        if slot == 1:
            firsts[4] = to_near(4, p, 0)
            firsts[5] = to_near(5, p, 1)
    for h in range(2):
        for i in range(4):
            for at, row in ((0, 7), (4, 40), (8, 39), (12, 72)):
                strip[h, at + i : at + i + 1, :] = s_buf[i, row + 64 * h : row + 64 * h + 1, :]
    strip_1 = remote(strip.at[1 - b], nstrip, st, rt, (near, x))

    sign = (1 - 2 * k).astype(F32)
    near_sign = (1 - 2 * b).astype(F32)
    far_sign = (1 - 2 * p).astype(F32)
    scale = ROOT * sign
    keep_low, keep_high = ones_where(x > 0), ones_where(x < 3)
    edge_low, edge_high = 1.0 - keep_low, 1.0 - keep_high
    shift_load.wait()
    shift_0 = shift_ref[0]
    for slot in range(4):
        pot_loads[slot].wait()
        rd[slot] = OMEGA / (6.0 + pot[slot] + shift_0)
        fd[slot] = (own[slot] - other[slot]) * scale * rd[slot]
    below, above = (t, (x + 3) % 4), (t, (x + 1) % 4)
    halo_d = [
        remote(fd.at[0, 8:136, :], hd.at[1], sx.at[0], rx.at[0], below),
        remote(fd.at[1, 8:136, :], hd.at[0], sx.at[1], rx.at[1], above),
    ]

    for slot in range(4):
        rv[slot] = OMEGA / (6.0 + pot[slot, rows(64 * b, 80), :] + shift_ref[1])
        here = 6.0 + pot[slot, rows(64 * b + 32 * p, 48), :]
        ru[0, slot] = OMEGA / (here + shift_ref[3])
        ru[1, slot] = OMEGA / (here + shift_ref[2])

    z_at, z_block = iota((256, 128), 0), iota((256, 128), 1)
    lane_block = ones_where(z_at // 8 == z_block % 32)
    row, col = iota((32, 128), 0), iota((32, 128), 1)
    rest_load.wait()
    pot_sum = (pot[0, 8:136, :] + pot[1, 8:136, :]) + (pot[2, 8:136, :] + pot[3, 8:136, :])
    pot_rest = (pot_other[0] + pot_other[1]) + (pot_other[2] + pot_other[3])
    pot_all[0] = dot(ones_where(col // 8 + 16 * k == row), dot(pot_sum, lane_block)) + dot(
        ones_where(col // 8 + 16 - 16 * k == row), dot(pot_rest, lane_block)
    )
    pots = [
        remote(pot_all.at[0], pot_all.at[m + 1], sp.at[m], rp.at[m], (t, peer)) for m, peer in enumerate(x_peers)
    ]
    block = ones_where(z_at // 8 == z_block)
    around = ones_where((z_at + 7) // 8 == z_block + 1) + ones_where((z_at + 1) // 8 == z_block)
    blocks[0] = block
    blocks[1] = jnp.where(z_block < 32, 2.0 * block + around, 0.0)

    row, col = iota((32, 64), 0), iota((32, 64), 1)
    sender, r = col // 8, col % 8
    sender_c = sender // 2
    sender_b, sender_p = sender_c % 2, sender_c // 2
    sender_at = 16 * (sender % 2) + 8 * sender_b - 1 + r
    pick[0] = ones_where((r < 6) & (sender_at + 4 * sender_p == row))
    pick[1] = ones_where((sender_p == p) & (sender_at == row))
    pick[2] = ones_where((sender_p == p) & (r < 2) & (sender_at + 8 == row))
    row, col = iota((32, 24), 0), iota((32, 24), 1)
    pick_d[0] = ones_where((col < 18) & (16 * k - 1 + col == row))
    pick_d[1] = ones_where((col < 18) & (16 * (1 - k) - 1 + col == row))

    def level_1(slot, q, start=0, count=32):
        inside = 32 * q + start
        here = s_buf[slot, rows(8 + 64 * b + inside, count), :]
        there = nb[slot, rows(inside, count), :]
        at = rows(8 + inside, count)
        u_buf[slot, at, :] = (here + there) * ROOT
        detail = (here - there) * (ROOT * near_sign)
        fv[slot, at, :] = detail * rv[slot, at, :]
        at = rows(inside, count)
        x_uv[at, :] = detail if slot == 0 else x_uv[at, :] + detail

    seconds = {}

    def to_far(index, slots, start=0, count=32):
        seconds[index] = remote(
            u_buf.at[slots, rows(40 - 32 * p + start, count), :], nu.at[slots, start : start + count, :],
            s2.at[index], r2.at[index], (far, x),
        )

    def level_2(slot, start=0, count=32):
        here = u_buf[slot, rows(8 + 32 * p + start, count), :]
        there = nu[slot, start : start + count, :]
        at = slice(8 + start, 8 + start + count)
        low, high = (here + there) * ROOT, (here - there) * (ROOT * far_sign)
        fu[0, slot, at, :] = low * ru[0, slot, at, :]
        fu[1, slot, at, :] = high * ru[1, slot, at, :]
        for base, field in ((64, low), (96, high)):
            at = slice(base + start, base + start + count)
            x_uv[at, :] = field if slot == 0 else x_uv[at, :] + field

    firsts[0].wait_recv()
    level_1(0, 1 - p)
    to_far(0, 0)
    firsts[2] = to_near(2, 1 - p, 2, 0, 24)
    firsts[1].wait_recv()
    level_1(1, 1 - p)
    to_far(1, 1)
    firsts[3] = to_near(3, 1 - p, 3, 0, 24)
    firsts[6] = to_near(6, p, 2, 0, 24)
    firsts[7] = to_near(7, p, 3, 0, 24)
    strip_1.wait_recv()
    ustrip[...] = (strip[b] + nstrip[...]) * ROOT
    strip_2 = remote(ustrip.at[rows(8 - 8 * p, 8), :], nustrip, su, ru_sem, (far, x))
    details = (strip[b] - nstrip[...]) * (ROOT * near_sign)
    for slot in range(4):
        fv[slot, 7:8, :] = details[slot : slot + 1] * rv[slot, 7:8, :]
        fv[slot, 72:73, :] = details[12 + slot : 13 + slot] * rv[slot, 72:73, :]
        if slot > 1:
            fv[slot, 39:40, :] = details[8 + slot : 9 + slot] * rv[slot, 39:40, :]
    for slot in (0, 1):
        firsts[4 + slot].wait_recv()
        level_1(slot, p)
    halo_v = [
        remote(fv.at[0, 8:72, :], hv.at[1], sx.at[2], rx.at[2], below),
        remote(fv.at[1, 8:72, :], hv.at[0], sx.at[3], rx.at[3], above),
    ]
    inner_planes = slice(2, 4)
    for slot in (2, 3):
        firsts[slot].wait_recv()
        level_1(slot, 1 - p, 0, 24)
        to_far(slot, slot, 0, 24)
        firsts[6 + slot] = to_near(6 + slot, 1 - p if slot == 2 else p, inner_planes, 24, 8)
    for slot in (0, 1):
        seconds[slot].wait_recv()
        level_2(slot)
    halo_u = [
        remote(fu.at[:, 0, 8:40, :], hu.at[1], sx.at[4], rx.at[4], below),
        remote(fu.at[:, 1, 8:40, :], hu.at[0], sx.at[5], rx.at[5], above),
    ]

    def second_pass(f, weight, low_rim, high_rim, at, count, order, done):
        center = rows(at + 8, count)
        total, outer = None, None
        for plane in order:
            slot = SLOT[plane]
            mid, beside = beside_yz(f[slot, rows(at, count + 16), :])
            low = f[SLOT[plane - 1], center, :] if plane > 0 else low_rim() * keep_low
            high = f[SLOT[plane + 1], center, :] if plane < 3 else high_rim() * keep_high
            second = 1.2 * mid + weight[slot, center, :] * (beside + (low + high))
            done(slot, second)
            q = second - OMEGA * mid
            total = q if total is None else total + q
            if plane in (0, 3):
                rim = q * (edge_low if plane == 0 else edge_high)
                outer = rim if outer is None else outer + rim
        return total, outer

    for copy in halo_d:
        copy.wait_recv()

    def odd_rows(step, _):
        at = 32 * step
        here = rows(at, 32)

        def done(slot, second):
            sd[slot, here, :] = second

        summed, outer = second_pass(
            fd, rd, lambda: hd[0, here, :], lambda: hd[1, here, :], at, 32, range(4), done
        )
        center = rows(at + 8, 32)
        waves = (own[0, center, :] - other[0, center, :]) + (own[1, center, :] - other[1, center, :])
        waves = waves + (own[2, center, :] - other[2, center, :]) + (own[3, center, :] - other[3, center, :])
        t_d[here, :] = summed
        x_d[here, :] = (0.04 * scale) * waves - outer
        return 0

    lax.fori_loop(0, 4, odd_rows, 0)
    for slot in (2, 3):
        firsts[4 + slot].wait_recv()
        level_1(slot, p, 0, 24)
    firsts[8].wait_recv()
    for slot in (2, 3):
        level_1(slot, 1 - p, 24, 8)
    to_far(4, inner_planes, 24, 8)

    def near_rows(half):
        def body(step, _):
            at = 32 * step + 16 * half
            here = rows(at, 16)

            def done(slot, second):
                sv[slot, here, :] = second

            summed, outer = second_pass(
                fv, rv, lambda: hv[0, here, :], lambda: hv[1, here, :], at, 16, range(4), done
            )
            t_uv[here, :] = summed
            x_uv[here, :] = 0.04 * x_uv[here, :] - outer
            return 0

        lax.fori_loop(0, 2, body, 0)

    for copy in halo_v:
        copy.wait_recv()
    near_rows(0)

    strip_2.wait_recv()
    here = ustrip[rows(8 * p, 8), :]
    low, high = (here + nustrip[...]) * ROOT, (here - nustrip[...]) * (ROOT * far_sign)
    for slot in range(4):
        for j, rim in enumerate((low, high)):
            fu[j, slot, 7:8, :] = rim[slot : slot + 1] * ru[j, slot, 7:8, :]
            fu[j, slot, 40:41, :] = rim[4 + slot : 5 + slot] * ru[j, slot, 40:41, :]
    for slot in (2, 3):
        seconds[slot].wait_recv()
        level_2(slot, 0, 24)

    backs_1, backs_2 = {}, {}

    def far_rows(half, planes):
        here = slice(16 * half, 16 * half + 16)
        for plane in planes:
            made = []
            for j in range(2):
                at = slice(64 + 32 * j + 16 * half, 80 + 32 * j + 16 * half)
                summed, outer = second_pass(
                    fu.at[j], ru.at[j], lambda: hu[0, j, here, :], lambda: hu[1, j, here, :], 16 * half, 16, (plane,),
                    lambda slot, second: made.append(second),
                )
                t_uv[at, :] = summed if plane == 1 else t_uv[at, :] + summed
                if plane == 1:
                    x_uv[at, :] = 0.04 * x_uv[at, :]
                if outer is not None:
                    x_uv[at, :] = x_uv[at, :] - outer
            low, high = made[0] * ROOT, made[1] * (ROOT * far_sign)
            give[SLOT[plane], here, :] = low - high
            ub_own[SLOT[plane], here, :] = low + high
        pair = SLOT[planes[0]] // 2
        slots, index = slice(2 * pair, 2 * pair + 2), 2 * half + pair
        backs_2[index] = remote(
            give.at[slots, here, :], ub.at[slots, here, :], sb2.at[index], rb2.at[index], (far, x)
        )

    def join(half, pair, q, ref, index):
        at = 32 * q + 16 * half
        slots = slice(2 * pair, 2 * pair + 2)
        for slot in (2 * pair, 2 * pair + 1):
            low = ref[slot, 16 * half : 16 * half + 16, :] * ROOT
            high = sv[slot, rows(at, 16), :] * (ROOT * near_sign)
            gives[slot, rows(at, 16), :] = low - high
            bk[slot, rows(64 * b + at, 16), :] = low + high
        backs_1[index] = remote(
            gives.at[slots, rows(at, 16), :], bk.at[slots, rows(64 * b + at, 16), :],
            sb1.at[index], rb1.at[index], (near, x),
        )

    def own_part(half):
        for pair in (1, 0):
            join(half, pair, p, ub_own, 2 * half + pair)

    def rest(half, pair):
        index = 2 * half + pair
        backs_2[index].wait_recv()
        join(half, pair, 1 - p, ub, 4 + index)

    far_rows(0, (1, 2))
    for copy in halo_u:
        copy.wait_recv()
    far_rows(0, (0, 3))
    own_part(0)
    firsts[9].wait_recv()
    for slot in (2, 3):
        level_1(slot, p, 24, 8)
    near_rows(1)
    seconds[4].wait_recv()
    for slot in (2, 3):
        level_2(slot, 24, 8)
    far_rows(1, (1, 2))
    far_rows(1, (0, 3))

    y_at, y_row = iota((32, 128), 1), iota((32, 128), 0)
    start = jnp.where(y_at < 64, 0, 16 + 8 * ((y_at - 64) // 32))
    y_in = jnp.where(y_at < 64, y_at, y_at % 32)
    inner = ones_where(start + y_in // 8 + 1 == y_row)
    beside = ones_where(start + (y_in + 7) // 8 == y_row) + ones_where(start + (y_in + 1) // 8 + 1 == y_row)
    sums = dot(inner, dot(x_uv[...], blocks[0]) + dot(t_uv[...], blocks[1])) + dot(beside, dot(t_uv[...], blocks[0]))
    uv_sums[...] = (sums[16:24] + pltpu.roll(sums[24:32], 32, 1)) + (
        pltpu.roll(sums[0:8], 64, 1) + pltpu.roll(sums[8:16], 96, 1)
    )
    uv_reduces = [
        remote(uv_sums, uv_x.at[m], sc.at[m], rc.at[m], (t, peer)) for m, peer in enumerate(x_peers)
    ]
    own_part(1)
    y_at, y_row = iota((24, 128), 1), iota((24, 128), 0)
    inner = ones_where(y_at // 8 + 1 == y_row)
    beside = ones_where((y_at + 7) // 8 == y_row) + ones_where((y_at + 1) // 8 + 1 == y_row)
    sums = dot(inner, dot(x_d[...], blocks[0]) + dot(t_d[...], blocks[1])) + dot(beside, dot(t_d[...], blocks[0]))
    d_sums[...] = pltpu.roll(sums, 96, 1)
    d_reduces = [
        remote(d_sums, d_x.at[m], sdx.at[m], rdx.at[m], (t, peer)) for m, peer in enumerate(x_peers)
    ]

    for copy in uv_reduces:
        copy.wait_recv()
    uv_total[...] = (uv_sums[...] + uv_x[0]) + (uv_x[1] + uv_x[2])
    gathers = [
        remote(uv_total, tr.at[e], sg.at[m], rg.at[m], (peer, x)) for m, peer in enumerate(group)
    ]
    tr[e] = uv_total[...]
    rest(0, 1)
    rest(0, 0)
    for copy in d_reduces + pots:
        copy.wait_recv()
    d_total[...] = (d_sums[...] + d_x[0]) + (d_x[1] + d_x[2])
    d_swap = remote(d_total, d_other, sdp, rdp, (partner, x))

    sends, stores = [], []

    def finish(slot, start, index):
        here = rows(start, 64)
        even, odd = bk[slot, here, :], sd[slot, here, :] * sign
        yours[slot, here, :] = (even - odd) * ROOT
        there = out.at[0, PLANES[slot], rows(128 * k + start, 64), :]
        sends.append(remote(yours.at[slot, here, :], there, so.at[index], ro.at[index], (partner, x)))
        mine[slot, here, :] = (even + odd) * ROOT
        stores.append(local(mine.at[slot, here, :], there, lo.at[index]))

    for pair in (1, 0):
        rest(1, pair)
        for slot in (2 * pair, 2 * pair + 1):
            finish(slot, 64 * b, slot)

    def finish_pair(pair):
        for index in (pair, 2 + pair, 4 + pair, 6 + pair):
            backs_1[index].wait_recv()
        for slot in (2 * pair, 2 * pair + 1):
            finish(slot, 64 - 64 * b, 4 + slot)

    finish_pair(1)
    for copy in gathers:
        copy.wait_recv()
    d_swap.wait_recv()

    lane = iota((32, 128), 1)
    coef = lane // 32
    sent = tr[...].reshape(64, 128)
    rem_v = dot(pick[1], sent) + pltpu.roll(dot(pick[2], sent), 96, 1)
    rem_d = dot(pick_d[0], d_total[...]) + dot(pick_d[1], d_other[...])
    rem = jnp.where(coef < 2, dot(pick[0], sent), jnp.where(coef == 2, rem_v, rem_d))
    shift = jnp.where(
        coef == 0, shift_ref[3], jnp.where(coef == 1, shift_ref[2], jnp.where(coef == 2, shift_ref[1], shift_0))
    )
    coarse_pot = (pot_all[0] + pot_all[1]) + (pot_all[2] + pot_all[3])
    diag = coarse_pot + shift * 1024.0 + 640.0
    one = rem / diag
    row = iota((32, 128), 0)
    up = jnp.where(row == 0, 0.0, pltpu.roll(one, 1, 0))
    down = jnp.where(row == 31, 0.0, pltpu.roll(one, 31, 0))
    left = jnp.where(lane % 32 == 0, 0.0, pltpu.roll(one, 1, 1))
    right = jnp.where(lane % 32 == 31, 0.0, pltpu.roll(one, 127, 1))
    applied = diag * one - 128.0 * ((up + down) + (left + right))
    fix = one + (rem - applied) / diag
    weight = jnp.where(
        coef == 0, 0.5 * ROOT, jnp.where(coef == 1, 0.5 * ROOT * far_sign, jnp.where(coef == 2, 0.5 * near_sign, scale))
    )
    widen = ones_where(iota((128, 256), 0) % 32 == iota((128, 256), 1) // 8)
    wide = dot(fix * weight, widen)
    for i in range(32):
        fix_all[8 * i : 8 * i + 8, :] = jnp.broadcast_to(wide[i : i + 1], (8, 256))
    stores.append(local(fix_all, fix_out, f_sem))
    finish_pair(0)

    sent_all = swaps + list(firsts.values()) + list(seconds.values()) + [strip_1, strip_2, d_swap] + halo_d + halo_v + halo_u + pots
    for copy in sent_all + d_reduces + uv_reduces + gathers + list(backs_2.values()) + list(backs_1.values()):
        copy.wait_send()
    for copy in sends + stores:
        copy.wait()


def shards(source, potential, level_shift):
    dma = pltpu.SemaphoreType.DMA
    vmem = lambda *shape: pltpu.VMEM(shape, F32)
    scratch = dict(
        shift_ref=pltpu.SMEM((4,), F32),
        own=vmem(4, 144, 256), other=vmem(4, 144, 256), pot=vmem(4, 144, 256), pot_other=vmem(4, 128, 256), s_buf=vmem(4, 144, 256),
        rd=vmem(4, 144, 256), fd=vmem(4, 144, 256), sd=vmem(4, 128, 256), strip=vmem(2, 16, 256),
        nb=vmem(4, 64, 256), nstrip=vmem(16, 256), u_buf=vmem(4, 80, 256), fv=vmem(4, 80, 256), rv=vmem(4, 80, 256),
        sv=vmem(4, 64, 256), ustrip=vmem(16, 256), nu=vmem(4, 32, 256), nustrip=vmem(8, 256),
        fu=vmem(2, 4, 48, 256), ru=vmem(2, 4, 48, 256),
        hd=vmem(2, 128, 256), hv=vmem(2, 64, 256), hu=vmem(2, 2, 32, 256),
        ub=vmem(4, 32, 256), ub_own=vmem(4, 32, 256), give=vmem(4, 32, 256), bk=vmem(4, 128, 256), gives=vmem(4, 64, 256),
        t_d=vmem(128, 256), x_d=vmem(128, 256), t_uv=vmem(128, 256), x_uv=vmem(128, 256),
        pot_all=vmem(4, 32, 128), d_sums=vmem(24, 128), d_x=vmem(3, 24, 128), d_total=vmem(24, 128),
        d_other=vmem(24, 128), uv_sums=vmem(8, 128), uv_x=vmem(3, 8, 128), uv_total=vmem(8, 128),
        tr=vmem(8, 8, 128), blocks=vmem(2, 256, 128), pick=vmem(3, 32, 64), pick_d=vmem(2, 32, 24),
        fix_all=vmem(256, 256), mine=vmem(4, 128, 256), yours=vmem(4, 128, 256),
        h_sem=dma(()), l_sem=dma((4,)), p_sem=dma((4,)), q_sem=dma(()), f_sem=dma(()), s0=dma((4,)), r0=dma((4,)), s1=dma((10,)), r1=dma((10,)),
        s2=dma((5,)), r2=dma((5,)), st=dma(()), rt=dma(()), su=dma(()), ru_sem=dma(()), sx=dma((6,)), rx=dma((6,)),
        sp=dma((3,)), rp=dma((3,)), sdx=dma((3,)), rdx=dma((3,)), sdp=dma(()), rdp=dma(()), sc=dma((3,)), rc=dma((3,)),
        sg=dma((7,)), rg=dma((7,)), sb2=dma((4,)), rb2=dma((4,)), sb1=dma((8,)), rb1=dma((8,)),
        so=dma((8,)), ro=dma((8,)), lo=dma((8,)),
    )
    raw, fix = pl.pallas_call(
        kernel,
        out_shape=(jax.ShapeDtypeStruct(source.shape, F32), jax.ShapeDtypeStruct(source.shape[2:], F32)),
        in_specs=[
            pl.BlockSpec(memory_space=pltpu.HBM),
            pl.BlockSpec(memory_space=pltpu.HBM),
            pl.BlockSpec(memory_space=pltpu.HBM),
        ],
        out_specs=(pl.BlockSpec(memory_space=pl.ANY), pl.BlockSpec(memory_space=pl.ANY)),
        scratch_shapes=list(scratch.values()),
        compiler_params=pltpu.CompilerParams(
            collective_id=0, has_side_effects=True, vmem_limit_bytes=105 * 2**19
        ),
        name="space_time_apply",
    )(level_shift, source, potential)
    return raw + fix[None, None]


def solution(mesh):
    in_specs = (P("tm", "plane", None, None), P("plane", None, None), P())
    out_specs = P("tm", "plane", None, None)
    return jax.shard_map(shards, mesh=mesh, in_specs=in_specs, out_specs=out_specs, check_vma=False)
```

```python
import math

import jax
import jax.numpy as jnp
from jax import lax
from jax.experimental import pallas as pl
from jax.experimental.pallas import tpu as pltpu
from jax.sharding import PartitionSpec as P

F32 = jnp.float32
MESH = pl.DeviceIdType.MESH
ROOT = 1.0 / math.sqrt(2.0)
OMEGA = 0.8
PLANES = (0, 3, 1, 2)
SLOT = {plane: slot for slot, plane in enumerate(PLANES)}


def dot(a, b):
    return jnp.dot(a, b, precision=lax.Precision.HIGHEST, preferred_element_type=F32)


def iota(shape, dim):
    return lax.broadcasted_iota(jnp.int32, shape, dim)


def ones_where(mask):
    return jnp.where(mask, 1.0, 0.0).astype(F32)


def beside_yz(ext):
    rows = ext.shape[0] - 16
    mid = ext[8 : 8 + rows]
    up = pltpu.roll(ext, 1, 0)[8 : 8 + rows]
    down = pltpu.roll(ext, rows + 15, 0)[8 : 8 + rows]
    col = iota(mid.shape, 1)
    left = jnp.where(col == 0, 0.0, pltpu.roll(mid, 1, 1))
    right = jnp.where(col == 255, 0.0, pltpu.roll(mid, 255, 1))
    return mid, (up + down) + (left + right)


def kernel(
    shift_hbm, source, potential, out, fix_out,
    shift_ref, own, other, pot, pot_other, s_buf, rd, fd, sd, strip, nb, nstrip, u_buf, fv, rv, sv, ustrip, nu, nustrip, fu, ru,
    hd, hv, hu, ub, ub_own, give, bk, gives, t_d, x_d, t_uv, x_uv, pot_all, d_sums, d_x, d_total, d_other, uv_sums, uv_x, uv_total,
    tr, blocks, pick, pick_d, fix_all, mine, yours,
    all_sent, h_sem, l_sem, p_sem, q_sem, f_sem, sent, r0, r1, r2, rt, ru_sem, rx, rp, rdx, rdp, rc, rg, rb2, rb1, ro, lo,
):
    t, x = lax.axis_index("tm"), lax.axis_index("plane")
    e = t % 8
    k, c = e % 2, e // 2
    b, p = c % 2, c // 2
    partner = t + 1 - 2 * k
    near = t + 2 - 4 * b
    far = t + 4 - 8 * p
    x_peers = [(x + m) % 4 for m in (1, 2, 3)]
    group = [t - e + (e + m) % 8 for m in range(1, 8)]

    barrier = pltpu.get_barrier_semaphore()
    for peer in group:
        pl.semaphore_signal(barrier, inc=1, device_id=(peer, x), device_id_type=MESH)
    for peer in x_peers:
        pl.semaphore_signal(barrier, inc=1, device_id=(t, peer), device_id_type=MESH)

    def rows(start, count):
        return pl.ds(pl.multiple_of(start, 8), count)

    def remote(src, dst, recv, where):
        copy = pltpu.make_async_remote_copy(
            src_ref=src, dst_ref=dst, send_sem=sent, recv_sem=recv, device_id=where, device_id_type=MESH
        )
        copy.start()
        return copy

    def absorb(ref, sem):
        pltpu.make_async_copy(ref, ref, sem).wait()

    def local(src, dst, sem):
        copy = pltpu.make_async_copy(src, dst, sem)
        copy.start()
        return copy

    for slot, plane in enumerate(PLANES):
        local(source.at[0, plane, rows(120 * k, 136), :], own.at[slot, rows(8 - 8 * k, 136), :], l_sem)
    shift_load = local(shift_hbm, shift_ref, h_sem)
    for slot, plane in enumerate(PLANES):
        local(potential.at[plane, rows(120 * k, 136), :], pot.at[slot, rows(8 - 8 * k, 136), :], p_sem)
    rest_load = local(potential.at[:, rows(128 - 128 * k, 128), :], pot_other, q_sem)
    for slot in range(4):
        for ref in (own, other, pot):
            ref[slot, rows(136 * k, 8), :] = jnp.zeros((8, 256), F32)

    pl.semaphore_wait(barrier, 10)

    swaps = [
        remote(
            source.at[0, plane, rows(120 - 120 * k, 136), :], other.at[slot, rows(8 * k, 136), :],
            r0.at[slot], (partner, x),
        )
        for slot, plane in enumerate(PLANES)
    ]

    def to_near(index, slot, q):
        firsts[index] = remote(
            s_buf.at[slot, rows(72 - 64 * b + 32 * q, 32), :], nb.at[slot, rows(32 * q, 32), :],
            r1.at[index], (near, x),
        )

    firsts = {}
    absorb(own.at[:, 0:136, :], l_sem)
    for slot in range(4):
        swaps[slot].wait_recv()
        s_buf[slot] = (own[slot] + other[slot]) * ROOT
        if slot < 2:
            to_near(slot, slot, 1 - p)
        if slot == 1:
            to_near(4, 0, p)
            to_near(5, 1, p)
    for h in range(2):
        for i in range(4):
            for at, row in ((0, 7), (4, 40), (8, 39), (12, 72)):
                strip[h, at + i : at + i + 1, :] = s_buf[i, row + 64 * h : row + 64 * h + 1, :]

    sign = (1 - 2 * k).astype(F32)
    near_sign = (1 - 2 * b).astype(F32)
    far_sign = (1 - 2 * p).astype(F32)
    scale = ROOT * sign
    keep_low, keep_high = ones_where(x > 0), ones_where(x < 3)
    edge_low, edge_high = 1.0 - keep_low, 1.0 - keep_high
    shift_load.wait()
    shift_0 = shift_ref[0]
    absorb(pot.at[:, 0:136, :], p_sem)
    for slot in range(4):
        rd[slot] = OMEGA / (6.0 + pot[slot] + shift_0)
        fd[slot] = (own[slot] - other[slot]) * scale * rd[slot]
    below, above = (t, (x + 3) % 4), (t, (x + 1) % 4)
    remote(fd.at[0, 8:136, :], hd.at[1], rx.at[0], below)
    remote(fd.at[1, 8:136, :], hd.at[0], rx.at[0], above)

    for slot in range(4):
        rv[slot] = OMEGA / (6.0 + pot[slot, rows(64 * b, 80), :] + shift_ref[1])
        here = 6.0 + pot[slot, rows(64 * b + 32 * p, 48), :]
        ru[0, slot] = OMEGA / (here + shift_ref[3])
        ru[1, slot] = OMEGA / (here + shift_ref[2])

    z_at, z_block = iota((256, 128), 0), iota((256, 128), 1)
    lane_block = ones_where(z_at // 8 == z_block % 32)
    row, col = iota((32, 128), 0), iota((32, 128), 1)
    rest_load.wait()
    pot_sum = (pot[0, 8:136, :] + pot[1, 8:136, :]) + (pot[2, 8:136, :] + pot[3, 8:136, :])
    pot_rest = (pot_other[0] + pot_other[1]) + (pot_other[2] + pot_other[3])
    pot_all[0] = dot(ones_where(col // 8 + 16 * k == row), dot(pot_sum, lane_block)) + dot(
        ones_where(col // 8 + 16 - 16 * k == row), dot(pot_rest, lane_block)
    )
    for m, peer in enumerate(x_peers):
        remote(pot_all.at[0], pot_all.at[m + 1], rp, (t, peer))
    block = ones_where(z_at // 8 == z_block)
    around = ones_where((z_at + 7) // 8 == z_block + 1) + ones_where((z_at + 1) // 8 == z_block)
    blocks[0] = block
    blocks[1] = jnp.where(z_block < 32, 2.0 * block + around, 0.0)

    row, col = iota((32, 64), 0), iota((32, 64), 1)
    sender, r = col // 8, col % 8
    sender_c = sender // 2
    sender_b, sender_p = sender_c % 2, sender_c // 2
    sender_at = 16 * (sender % 2) + 8 * sender_b - 1 + r
    pick[0] = ones_where((r < 6) & (sender_at + 4 * sender_p == row))
    pick[1] = ones_where((sender_p == p) & (sender_at == row))
    pick[2] = ones_where((sender_p == p) & (r < 2) & (sender_at + 8 == row))
    row, col = iota((32, 24), 0), iota((32, 24), 1)
    pick_d[0] = ones_where((col < 18) & (16 * k - 1 + col == row))
    pick_d[1] = ones_where((col < 18) & (16 * (1 - k) - 1 + col == row))

    def level_1(slot, q):
        here = s_buf[slot, rows(8 + 64 * b + 32 * q, 32), :]
        there = nb[slot, rows(32 * q, 32), :]
        at = rows(8 + 32 * q, 32)
        u_buf[slot, at, :] = (here + there) * ROOT
        detail = (here - there) * (ROOT * near_sign)
        fv[slot, at, :] = detail * rv[slot, at, :]
        at = rows(32 * q, 32)
        x_uv[at, :] = detail if slot == 0 else x_uv[at, :] + detail

    seconds = {}

    def passed_on(slot):
        firsts[slot].wait_recv()
        level_1(slot, 1 - p)
        seconds[slot] = remote(
            u_buf.at[slot, rows(40 - 32 * p, 32), :], nu.at[slot], r2.at[slot], (far, x)
        )

    def level_2(slot):
        seconds[slot].wait_recv()
        here = u_buf[slot, rows(8 + 32 * p, 32), :]
        low, high = (here + nu[slot]) * ROOT, (here - nu[slot]) * (ROOT * far_sign)
        fu[0, slot, 8:40, :] = low * ru[0, slot, 8:40, :]
        fu[1, slot, 8:40, :] = high * ru[1, slot, 8:40, :]
        for at, field in ((64, low), (96, high)):
            x_uv[at : at + 32, :] = field if slot == 0 else x_uv[at : at + 32, :] + field

    passed_on(0)
    passed_on(1)
    to_near(2, 2, 1 - p)
    to_near(3, 3, 1 - p)
    strip_1 = remote(strip.at[1 - b], nstrip, rt, (near, x))
    to_near(6, 2, p)
    for slot in (0, 1):
        firsts[4 + slot].wait_recv()
        level_1(slot, p)
    remote(fv.at[0, 8:72, :], hv.at[1], rx.at[1], below)
    remote(fv.at[1, 8:72, :], hv.at[0], rx.at[1], above)
    passed_on(2)
    passed_on(3)
    to_near(7, 3, p)
    strip_1.wait_recv()
    ustrip[...] = (strip[b] + nstrip[...]) * ROOT
    strip_2 = remote(ustrip.at[rows(8 - 8 * p, 8), :], nustrip, ru_sem, (far, x))
    details = (strip[b] - nstrip[...]) * (ROOT * near_sign)
    for slot in range(4):
        fv[slot, 7:8, :] = details[slot : slot + 1] * rv[slot, 7:8, :]
        fv[slot, 72:73, :] = details[12 + slot : 13 + slot] * rv[slot, 72:73, :]
    level_2(0)
    level_2(1)
    remote(fu.at[:, 0, 8:40, :], hu.at[1], rx.at[2], below)
    remote(fu.at[:, 1, 8:40, :], hu.at[0], rx.at[2], above)

    def second_pass(f, weight, low_rim, high_rim, at, count, order, done):
        center = rows(at + 8, count)
        total, outer = None, None
        for plane in order:
            slot = SLOT[plane]
            mid, beside = beside_yz(f[slot, rows(at, count + 16), :])
            low = f[SLOT[plane - 1], center, :] if plane > 0 else low_rim() * keep_low
            high = f[SLOT[plane + 1], center, :] if plane < 3 else high_rim() * keep_high
            second = 1.2 * mid + weight[slot, center, :] * (beside + (low + high))
            done(slot, second)
            q = second - OMEGA * mid
            total = q if total is None else total + q
            if plane in (0, 3):
                rim = q * (edge_low if plane == 0 else edge_high)
                outer = rim if outer is None else outer + rim
        return total, outer

    absorb(hd, rx.at[0])

    def odd_rows(step, _):
        at = 32 * step
        here = rows(at, 32)

        def done(slot, second):
            sd[slot, here, :] = second

        summed, outer = second_pass(
            fd, rd, lambda: hd[0, here, :], lambda: hd[1, here, :], at, 32, range(4), done
        )
        center = rows(at + 8, 32)
        waves = (own[0, center, :] - other[0, center, :]) + (own[1, center, :] - other[1, center, :])
        waves = waves + (own[2, center, :] - other[2, center, :]) + (own[3, center, :] - other[3, center, :])
        t_d[here, :] = summed
        x_d[here, :] = (0.04 * scale) * waves - outer
        return 0

    lax.fori_loop(0, 4, odd_rows, 0)
    for slot in (2, 3):
        firsts[4 + slot].wait_recv()
        level_1(slot, p)

    def near_rows(step, _):
        at = 32 * step
        here = rows(at, 32)

        def done(slot, second):
            sv[slot, here, :] = second

        summed, outer = second_pass(
            fv, rv, lambda: hv[0, here, :], lambda: hv[1, here, :], at, 32, range(4), done
        )
        t_uv[here, :] = summed
        x_uv[here, :] = 0.04 * x_uv[here, :] - outer
        return 0

    absorb(hv, rx.at[1])
    lax.fori_loop(0, 2, near_rows, 0)

    strip_2.wait_recv()
    here = ustrip[rows(8 * p, 8), :]
    low, high = (here + nustrip[...]) * ROOT, (here - nustrip[...]) * (ROOT * far_sign)
    for slot in range(4):
        for j, rim in enumerate((low, high)):
            fu[j, slot, 7:8, :] = rim[slot : slot + 1] * ru[j, slot, 7:8, :]
            fu[j, slot, 40:41, :] = rim[4 + slot : 5 + slot] * ru[j, slot, 40:41, :]
    level_2(2)
    level_2(3)

    backs_2 = {}

    def far_rows(plane):
        made = []
        for j, at in ((0, slice(64, 96)), (1, slice(96, 128))):
            summed, outer = second_pass(
                fu.at[j], ru.at[j], lambda: hu[0, j], lambda: hu[1, j], 0, 32, (plane,),
                lambda slot, second: made.append(second),
            )
            t_uv[at, :] = summed if plane == 1 else t_uv[at, :] + summed
            if plane == 1:
                x_uv[at, :] = 0.04 * x_uv[at, :]
            if outer is not None:
                x_uv[at, :] = x_uv[at, :] - outer
        slot = SLOT[plane]
        low, high = made[0] * ROOT, made[1] * (ROOT * far_sign)
        give[slot] = low - high
        ub_own[slot] = low + high
        backs_2[slot] = remote(give.at[slot], ub.at[slot], rb2.at[slot], (far, x))

    def join(slot, q, ref):
        low, high = ref[slot] * ROOT, sv[slot, rows(32 * q, 32), :] * (ROOT * near_sign)
        gives[slot, rows(32 * q, 32), :] = low - high
        bk[slot, rows(64 * b + 32 * q, 32), :] = low + high
        remote(
            gives.at[slot, rows(32 * q, 32), :], bk.at[slot, rows(64 * b + 32 * q, 32), :],
            rb1.at[slot], (near, x),
        )

    def rest(slot):
        backs_2[slot].wait_recv()
        join(slot, 1 - p, ub)

    far_rows(1)
    far_rows(2)
    absorb(hu, rx.at[2])
    far_rows(0)
    far_rows(3)

    y_at, y_row = iota((32, 128), 1), iota((32, 128), 0)
    start = jnp.where(y_at < 64, 0, 16 + 8 * ((y_at - 64) // 32))
    y_in = jnp.where(y_at < 64, y_at, y_at % 32)
    inner = ones_where(start + y_in // 8 + 1 == y_row)
    beside = ones_where(start + (y_in + 7) // 8 == y_row) + ones_where(start + (y_in + 1) // 8 + 1 == y_row)
    sums = dot(inner, dot(x_uv[...], blocks[0]) + dot(t_uv[...], blocks[1])) + dot(beside, dot(t_uv[...], blocks[0]))
    uv_sums[...] = (sums[16:24] + pltpu.roll(sums[24:32], 32, 1)) + (
        pltpu.roll(sums[0:8], 64, 1) + pltpu.roll(sums[8:16], 96, 1)
    )
    for m, peer in enumerate(x_peers):
        remote(uv_sums, uv_x.at[m], rc, (t, peer))
    for slot in (2, 3, 0, 1):
        join(slot, p, ub_own)
    y_at, y_row = iota((24, 128), 1), iota((24, 128), 0)
    inner = ones_where(y_at // 8 + 1 == y_row)
    beside = ones_where((y_at + 7) // 8 == y_row) + ones_where((y_at + 1) // 8 + 1 == y_row)
    sums = dot(inner, dot(x_d[...], blocks[0]) + dot(t_d[...], blocks[1])) + dot(beside, dot(t_d[...], blocks[0]))
    d_sums[...] = pltpu.roll(sums, 96, 1)
    for m, peer in enumerate(x_peers):
        remote(d_sums, d_x.at[m], rdx, (t, peer))

    absorb(uv_x, rc)
    uv_total[...] = (uv_sums[...] + uv_x[0]) + (uv_x[1] + uv_x[2])
    for peer in group:
        remote(uv_total, tr.at[e], rg, (peer, x))
    tr[e] = uv_total[...]
    rest(2)
    rest(3)
    absorb(d_x, rdx)
    absorb(pot_all.at[1:4], rp)
    d_total[...] = (d_sums[...] + d_x[0]) + (d_x[1] + d_x[2])
    d_swap = remote(d_total, d_other, rdp, (partner, x))

    def finish(slot, start):
        here = rows(start, 64)
        even, odd = bk[slot, here, :], sd[slot, here, :] * sign
        yours[slot, here, :] = (even - odd) * ROOT
        there = out.at[0, PLANES[slot], rows(128 * k + start, 64), :]
        remote(yours.at[slot, here, :], there, ro, (partner, x))
        mine[slot, here, :] = (even + odd) * ROOT
        local(mine.at[slot, here, :], there, lo)

    rest(0)
    rest(1)
    for slot in (2, 3, 0, 1):
        finish(slot, 64 * b)

    def finish_far(slot):
        absorb(gives.at[slot], rb1.at[slot])
        finish(slot, 64 - 64 * b)

    for slot in (2, 3, 0, 1):
        finish_far(slot)
    absorb(tr.at[0:7], rg)
    d_swap.wait_recv()

    lane = iota((32, 128), 1)
    coef = lane // 32
    gathered = tr[...].reshape(64, 128)
    rem_v = dot(pick[1], gathered) + pltpu.roll(dot(pick[2], gathered), 96, 1)
    rem_d = dot(pick_d[0], d_total[...]) + dot(pick_d[1], d_other[...])
    rem = jnp.where(coef < 2, dot(pick[0], gathered), jnp.where(coef == 2, rem_v, rem_d))
    shift = jnp.where(
        coef == 0, shift_ref[3], jnp.where(coef == 1, shift_ref[2], jnp.where(coef == 2, shift_ref[1], shift_0))
    )
    coarse_pot = (pot_all[0] + pot_all[1]) + (pot_all[2] + pot_all[3])
    diag = coarse_pot + shift * 1024.0 + 640.0
    one = rem / diag
    row = iota((32, 128), 0)
    up = jnp.where(row == 0, 0.0, pltpu.roll(one, 1, 0))
    down = jnp.where(row == 31, 0.0, pltpu.roll(one, 31, 0))
    left = jnp.where(lane % 32 == 0, 0.0, pltpu.roll(one, 1, 1))
    right = jnp.where(lane % 32 == 31, 0.0, pltpu.roll(one, 127, 1))
    applied = diag * one - 128.0 * ((up + down) + (left + right))
    fix = one + (rem - applied) / diag
    weight = jnp.where(
        coef == 0, 0.5 * ROOT, jnp.where(coef == 1, 0.5 * ROOT * far_sign, jnp.where(coef == 2, 0.5 * near_sign, scale))
    )
    widen = ones_where(iota((128, 256), 0) % 32 == iota((128, 256), 1) // 8)
    fix_all[...] = dot(fix * weight, widen)
    fix_store = local(fix_all, fix_out, f_sem)

    absorb(all_sent, sent)
    absorb(yours, ro)
    absorb(mine, lo)
    fix_store.wait()


def shards(source, potential, level_shift):
    dma = pltpu.SemaphoreType.DMA
    vmem = lambda *shape: pltpu.VMEM(shape, F32)
    scratch = dict(
        shift_ref=pltpu.SMEM((4,), F32),
        own=vmem(4, 144, 256), other=vmem(4, 144, 256), pot=vmem(4, 144, 256), pot_other=vmem(4, 128, 256), s_buf=vmem(4, 144, 256),
        rd=vmem(4, 144, 256), fd=vmem(4, 144, 256), sd=vmem(4, 128, 256), strip=vmem(2, 16, 256),
        nb=vmem(4, 64, 256), nstrip=vmem(16, 256), u_buf=vmem(4, 80, 256), fv=vmem(4, 80, 256), rv=vmem(4, 80, 256),
        sv=vmem(4, 64, 256), ustrip=vmem(16, 256), nu=vmem(4, 32, 256), nustrip=vmem(8, 256),
        fu=vmem(2, 4, 48, 256), ru=vmem(2, 4, 48, 256),
        hd=vmem(2, 128, 256), hv=vmem(2, 64, 256), hu=vmem(2, 2, 32, 256),
        ub=vmem(4, 32, 256), ub_own=vmem(4, 32, 256), give=vmem(4, 32, 256), bk=vmem(4, 128, 256), gives=vmem(4, 64, 256),
        t_d=vmem(128, 256), x_d=vmem(128, 256), t_uv=vmem(128, 256), x_uv=vmem(128, 256),
        pot_all=vmem(4, 32, 128), d_sums=vmem(24, 128), d_x=vmem(3, 24, 128), d_total=vmem(24, 128),
        d_other=vmem(24, 128), uv_sums=vmem(8, 128), uv_x=vmem(3, 8, 128), uv_total=vmem(8, 128),
        tr=vmem(8, 8, 128), blocks=vmem(2, 256, 128), pick=vmem(3, 32, 64), pick_d=vmem(2, 32, 24),
        fix_all=vmem(32, 256), mine=vmem(4, 128, 256), yours=vmem(4, 128, 256),
        all_sent=vmem(2496, 256),
        h_sem=dma(()), l_sem=dma(()), p_sem=dma(()), q_sem=dma(()), f_sem=dma(()), sent=dma(()), r0=dma((4,)), r1=dma((8,)),
        r2=dma((4,)), rt=dma(()), ru_sem=dma(()), rx=dma((3,)), rp=dma(()), rdx=dma(()), rdp=dma(()), rc=dma(()),
        rg=dma(()), rb2=dma((4,)), rb1=dma((4,)), ro=dma(()), lo=dma(()),
    )
    raw, fix = pl.pallas_call(
        kernel,
        out_shape=(jax.ShapeDtypeStruct(source.shape, F32), jax.ShapeDtypeStruct((32, 256), F32)),
        in_specs=[
            pl.BlockSpec(memory_space=pltpu.HBM),
            pl.BlockSpec(memory_space=pltpu.HBM),
            pl.BlockSpec(memory_space=pltpu.HBM),
        ],
        out_specs=(pl.BlockSpec(memory_space=pl.ANY), pl.BlockSpec(memory_space=pl.ANY)),
        scratch_shapes=list(scratch.values()),
        compiler_params=pltpu.CompilerParams(
            collective_id=0, has_side_effects=True, vmem_limit_bytes=40 * 2**20
        ),
        name="space_time_apply",
    )(*(pltpu.with_memory_space_constraint(a, pltpu.HBM) for a in (level_shift, source, potential)))
    return (raw.reshape(4, 32, 8, 256) + fix[None, :, None, :]).reshape(source.shape)


def solution(mesh):
    in_specs = (P("tm", "plane", None, None), P("plane", None, None), P())
    out_specs = P("tm", "plane", None, None)
    return jax.shard_map(shards, mesh=mesh, in_specs=in_specs, out_specs=out_specs, check_vma=False)
```

```python
import math

import jax
import jax.numpy as jnp
from jax import lax
from jax.experimental import pallas as pl
from jax.experimental.pallas import tpu as pltpu
from jax.sharding import PartitionSpec as P

F32 = jnp.float32
MESH = pl.DeviceIdType.MESH
ROOT = 1.0 / math.sqrt(2.0)
OMEGA = 0.8
PLANES = (0, 3, 1, 2)
SLOT = {plane: slot for slot, plane in enumerate(PLANES)}


def dot(a, b):
    return jnp.dot(a, b, precision=lax.Precision.HIGHEST, preferred_element_type=F32)


def iota(shape, dim):
    return lax.broadcasted_iota(jnp.int32, shape, dim)


def ones_where(mask):
    return jnp.where(mask, 1.0, 0.0).astype(F32)


def beside_yz(ext):
    rows = ext.shape[0] - 16
    mid = ext[8 : 8 + rows]
    up = pltpu.roll(ext, 1, 0)[8 : 8 + rows]
    down = pltpu.roll(ext, rows + 15, 0)[8 : 8 + rows]
    col = iota(mid.shape, 1)
    left = jnp.where(col == 0, 0.0, pltpu.roll(mid, 1, 1))
    right = jnp.where(col == 255, 0.0, pltpu.roll(mid, 255, 1))
    return mid, (up + down) + (left + right)


def kernel(
    shift_hbm, source, potential, out, fix_out,
    shift_ref, own, other, pot, pot_other, s_buf, rd, fd, sd, strip, nb, nstrip, u_buf, fv, rv, sv, ustrip, nu, nustrip, fu, ru,
    hd, hv, hu, ub, ub_own, give, bk, gives, t_d, x_d, t_uv, x_uv, pot_all, d_sums, d_x, d_total, d_other, uv_sums, uv_x, uv_total,
    tr, blocks, pick, pick_d, fix_all, mine, yours,
    all_sent, h_sem, l_sem, p_sem, q_sem, f_sem, sent, r0, r1, r2, rt, ru_sem, rxd, rxv, rxu, rp, rdx, rdp, rc, rg, rb2, rb1, ro, lo,
):
    t, x = lax.axis_index("tm"), lax.axis_index("plane")
    e = t % 8
    k, c = e % 2, e // 2
    b, p = c % 2, c // 2
    partner = t + 1 - 2 * k
    near = t + 2 - 4 * b
    far = t + 4 - 8 * p
    x_peers = [(x + m) % 4 for m in (1, 2, 3)]
    group = [t - e + (e + m) % 8 for m in range(1, 8)]

    barrier = pltpu.get_barrier_semaphore()
    for peer in group:
        pl.semaphore_signal(barrier, inc=1, device_id=(peer, x), device_id_type=MESH)
    for peer in x_peers:
        pl.semaphore_signal(barrier, inc=1, device_id=(t, peer), device_id_type=MESH)

    def rows(start, count):
        return pl.ds(pl.multiple_of(start, 8), count)

    def remote(src, dst, recv, where):
        copy = pltpu.make_async_remote_copy(
            src_ref=src, dst_ref=dst, send_sem=sent, recv_sem=recv, device_id=where, device_id_type=MESH
        )
        copy.start()
        return copy

    def absorb(ref, sem):
        pltpu.make_async_copy(ref, ref, sem).wait()

    def local(src, dst, sem):
        copy = pltpu.make_async_copy(src, dst, sem)
        copy.start()
        return copy

    for slot, plane in enumerate(PLANES):
        local(source.at[0, plane, rows(120 * k, 136), :], own.at[slot, rows(8 - 8 * k, 136), :], l_sem)
    shift_load = local(shift_hbm, shift_ref, h_sem)
    for slot, plane in enumerate(PLANES):
        local(potential.at[plane, rows(120 * k, 136), :], pot.at[slot, rows(8 - 8 * k, 136), :], p_sem)
    rest_load = local(potential.at[:, rows(128 - 128 * k, 128), :], pot_other, q_sem)
    for slot in range(4):
        for ref in (own, other, pot):
            ref[slot, rows(136 * k, 8), :] = jnp.zeros((8, 256), F32)

    pl.semaphore_wait(barrier, 10)

    swaps = [
        remote(
            source.at[0, plane, rows(120 - 120 * k, 136), :], other.at[slot, rows(8 * k, 136), :],
            r0.at[slot], (partner, x),
        )
        for slot, plane in enumerate(PLANES)
    ]

    def to_near(index, slot, q):
        firsts[index] = remote(
            s_buf.at[slot, rows(72 - 64 * b + 32 * q, 32), :], nb.at[slot, rows(32 * q, 32), :],
            r1.at[index], (near, x),
        )

    firsts = {}
    absorb(own.at[:, 0:136, :], l_sem)
    for slot in range(4):
        swaps[slot].wait_recv()
        s_buf[slot] = (own[slot] + other[slot]) * ROOT
        if slot < 2:
            to_near(slot, slot, 1 - p)
    for h in range(2):
        for i in range(4):
            for at, row in ((0, 7), (4, 40), (8, 39), (12, 72)):
                strip[h, at + i : at + i + 1, :] = s_buf[i, row + 64 * h : row + 64 * h + 1, :]
    strip_1 = remote(strip.at[1 - b], nstrip, rt, (near, x))
    to_near(2, 2, 1 - p)
    to_near(3, 3, 1 - p)

    sign = (1 - 2 * k).astype(F32)
    near_sign = (1 - 2 * b).astype(F32)
    far_sign = (1 - 2 * p).astype(F32)
    scale = ROOT * sign
    edge_low, edge_high = ones_where(x == 0), ones_where(x == 3)
    shift_load.wait()
    shift_0 = shift_ref[0]
    absorb(pot.at[:, 0:136, :], p_sem)
    for slot in range(4):
        rd[slot] = OMEGA / (6.0 + pot[slot] + shift_0)
        fd[slot] = (own[slot] - other[slot]) * scale * rd[slot]

    def to_side(src, halo, end, sem):
        @pl.when(x < 3 if end == 0 else x > 0)
        def _():
            remote(src, halo.at[end], sem.at[end], (t, x + 1 - 2 * end))

    def from_sides(halo, sem):
        for end in range(2):
            pl.when(x > 0 if end == 0 else x < 3)(lambda end=end: absorb(halo.at[end], sem.at[end]))

    for end in range(2):
        @pl.when(x == 3 * end)
        def _():
            hd[end] = jnp.zeros((128, 256), F32)
            hv[end] = jnp.zeros((64, 256), F32)
            hu[end] = jnp.zeros((2, 32, 256), F32)

    to_side(fd.at[0, 8:136, :], hd, 1, rxd)
    to_side(fd.at[1, 8:136, :], hd, 0, rxd)

    for slot in range(4):
        rv[slot] = OMEGA / (6.0 + pot[slot, rows(64 * b, 80), :] + shift_ref[1])
        here = 6.0 + pot[slot, rows(64 * b + 32 * p, 48), :]
        ru[0, slot] = OMEGA / (here + shift_ref[3])
        ru[1, slot] = OMEGA / (here + shift_ref[2])

    z_at, z_block = iota((256, 128), 0), iota((256, 128), 1)
    lane_block = ones_where(z_at // 8 == z_block % 32)
    row, col = iota((32, 128), 0), iota((32, 128), 1)
    rest_load.wait()
    pot_sum = (pot[0, 8:136, :] + pot[1, 8:136, :]) + (pot[2, 8:136, :] + pot[3, 8:136, :])
    pot_rest = (pot_other[0] + pot_other[1]) + (pot_other[2] + pot_other[3])
    pot_all[0] = dot(ones_where(col // 8 + 16 * k == row), dot(pot_sum, lane_block)) + dot(
        ones_where(col // 8 + 16 - 16 * k == row), dot(pot_rest, lane_block)
    )
    for m, peer in enumerate(x_peers):
        remote(pot_all.at[0], pot_all.at[m + 1], rp, (t, peer))
    block = ones_where(z_at // 8 == z_block)
    around = ones_where((z_at + 7) // 8 == z_block + 1) + ones_where((z_at + 1) // 8 == z_block)
    blocks[0] = block
    blocks[1] = jnp.where(z_block < 32, 2.0 * block + around, 0.0)

    row, col = iota((32, 64), 0), iota((32, 64), 1)
    sender, r = col // 8, col % 8
    sender_c = sender // 2
    sender_b, sender_p = sender_c % 2, sender_c // 2
    sender_at = 16 * (sender % 2) + 8 * sender_b - 1 + r
    pick[0] = ones_where((r < 6) & (sender_at + 4 * sender_p == row))
    pick[1] = ones_where((sender_p == p) & (sender_at == row))
    pick[2] = ones_where((sender_p == p) & (r < 2) & (sender_at + 8 == row))
    row, col = iota((32, 24), 0), iota((32, 24), 1)
    pick_d[0] = ones_where((col < 18) & (16 * k - 1 + col == row))
    pick_d[1] = ones_where((col < 18) & (16 * (1 - k) - 1 + col == row))

    def level_1(slot, q):
        here = s_buf[slot, rows(8 + 64 * b + 32 * q, 32), :]
        there = nb[slot, rows(32 * q, 32), :]
        at = rows(8 + 32 * q, 32)
        u_buf[slot, at, :] = (here + there) * ROOT
        detail = (here - there) * (ROOT * near_sign)
        fv[slot, at, :] = detail * rv[slot, at, :]
        at = rows(32 * q, 32)
        x_uv[at, :] = detail if slot == 0 else x_uv[at, :] + detail

    seconds = {}

    def passed_on(slot):
        firsts[slot].wait_recv()
        level_1(slot, 1 - p)
        seconds[slot] = remote(
            u_buf.at[slot, rows(40 - 32 * p, 32), :], nu.at[slot], r2.at[slot], (far, x)
        )

    def level_2(slot):
        seconds[slot].wait_recv()
        here = u_buf[slot, rows(8 + 32 * p, 32), :]
        low, high = (here + nu[slot]) * ROOT, (here - nu[slot]) * (ROOT * far_sign)
        fu[0, slot, 8:40, :] = low * ru[0, slot, 8:40, :]
        fu[1, slot, 8:40, :] = high * ru[1, slot, 8:40, :]
        for at, field in ((64, low), (96, high)):
            x_uv[at : at + 32, :] = field if slot == 0 else x_uv[at : at + 32, :] + field

    for slot in range(4):
        passed_on(slot)
        for other_slot in ((0,), (1,), (), (2, 3))[slot]:
            to_near(4 + other_slot, other_slot, p)
        if slot == 0:
            strip_1.wait_recv()
            ustrip[...] = (strip[b] + nstrip[...]) * ROOT
            strip_2 = remote(ustrip.at[rows(8 - 8 * p, 8), :], nustrip, ru_sem, (far, x))
    details = (strip[b] - nstrip[...]) * (ROOT * near_sign)
    for slot in range(4):
        fv[slot, 7:8, :] = details[slot : slot + 1] * rv[slot, 7:8, :]
        fv[slot, 72:73, :] = details[12 + slot : 13 + slot] * rv[slot, 72:73, :]
    for slot, end in ((0, 1), (1, 0)):
        firsts[4 + slot].wait_recv()
        level_1(slot, p)
        level_2(slot)
        to_side(fu.at[:, slot, 8:40, :], hu, end, rxu)
        to_side(fv.at[slot, 8:72, :], hv, end, rxv)

    def second_pass(f, weight, low_rim, high_rim, at, count, order, done):
        center = rows(at + 8, count)
        total, outer = None, None
        for plane in order:
            slot = SLOT[plane]
            mid, beside = beside_yz(f[slot, rows(at, count + 16), :])
            low = f[SLOT[plane - 1], center, :] if plane > 0 else low_rim()
            high = f[SLOT[plane + 1], center, :] if plane < 3 else high_rim()
            second = 1.2 * mid + weight[slot, center, :] * (beside + (low + high))
            done(slot, second)
            q = second - OMEGA * mid
            total = q if total is None else total + q
            if plane in (0, 3):
                rim = q * (edge_low if plane == 0 else edge_high)
                outer = rim if outer is None else outer + rim
        return total, outer

    from_sides(hd, rxd)

    def odd_rows(step, _):
        at = 32 * step
        here = rows(at, 32)

        def done(slot, second):
            sd[slot, here, :] = second

        summed, outer = second_pass(
            fd, rd, lambda: hd[0, here, :], lambda: hd[1, here, :], at, 32, range(4), done
        )
        center = rows(at + 8, 32)
        waves = (own[0, center, :] - other[0, center, :]) + (own[1, center, :] - other[1, center, :])
        waves = waves + (own[2, center, :] - other[2, center, :]) + (own[3, center, :] - other[3, center, :])
        t_d[here, :] = summed
        x_d[here, :] = (0.04 * scale) * waves - outer
        return 0

    lax.fori_loop(0, 4, odd_rows, 0)
    y_at, y_row = iota((24, 128), 1), iota((24, 128), 0)
    inner = ones_where(y_at // 8 + 1 == y_row)
    beside = ones_where((y_at + 7) // 8 == y_row) + ones_where((y_at + 1) // 8 + 1 == y_row)
    sums = dot(inner, dot(x_d[...], blocks[0]) + dot(t_d[...], blocks[1])) + dot(beside, dot(t_d[...], blocks[0]))
    d_sums[...] = pltpu.roll(sums, 96, 1)
    for m, peer in enumerate(x_peers):
        remote(d_sums, d_x.at[m], rdx, (t, peer))

    strip_2.wait_recv()
    here = ustrip[rows(8 * p, 8), :]
    low, high = (here + nustrip[...]) * ROOT, (here - nustrip[...]) * (ROOT * far_sign)
    for slot in range(4):
        for j, rim in enumerate((low, high)):
            fu[j, slot, 7:8, :] = rim[slot : slot + 1] * ru[j, slot, 7:8, :]
            fu[j, slot, 40:41, :] = rim[4 + slot : 5 + slot] * ru[j, slot, 40:41, :]
    for slot in (2, 3):
        firsts[4 + slot].wait_recv()
        level_1(slot, p)
        level_2(slot)

    def near_rows(planes):
        def body(step, _):
            at = 32 * step
            here = rows(at, 32)

            def done(slot, second):
                sv[slot, here, :] = second

            summed, outer = second_pass(
                fv, rv, lambda: hv[0, here, :], lambda: hv[1, here, :], at, 32, planes, done
            )
            t_uv[here, :] = summed if outer is None else t_uv[here, :] + summed
            x_uv[here, :] = 0.04 * x_uv[here, :] if outer is None else x_uv[here, :] - outer
            return 0

        lax.fori_loop(0, 2, body, 0)

    backs_2 = {}

    def far_rows(plane):
        made = []
        for j, at in ((0, slice(64, 96)), (1, slice(96, 128))):
            summed, outer = second_pass(
                fu.at[j], ru.at[j], lambda: hu[0, j], lambda: hu[1, j], 0, 32, (plane,),
                lambda slot, second: made.append(second),
            )
            t_uv[at, :] = summed if plane == 1 else t_uv[at, :] + summed
            if plane == 1:
                x_uv[at, :] = 0.04 * x_uv[at, :]
            if outer is not None:
                x_uv[at, :] = x_uv[at, :] - outer
        slot = SLOT[plane]
        low, high = made[0] * ROOT, made[1] * (ROOT * far_sign)
        give[slot] = low - high
        ub_own[slot] = low + high
        backs_2[slot] = remote(give.at[slot], ub.at[slot], rb2.at[slot], (far, x))

    def join(slot, q, ref):
        low, high = ref[slot] * ROOT, sv[slot, rows(32 * q, 32), :] * (ROOT * near_sign)
        gives[slot, rows(32 * q, 32), :] = low - high
        bk[slot, rows(64 * b + 32 * q, 32), :] = low + high
        remote(
            gives.at[slot, rows(32 * q, 32), :], bk.at[slot, rows(64 * b + 32 * q, 32), :],
            rb1.at[slot], (near, x),
        )

    def rest(slot):
        backs_2[slot].wait_recv()
        join(slot, 1 - p, ub)

    far_rows(1)
    far_rows(2)
    near_rows((1, 2))
    join(2, p, ub_own)
    join(3, p, ub_own)
    from_sides(hu, rxu)
    far_rows(0)
    far_rows(3)
    from_sides(hv, rxv)
    near_rows((0, 3))

    y_at, y_row = iota((32, 128), 1), iota((32, 128), 0)
    start = jnp.where(y_at < 64, 0, 16 + 8 * ((y_at - 64) // 32))
    y_in = jnp.where(y_at < 64, y_at, y_at % 32)
    inner = ones_where(start + y_in // 8 + 1 == y_row)
    beside = ones_where(start + (y_in + 7) // 8 == y_row) + ones_where(start + (y_in + 1) // 8 + 1 == y_row)
    sums = dot(inner, dot(x_uv[...], blocks[0]) + dot(t_uv[...], blocks[1])) + dot(beside, dot(t_uv[...], blocks[0]))
    uv_sums[...] = (sums[16:24] + pltpu.roll(sums[24:32], 32, 1)) + (
        pltpu.roll(sums[0:8], 64, 1) + pltpu.roll(sums[8:16], 96, 1)
    )
    for m, peer in enumerate(x_peers):
        remote(uv_sums, uv_x.at[m], rc, (t, peer))
    join(0, p, ub_own)
    join(1, p, ub_own)
    absorb(uv_x, rc)
    uv_total[...] = (uv_sums[...] + uv_x[0]) + (uv_x[1] + uv_x[2])
    for peer in group:
        remote(uv_total, tr.at[e], rg, (peer, x))
    tr[e] = uv_total[...]
    rest(2)
    rest(3)
    absorb(d_x, rdx)
    absorb(pot_all.at[1:4], rp)
    d_total[...] = (d_sums[...] + d_x[0]) + (d_x[1] + d_x[2])
    d_swap = remote(d_total, d_other, rdp, (partner, x))

    def finish(slot, start):
        here = rows(start, 64)
        even, odd = bk[slot, here, :], sd[slot, here, :] * sign
        yours[slot, here, :] = (even - odd) * ROOT
        there = out.at[0, PLANES[slot], rows(128 * k + start, 64), :]
        remote(yours.at[slot, here, :], there, ro, (partner, x))
        mine[slot, here, :] = (even + odd) * ROOT
        local(mine.at[slot, here, :], there, lo)

    rest(0)
    rest(1)
    for slot in (2, 3, 0, 1):
        finish(slot, 64 * b)

    def finish_far(slot):
        absorb(gives.at[slot], rb1.at[slot])
        finish(slot, 64 - 64 * b)

    for slot in (2, 3, 0, 1):
        finish_far(slot)
    absorb(tr.at[0:7], rg)
    d_swap.wait_recv()

    lane = iota((32, 128), 1)
    coef = lane // 32
    gathered = tr[...].reshape(64, 128)
    rem_v = dot(pick[1], gathered) + pltpu.roll(dot(pick[2], gathered), 96, 1)
    rem_d = dot(pick_d[0], d_total[...]) + dot(pick_d[1], d_other[...])
    rem = jnp.where(coef < 2, dot(pick[0], gathered), jnp.where(coef == 2, rem_v, rem_d))
    shift = jnp.where(
        coef == 0, shift_ref[3], jnp.where(coef == 1, shift_ref[2], jnp.where(coef == 2, shift_ref[1], shift_0))
    )
    coarse_pot = (pot_all[0] + pot_all[1]) + (pot_all[2] + pot_all[3])
    diag = coarse_pot + shift * 1024.0 + 640.0
    one = rem / diag
    row = iota((32, 128), 0)
    up = jnp.where(row == 0, 0.0, pltpu.roll(one, 1, 0))
    down = jnp.where(row == 31, 0.0, pltpu.roll(one, 31, 0))
    left = jnp.where(lane % 32 == 0, 0.0, pltpu.roll(one, 1, 1))
    right = jnp.where(lane % 32 == 31, 0.0, pltpu.roll(one, 127, 1))
    applied = diag * one - 128.0 * ((up + down) + (left + right))
    fix = one + (rem - applied) / diag
    weight = jnp.where(
        coef == 0, 0.5 * ROOT, jnp.where(coef == 1, 0.5 * ROOT * far_sign, jnp.where(coef == 2, 0.5 * near_sign, scale))
    )
    widen = ones_where(iota((128, 256), 0) % 32 == iota((128, 256), 1) // 8)
    fix_all[...] = dot(fix * weight, widen)
    fix_store = local(fix_all, fix_out, f_sem)

    outer = (x == 0) | (x == 3)
    pl.when(outer)(lambda: absorb(all_sent.at[0:2240, :], sent))
    pl.when(jnp.logical_not(outer))(lambda: absorb(all_sent, sent))
    absorb(yours, ro)
    absorb(mine, lo)
    fix_store.wait()


def shards(source, potential, level_shift):
    dma = pltpu.SemaphoreType.DMA
    vmem = lambda *shape: pltpu.VMEM(shape, F32)
    scratch = dict(
        shift_ref=pltpu.SMEM((4,), F32),
        own=vmem(4, 144, 256), other=vmem(4, 144, 256), pot=vmem(4, 144, 256), pot_other=vmem(4, 128, 256), s_buf=vmem(4, 144, 256),
        rd=vmem(4, 144, 256), fd=vmem(4, 144, 256), sd=vmem(4, 128, 256), strip=vmem(2, 16, 256),
        nb=vmem(4, 64, 256), nstrip=vmem(16, 256), u_buf=vmem(4, 80, 256), fv=vmem(4, 80, 256), rv=vmem(4, 80, 256),
        sv=vmem(4, 64, 256), ustrip=vmem(16, 256), nu=vmem(4, 32, 256), nustrip=vmem(8, 256),
        fu=vmem(2, 4, 48, 256), ru=vmem(2, 4, 48, 256),
        hd=vmem(2, 128, 256), hv=vmem(2, 64, 256), hu=vmem(2, 2, 32, 256),
        ub=vmem(4, 32, 256), ub_own=vmem(4, 32, 256), give=vmem(4, 32, 256), bk=vmem(4, 128, 256), gives=vmem(4, 64, 256),
        t_d=vmem(128, 256), x_d=vmem(128, 256), t_uv=vmem(128, 256), x_uv=vmem(128, 256),
        pot_all=vmem(4, 32, 128), d_sums=vmem(24, 128), d_x=vmem(3, 24, 128), d_total=vmem(24, 128),
        d_other=vmem(24, 128), uv_sums=vmem(8, 128), uv_x=vmem(3, 8, 128), uv_total=vmem(8, 128),
        tr=vmem(8, 8, 128), blocks=vmem(2, 256, 128), pick=vmem(3, 32, 64), pick_d=vmem(2, 32, 24),
        fix_all=vmem(32, 256), mine=vmem(4, 128, 256), yours=vmem(4, 128, 256),
        all_sent=vmem(2496, 256),
        h_sem=dma(()), l_sem=dma(()), p_sem=dma(()), q_sem=dma(()), f_sem=dma(()), sent=dma(()), r0=dma((4,)), r1=dma((8,)),
        r2=dma((4,)), rt=dma(()), ru_sem=dma(()), rxd=dma((2,)), rxv=dma((2,)), rxu=dma((2,)), rp=dma(()), rdx=dma(()), rdp=dma(()), rc=dma(()),
        rg=dma(()), rb2=dma((4,)), rb1=dma((4,)), ro=dma(()), lo=dma(()),
    )
    raw, fix = pl.pallas_call(
        kernel,
        out_shape=(jax.ShapeDtypeStruct(source.shape, F32), jax.ShapeDtypeStruct((32, 256), F32)),
        in_specs=[
            pl.BlockSpec(memory_space=pltpu.HBM),
            pl.BlockSpec(memory_space=pltpu.HBM),
            pl.BlockSpec(memory_space=pltpu.HBM),
        ],
        out_specs=(pl.BlockSpec(memory_space=pl.ANY), pl.BlockSpec(memory_space=pl.ANY)),
        scratch_shapes=list(scratch.values()),
        compiler_params=pltpu.CompilerParams(
            collective_id=0, has_side_effects=True, vmem_limit_bytes=40 * 2**20
        ),
        name="space_time_apply",
    )(*(pltpu.with_memory_space_constraint(a, pltpu.HBM) for a in (level_shift, source, potential)))
    return (raw.reshape(4, 32, 8, 256) + fix[None, :, None, :]).reshape(source.shape)


def solution(mesh):
    in_specs = (P("tm", "plane", None, None), P("plane", None, None), P())
    out_specs = P("tm", "plane", None, None)
    return jax.shard_map(shards, mesh=mesh, in_specs=in_specs, out_specs=out_specs, check_vma=False)
```

```python
import math

import jax
import jax.numpy as jnp
from jax import lax
from jax.experimental import pallas as pl
from jax.experimental.pallas import tpu as pltpu
from jax.sharding import PartitionSpec as P

F32 = jnp.float32
MESH = pl.DeviceIdType.MESH
ROOT = 1.0 / math.sqrt(2.0)
OMEGA = 0.8
PLANES = (0, 3, 1, 2)
SLOT = {plane: slot for slot, plane in enumerate(PLANES)}


def dot(a, b):
    return jnp.dot(a, b, precision=lax.Precision.HIGHEST, preferred_element_type=F32)


def iota(shape, dim):
    return lax.broadcasted_iota(jnp.int32, shape, dim)


def ones_where(mask):
    return jnp.where(mask, 1.0, 0.0).astype(F32)


def beside_yz(ext):
    rows = ext.shape[0] - 16
    mid = ext[8 : 8 + rows]
    up = pltpu.roll(ext, 1, 0)[8 : 8 + rows]
    down = pltpu.roll(ext, rows + 15, 0)[8 : 8 + rows]
    col = iota(mid.shape, 1)
    left = jnp.where(col == 0, 0.0, pltpu.roll(mid, 1, 1))
    right = jnp.where(col == 255, 0.0, pltpu.roll(mid, 255, 1))
    return mid, (up + down) + (left + right)


def kernel(
    shift_hbm, source, potential, out, fix_out,
    shift_ref, own, other, pot, pot_other, s_buf, rd, fd, sd, strip, nb, nstrip, u_buf, fv, rv, sv, ustrip, nu, nustrip, fu, ru,
    pot_side, wv, wu, base_v, base_u, hd, hv, hu, ub, ub_own, give, bk, gives, t_d, x_d, t_uv, x_uv, pot_all, d_sums, d_x, d_total, d_other, uv_sums, uv_x, uv_total,
    tr, blocks, pick, pick_d, fix_all, mine, yours,
    all_sent, h_sem, l_sem, p_sem, q_sem, f_sem, sent, r0, r1, r2, rt, ru_sem, rxp, rxd, rxv, rxu, rp, rdx, rdp, rc, rg, rb2, rb1, ro, lo,
):
    t, x = lax.axis_index("tm"), lax.axis_index("plane")
    e = t % 8
    k, c = e % 2, e // 2
    b, p = c % 2, c // 2
    partner = t + 1 - 2 * k
    near = t + 2 - 4 * b
    far = t + 4 - 8 * p
    x_peers = [(x + m) % 4 for m in (1, 2, 3)]
    group = [t - e + (e + m) % 8 for m in range(1, 8)]

    barrier = pltpu.get_barrier_semaphore()
    for peer in group:
        pl.semaphore_signal(barrier, inc=1, device_id=(peer, x), device_id_type=MESH)
    for peer in x_peers:
        pl.semaphore_signal(barrier, inc=1, device_id=(t, peer), device_id_type=MESH)

    def rows(start, count):
        return pl.ds(pl.multiple_of(start, 8), count)

    def remote(src, dst, recv, where):
        copy = pltpu.make_async_remote_copy(
            src_ref=src, dst_ref=dst, send_sem=sent, recv_sem=recv, device_id=where, device_id_type=MESH
        )
        copy.start()
        return copy

    def absorb(ref, sem):
        pltpu.make_async_copy(ref, ref, sem).wait()

    def local(src, dst, sem):
        copy = pltpu.make_async_copy(src, dst, sem)
        copy.start()
        return copy

    for slot, plane in enumerate(PLANES):
        local(source.at[0, plane, rows(120 * k, 136), :], own.at[slot, rows(8 - 8 * k, 136), :], l_sem)
    shift_load = local(shift_hbm, shift_ref, h_sem)
    for slot, plane in enumerate(PLANES):
        local(potential.at[plane, rows(120 * k, 136), :], pot.at[slot, rows(8 - 8 * k, 136), :], p_sem)
    rest_load = local(potential.at[:, rows(128 - 128 * k, 128), :], pot_other, q_sem)
    for slot in range(4):
        for ref in (own, other, pot):
            ref[slot, rows(136 * k, 8), :] = jnp.zeros((8, 256), F32)

    pl.semaphore_wait(barrier, 10)

    swaps = [
        remote(
            source.at[0, plane, rows(120 - 120 * k, 136), :], other.at[slot, rows(8 * k, 136), :],
            r0.at[slot], (partner, x),
        )
        for slot, plane in enumerate(PLANES)
    ]

    def to_side(src, halo, end, sem):
        @pl.when(x < 3 if end == 0 else x > 0)
        def _():
            remote(src, halo.at[end], sem.at[end], (t, x + 1 - 2 * end))

    def from_sides(halo, sem):
        for end in range(2):
            pl.when(x > 0 if end == 0 else x < 3)(lambda end=end: absorb(halo.at[end], sem.at[end]))

    for end in range(2):
        @pl.when(x == 3 * end)
        def _():
            hd[end] = jnp.zeros((128, 256), F32)
            hv[end] = jnp.zeros((64, 256), F32)
            hu[end] = jnp.zeros((2, 32, 256), F32)
            pot_side[end] = jnp.zeros((128, 256), F32)

    to_side(potential.at[0, rows(128 * k, 128), :], pot_side, 1, rxp)
    to_side(potential.at[3, rows(128 * k, 128), :], pot_side, 0, rxp)

    def to_near(index, slots, q, start=0, count=32):
        at = 32 * q + start
        firsts[index] = remote(
            s_buf.at[slots, rows(72 - 64 * b + at, count), :], nb.at[slots, rows(at, count), :],
            r1.at[index], (near, x),
        )

    firsts = {}
    absorb(own.at[:, 0:136, :], l_sem)
    for slot in range(4):
        swaps[slot].wait_recv()
        s_buf[slot] = (own[slot] + other[slot]) * ROOT
        if slot < 2:
            to_near(slot, slot, 1 - p)
    for h in range(2):
        for i in range(4):
            for at, row in ((0, 7), (4, 40), (8, 39), (12, 72)):
                strip[h, at + i : at + i + 1, :] = s_buf[i, row + 64 * h : row + 64 * h + 1, :]
    strip_1 = remote(strip.at[1 - b], nstrip, rt, (near, x))
    to_near(2, 2, 1 - p)
    to_near(3, 3, 1 - p)

    sign = (1 - 2 * k).astype(F32)
    near_sign = (1 - 2 * b).astype(F32)
    far_sign = (1 - 2 * p).astype(F32)
    scale = ROOT * sign
    edge_low, edge_high = ones_where(x == 0), ones_where(x == 3)
    shift_load.wait()
    shift_0 = shift_ref[0]
    absorb(pot.at[:, 0:136, :], p_sem)
    for slot in range(4):
        rd[slot] = OMEGA / (6.0 + pot[slot] + shift_0)
        fd[slot] = (own[slot] - other[slot]) * scale * rd[slot]


    to_side(fd.at[0, 8:136, :], hd, 1, rxd)
    to_side(fd.at[1, 8:136, :], hd, 0, rxd)

    for slot in range(4):
        rv[slot] = OMEGA / (6.0 + pot[slot, rows(64 * b, 80), :] + shift_ref[1])
        here = 6.0 + pot[slot, rows(64 * b + 32 * p, 48), :]
        ru[0, slot] = OMEGA / (here + shift_ref[3])
        ru[1, slot] = OMEGA / (here + shift_ref[2])

    z_at, z_block = iota((256, 128), 0), iota((256, 128), 1)
    lane_block = ones_where(z_at // 8 == z_block % 32)
    row, col = iota((32, 128), 0), iota((32, 128), 1)
    rest_load.wait()
    pot_sum = (pot[0, 8:136, :] + pot[1, 8:136, :]) + (pot[2, 8:136, :] + pot[3, 8:136, :])
    pot_rest = (pot_other[0] + pot_other[1]) + (pot_other[2] + pot_other[3])
    pot_all[0] = dot(ones_where(col // 8 + 16 * k == row), dot(pot_sum, lane_block)) + dot(
        ones_where(col // 8 + 16 - 16 * k == row), dot(pot_rest, lane_block)
    )
    for m, peer in enumerate(x_peers):
        remote(pot_all.at[0], pot_all.at[m + 1], rp, (t, peer))
    block = ones_where(z_at // 8 == z_block)
    around = ones_where((z_at + 7) // 8 == z_block + 1) + ones_where((z_at + 1) // 8 == z_block)
    blocks[0] = block
    blocks[1] = jnp.where(z_block < 32, 2.0 * block + around, 0.0)

    row, col = iota((32, 64), 0), iota((32, 64), 1)
    sender, r = col // 8, col % 8
    sender_c = sender // 2
    sender_b, sender_p = sender_c % 2, sender_c // 2
    sender_at = 16 * (sender % 2) + 8 * sender_b - 1 + r
    pick[0] = ones_where((r < 6) & (sender_at + 4 * sender_p == row))
    pick[1] = ones_where((sender_p == p) & (sender_at == row))
    pick[2] = ones_where((sender_p == p) & (r < 2) & (sender_at + 8 == row))
    row, col = iota((32, 24), 0), iota((32, 24), 1)
    pick_d[0] = ones_where((col < 18) & (16 * k - 1 + col == row))
    pick_d[1] = ones_where((col < 18) & (16 * (1 - k) - 1 + col == row))

    def level_1(slot, q, start=0, count=32):
        inside = 32 * q + start
        here = s_buf[slot, rows(8 + 64 * b + inside, count), :]
        there = nb[slot, rows(inside, count), :]
        at = rows(8 + inside, count)
        u_buf[slot, at, :] = (here + there) * ROOT
        detail = (here - there) * (ROOT * near_sign)
        fv[slot, at, :] = detail * rv[slot, at, :]
        at = rows(inside, count)
        x_uv[at, :] = detail if slot == 0 else x_uv[at, :] + detail

    seconds = {}

    def to_far(index, slots, start=0, count=32):
        seconds[index] = remote(
            u_buf.at[slots, rows(40 - 32 * p + start, count), :], nu.at[slots, start : start + count, :],
            r2.at[index], (far, x),
        )

    def passed_on(slot):
        firsts[slot].wait_recv()
        level_1(slot, 1 - p)
        to_far(slot, slot, 0, 32 if slot < 2 else 24)

    def level_2(slot, start=0, count=32):
        here = u_buf[slot, rows(8 + 32 * p + start, count), :]
        there = nu[slot, start : start + count, :]
        low, high = (here + there) * ROOT, (here - there) * (ROOT * far_sign)
        at = slice(8 + start, 8 + start + count)
        fu[0, slot, at, :] = low * ru[0, slot, at, :]
        fu[1, slot, at, :] = high * ru[1, slot, at, :]
        for first, field in ((64 + start, low), (96 + start, high)):
            at = slice(first, first + count)
            x_uv[at, :] = field if slot == 0 else x_uv[at, :] + field

    inner_slots = slice(2, 4)
    for slot in range(4):
        passed_on(slot)
        if slot < 2:
            to_near(4 + slot, slot, p)
        if slot == 0:
            strip_1.wait_recv()
            ustrip[...] = (strip[b] + nstrip[...]) * ROOT
            strip_2 = remote(ustrip.at[rows(8 - 8 * p, 8), :], nustrip, ru_sem, (far, x))
    to_near(6, 2, p, 0, 24)
    to_near(7, 3, p, 0, 24)
    to_far(4, inner_slots, 24, 8)
    to_near(8, inner_slots, p, 24, 8)
    details = (strip[b] - nstrip[...]) * (ROOT * near_sign)
    for slot in range(4):
        fv[slot, 7:8, :] = details[slot : slot + 1] * rv[slot, 7:8, :]
        fv[slot, 72:73, :] = details[12 + slot : 13 + slot] * rv[slot, 72:73, :]
        if slot > 1:
            fv[slot, 39:40, :] = details[8 + slot : 9 + slot] * rv[slot, 39:40, :]
    from_sides(pot_side, rxp)
    kept = [ones_where(x > 0), ones_where(x < 3)]

    def beside_weights(weight, start, count, shift, out):
        side = []
        for end in range(2):
            field = 6.0 + pot_side[end, rows(start, count), :] + shift
            side.append((OMEGA * kept[end]) / field)
        inner = [weight[SLOT[plane], 8 : 8 + count, :] for plane in range(4)]
        out[SLOT[0]] = side[0] + inner[1]
        out[SLOT[1]] = inner[0] + inner[2]
        out[SLOT[2]] = inner[1] + inner[3]
        out[SLOT[3]] = inner[2] + side[1]

    beside_weights(rv, 64 * b, 64, shift_ref[1], wv)
    for j, level in ((0, 3), (1, 2)):
        beside_weights(ru.at[j], 64 * b + 32 * p, 32, shift_ref[level], wu.at[j])

    for slot, end in ((0, 1), (1, 0)):
        firsts[4 + slot].wait_recv()
        level_1(slot, p)
        seconds[slot].wait_recv()
        level_2(slot)
        to_side(fu.at[:, slot, 8:40, :], hu, end, rxu)
        to_side(fv.at[slot, 8:72, :], hv, end, rxv)

    def second_pass(f, weight, low_rim, high_rim, at, count, order, done):
        center = rows(at + 8, count)
        total, outer = None, None
        for plane in order:
            slot = SLOT[plane]
            mid, beside = beside_yz(f[slot, rows(at, count + 16), :])
            low = f[SLOT[plane - 1], center, :] if plane > 0 else low_rim()
            high = f[SLOT[plane + 1], center, :] if plane < 3 else high_rim()
            second = 1.2 * mid + weight[slot, center, :] * (beside + (low + high))
            done(slot, second)
            q = second - OMEGA * mid
            total = q if total is None else total + q
            if plane in (0, 3):
                rim = q * (edge_low if plane == 0 else edge_high)
                outer = rim if outer is None else outer + rim
        return total, outer

    from_sides(hd, rxd)

    def odd_rows(step, _):
        at = 32 * step
        here = rows(at, 32)

        def done(slot, second):
            sd[slot, here, :] = second

        summed, outer = second_pass(
            fd, rd, lambda: hd[0, here, :], lambda: hd[1, here, :], at, 32, range(4), done
        )
        center = rows(at + 8, 32)
        waves = (own[0, center, :] - other[0, center, :]) + (own[1, center, :] - other[1, center, :])
        waves = waves + (own[2, center, :] - other[2, center, :]) + (own[3, center, :] - other[3, center, :])
        t_d[here, :] = summed
        x_d[here, :] = (0.04 * scale) * waves - outer
        return 0

    lax.fori_loop(0, 4, odd_rows, 0)
    y_at, y_row = iota((24, 128), 1), iota((24, 128), 0)
    inner = ones_where(y_at // 8 + 1 == y_row)
    beside = ones_where((y_at + 7) // 8 == y_row) + ones_where((y_at + 1) // 8 + 1 == y_row)
    sums = dot(inner, dot(x_d[...], blocks[0]) + dot(t_d[...], blocks[1])) + dot(beside, dot(t_d[...], blocks[0]))
    d_sums[...] = pltpu.roll(sums, 96, 1)
    for m, peer in enumerate(x_peers):
        remote(d_sums, d_x.at[m], rdx, (t, peer))

    strip_2.wait_recv()
    here = ustrip[rows(8 * p, 8), :]
    low, high = (here + nustrip[...]) * ROOT, (here - nustrip[...]) * (ROOT * far_sign)
    for slot in range(4):
        for j, rim in enumerate((low, high)):
            fu[j, slot, 7:8, :] = rim[slot : slot + 1] * ru[j, slot, 7:8, :]
            fu[j, slot, 40:41, :] = rim[4 + slot : 5 + slot] * ru[j, slot, 40:41, :]
    for slot in (2, 3):
        seconds[slot].wait_recv()
        firsts[4 + slot].wait_recv()
        level_1(slot, p, 0, 24)
        level_2(slot, 0, 24)

    def own_planes(f, weight, sides, base, at, count, planes):
        here, center = rows(at, count), rows(at + 8, count)
        total, outer = None, None
        for plane in planes:
            slot = SLOT[plane]
            mid, beside = beside_yz(f[slot, rows(at, count + 16), :])
            within = weight[slot, center, :] * beside
            base[slot, here, :] = 1.2 * mid + within
            within = 0.4 * mid + within
            q = within + mid * sides[slot, here, :]
            total = q if total is None else total + q
            if plane in (0, 3):
                next_in = f[SLOT[1 if plane == 0 else 2], center, :]
                rim = (within + weight[slot, center, :] * next_in) * (edge_low if plane == 0 else edge_high)
                outer = rim if outer is None else outer + rim
        return total, outer

    def with_sides(f, weight, base, halo, at, count, plane):
        here, center = rows(at, count), rows(at + 8, count)
        low = f[SLOT[plane - 1], center, :] if plane > 0 else halo(0)
        high = f[SLOT[plane + 1], center, :] if plane < 3 else halo(1)
        return base[SLOT[plane], here, :] + weight[SLOT[plane], center, :] * (low + high)

    def near_planes(planes, start, count):
        def body(step, _):
            here = rows(32 * step + start, count)
            summed, outer = own_planes(fv, rv, wv, base_v, 32 * step + start, count, planes)
            if outer is None:
                t_uv[here, :] = summed
            else:
                t_uv[here, :] += summed
                x_uv[here, :] = 0.04 * x_uv[here, :] - outer
            return 0

        lax.fori_loop(0, 2, body, 0)

    def near_rows(planes, start, count):
        def body(step, _):
            here = rows(32 * step + start, count)
            for plane in planes:
                sv[SLOT[plane], here, :] = with_sides(
                    fv, rv, base_v, lambda end: hv[end, here, :], 32 * step + start, count, plane
                )
            return 0

        lax.fori_loop(0, 2, body, 0)

    backs_2 = {}

    def far_planes(planes, start, count):
        for j in range(2):
            at = slice(64 + 32 * j + start, 64 + 32 * j + start + count)
            summed, outer = own_planes(fu.at[j], ru.at[j], wu.at[j], base_u.at[j], start, count, planes)
            if outer is None:
                t_uv[at, :] = summed
            else:
                t_uv[at, :] += summed
                x_uv[at, :] = 0.04 * x_uv[at, :] - outer

    def far_rows(plane, index, start=0, count=32):
        here = slice(start, start + count)
        made = [
            with_sides(fu.at[j], ru.at[j], base_u.at[j], lambda end, j=j: hu[end, j, here, :], start, count, plane)
            for j in range(2)
        ]
        slot = SLOT[plane]
        low, high = made[0] * ROOT, made[1] * (ROOT * far_sign)
        give[slot, here, :] = low - high
        ub_own[slot, here, :] = low + high
        backs_2[index] = remote(give.at[slot, here, :], ub.at[slot, here, :], rb2.at[index], (far, x))

    def join(slot, q, ref, start=0, count=32):
        at = 32 * q + start
        low = ref[slot, start : start + count, :] * ROOT
        high = sv[slot, rows(at, count), :] * (ROOT * near_sign)
        gives[slot, rows(at, count), :] = low - high
        bk[slot, rows(64 * b + at, count), :] = low + high
        remote(
            gives.at[slot, rows(at, count), :], bk.at[slot, rows(64 * b + at, count), :], rb1.at[slot], (near, x)
        )

    def rest(slot):
        backs_2[slot].wait_recv()
        if slot > 1:
            backs_2[2 + slot].wait_recv()
        join(slot, 1 - p, ub)

    def inner_rows(start):
        far_planes((1, 2), start, 16)
        far_rows(1, 2 + start // 8, start, 16)
        far_rows(2, 3 + start // 8, start, 16)
        near_planes((1, 2), start, 16)
        near_rows((1, 2), start, 16)
        join(2, p, ub_own, start, 16)
        join(3, p, ub_own, start, 16)

    inner_rows(0)
    seconds[4].wait_recv()
    firsts[8].wait_recv()
    for slot in (2, 3):
        level_1(slot, p, 24, 8)
        level_2(slot, 24, 8)
    inner_rows(16)
    far_planes((0, 3), 0, 32)
    near_planes((0, 3), 0, 32)

    y_at, y_row = iota((32, 128), 1), iota((32, 128), 0)
    start = jnp.where(y_at < 64, 0, 16 + 8 * ((y_at - 64) // 32))
    y_in = jnp.where(y_at < 64, y_at, y_at % 32)
    inner = ones_where(start + y_in // 8 + 1 == y_row)
    beside = ones_where(start + (y_in + 7) // 8 == y_row) + ones_where(start + (y_in + 1) // 8 + 1 == y_row)
    sums = dot(inner, dot(x_uv[...], blocks[0]) + dot(t_uv[...], blocks[1])) + dot(beside, dot(t_uv[...], blocks[0]))
    uv_sums[...] = (sums[16:24] + pltpu.roll(sums[24:32], 32, 1)) + (
        pltpu.roll(sums[0:8], 64, 1) + pltpu.roll(sums[8:16], 96, 1)
    )
    for m, peer in enumerate(x_peers):
        remote(uv_sums, uv_x.at[m], rc, (t, peer))
    from_sides(hu, rxu)
    far_rows(0, 0)
    far_rows(3, 1)
    from_sides(hv, rxv)
    near_rows((0, 3), 0, 32)
    join(0, p, ub_own)
    join(1, p, ub_own)
    rest(2)
    absorb(uv_x, rc)
    uv_total[...] = (uv_sums[...] + uv_x[0]) + (uv_x[1] + uv_x[2])
    for peer in group:
        remote(uv_total, tr.at[e], rg, (peer, x))
    tr[e] = uv_total[...]
    rest(3)
    absorb(d_x, rdx)
    absorb(pot_all.at[1:4], rp)
    d_total[...] = (d_sums[...] + d_x[0]) + (d_x[1] + d_x[2])
    d_swap = remote(d_total, d_other, rdp, (partner, x))

    def finish(slot, start):
        here = rows(start, 64)
        even, odd = bk[slot, here, :], sd[slot, here, :] * sign
        yours[slot, here, :] = (even - odd) * ROOT
        there = out.at[0, PLANES[slot], rows(128 * k + start, 64), :]
        remote(yours.at[slot, here, :], there, ro, (partner, x))
        mine[slot, here, :] = (even + odd) * ROOT
        local(mine.at[slot, here, :], there, lo)

    rest(0)
    rest(1)
    for slot in (2, 3, 0, 1):
        finish(slot, 64 * b)

    def finish_far(slot):
        absorb(gives.at[slot], rb1.at[slot])
        finish(slot, 64 - 64 * b)

    for slot in (2, 3, 0, 1):
        finish_far(slot)
    absorb(tr.at[0:7], rg)
    d_swap.wait_recv()

    lane = iota((32, 128), 1)
    coef = lane // 32
    gathered = tr[...].reshape(64, 128)
    rem_v = dot(pick[1], gathered) + pltpu.roll(dot(pick[2], gathered), 96, 1)
    rem_d = dot(pick_d[0], d_total[...]) + dot(pick_d[1], d_other[...])
    rem = jnp.where(coef < 2, dot(pick[0], gathered), jnp.where(coef == 2, rem_v, rem_d))
    shift = jnp.where(
        coef == 0, shift_ref[3], jnp.where(coef == 1, shift_ref[2], jnp.where(coef == 2, shift_ref[1], shift_0))
    )
    coarse_pot = (pot_all[0] + pot_all[1]) + (pot_all[2] + pot_all[3])
    diag = coarse_pot + shift * 1024.0 + 640.0
    one = rem / diag
    row = iota((32, 128), 0)
    up = jnp.where(row == 0, 0.0, pltpu.roll(one, 1, 0))
    down = jnp.where(row == 31, 0.0, pltpu.roll(one, 31, 0))
    left = jnp.where(lane % 32 == 0, 0.0, pltpu.roll(one, 1, 1))
    right = jnp.where(lane % 32 == 31, 0.0, pltpu.roll(one, 127, 1))
    applied = diag * one - 128.0 * ((up + down) + (left + right))
    fix = one + (rem - applied) / diag
    weight = jnp.where(
        coef == 0, 0.5 * ROOT, jnp.where(coef == 1, 0.5 * ROOT * far_sign, jnp.where(coef == 2, 0.5 * near_sign, scale))
    )
    widen = ones_where(iota((128, 256), 0) % 32 == iota((128, 256), 1) // 8)
    fix_all[...] = dot(fix * weight, widen)
    fix_store = local(fix_all, fix_out, f_sem)

    outer = (x == 0) | (x == 3)
    pl.when(outer)(lambda: absorb(all_sent.at[0:2368, :], sent))
    pl.when(jnp.logical_not(outer))(lambda: absorb(all_sent, sent))
    absorb(yours, ro)
    absorb(mine, lo)
    fix_store.wait()


def shards(source, potential, level_shift):
    dma = pltpu.SemaphoreType.DMA
    vmem = lambda *shape: pltpu.VMEM(shape, F32)
    scratch = dict(
        shift_ref=pltpu.SMEM((4,), F32),
        own=vmem(4, 144, 256), other=vmem(4, 144, 256), pot=vmem(4, 144, 256), pot_other=vmem(4, 128, 256), s_buf=vmem(4, 144, 256),
        rd=vmem(4, 144, 256), fd=vmem(4, 144, 256), sd=vmem(4, 128, 256), strip=vmem(2, 16, 256),
        nb=vmem(4, 64, 256), nstrip=vmem(16, 256), u_buf=vmem(4, 80, 256), fv=vmem(4, 80, 256), rv=vmem(4, 80, 256),
        sv=vmem(4, 64, 256), ustrip=vmem(16, 256), nu=vmem(4, 32, 256), nustrip=vmem(8, 256),
        fu=vmem(2, 4, 48, 256), ru=vmem(2, 4, 48, 256),
        pot_side=vmem(2, 128, 256), wv=vmem(4, 64, 256), wu=vmem(2, 4, 32, 256), base_v=vmem(4, 64, 256), base_u=vmem(2, 4, 32, 256),
        hd=vmem(2, 128, 256), hv=vmem(2, 64, 256), hu=vmem(2, 2, 32, 256),
        ub=vmem(4, 32, 256), ub_own=vmem(4, 32, 256), give=vmem(4, 32, 256), bk=vmem(4, 128, 256), gives=vmem(4, 64, 256),
        t_d=vmem(128, 256), x_d=vmem(128, 256), t_uv=vmem(128, 256), x_uv=vmem(128, 256),
        pot_all=vmem(4, 32, 128), d_sums=vmem(24, 128), d_x=vmem(3, 24, 128), d_total=vmem(24, 128),
        d_other=vmem(24, 128), uv_sums=vmem(8, 128), uv_x=vmem(3, 8, 128), uv_total=vmem(8, 128),
        tr=vmem(8, 8, 128), blocks=vmem(2, 256, 128), pick=vmem(3, 32, 64), pick_d=vmem(2, 32, 24),
        fix_all=vmem(32, 256), mine=vmem(4, 128, 256), yours=vmem(4, 128, 256),
        all_sent=vmem(2752, 256),
        h_sem=dma(()), l_sem=dma(()), p_sem=dma(()), q_sem=dma(()), f_sem=dma(()), sent=dma(()), r0=dma((4,)), r1=dma((9,)),
        r2=dma((5,)), rt=dma(()), ru_sem=dma(()), rxp=dma((2,)), rxd=dma((2,)), rxv=dma((2,)), rxu=dma((2,)), rp=dma(()), rdx=dma(()), rdp=dma(()), rc=dma(()),
        rg=dma(()), rb2=dma((6,)), rb1=dma((4,)), ro=dma(()), lo=dma(()),
    )
    raw, fix = pl.pallas_call(
        kernel,
        out_shape=(jax.ShapeDtypeStruct(source.shape, F32), jax.ShapeDtypeStruct((32, 256), F32)),
        in_specs=[
            pl.BlockSpec(memory_space=pltpu.HBM),
            pl.BlockSpec(memory_space=pltpu.HBM),
            pl.BlockSpec(memory_space=pltpu.HBM),
        ],
        out_specs=(pl.BlockSpec(memory_space=pl.ANY), pl.BlockSpec(memory_space=pl.ANY)),
        scratch_shapes=list(scratch.values()),
        compiler_params=pltpu.CompilerParams(
            collective_id=0, has_side_effects=True, vmem_limit_bytes=40 * 2**20
        ),
        name="space_time_apply",
    )(*(pltpu.with_memory_space_constraint(a, pltpu.HBM) for a in (level_shift, source, potential)))
    return (raw.reshape(4, 32, 8, 256) + fix[None, :, None, :]).reshape(source.shape)


def solution(mesh):
    in_specs = (P("tm", "plane", None, None), P("plane", None, None), P())
    out_specs = P("tm", "plane", None, None)
    return jax.shard_map(shards, mesh=mesh, in_specs=in_specs, out_specs=out_specs, check_vma=False)
```

```python
import math

import jax
import jax.numpy as jnp
from jax import lax
from jax.experimental import pallas as pl
from jax.experimental.pallas import tpu as pltpu
from jax.sharding import PartitionSpec as P

F32 = jnp.float32
MESH = pl.DeviceIdType.MESH
ROOT = 1.0 / math.sqrt(2.0)
OMEGA = 0.8
PLANES = (0, 3, 1, 2)
SLOT = {plane: slot for slot, plane in enumerate(PLANES)}


def dot(a, b):
    return jnp.dot(a, b, precision=lax.Precision.HIGHEST, preferred_element_type=F32)


def iota(shape, dim):
    return lax.broadcasted_iota(jnp.int32, shape, dim)


def ones_where(mask):
    return jnp.where(mask, 1.0, 0.0).astype(F32)


def beside_yz(ext):
    rows = ext.shape[0] - 16
    mid = ext[8 : 8 + rows]
    up = pltpu.roll(ext, 1, 0)[8 : 8 + rows]
    down = pltpu.roll(ext, rows + 15, 0)[8 : 8 + rows]
    col = iota(mid.shape, 1)
    left = jnp.where(col == 0, 0.0, pltpu.roll(mid, 1, 1))
    right = jnp.where(col == 255, 0.0, pltpu.roll(mid, 255, 1))
    return mid, (up + down) + (left + right)


def kernel(
    shift_hbm, source, potential, out, fix_out,
    shift_ref, own, other, pot, pot_other, s_buf, rd, fd, sd, strip, nb, raw, nstrip, u_buf, fv, rv, sv, ustrip, nu, nustrip, fu, ru,
    pot_side, wv, wu, base_v, base_u, hd, hv, hu, ub, ub_own, give, bk, gives, t_d, x_d, t_uv, x_uv, pot_all, d_sums, d_x, d_total, d_other, uv_sums, uv_x, uv_total,
    tr, blocks, pick, pick_d, fix_all, mine, yours,
    all_sent, h_sem, l_sem, p_sem, q_sem, f_sem, sent, r_raw, r0, r1, r2, rt, ru_sem, rxp, rxd, rxv, rxu, rp, rdx, rdp, rc, rg, rb2, rb1, ro, lo,
):
    t, x = lax.axis_index("tm"), lax.axis_index("plane")
    e = t % 8
    k, c = e % 2, e // 2
    b, p = c % 2, c // 2
    partner = t + 1 - 2 * k
    near = t + 2 - 4 * b
    far = t + 4 - 8 * p
    x_peers = [(x + m) % 4 for m in (1, 2, 3)]
    group = [t - e + (e + m) % 8 for m in range(1, 8)]

    barrier = pltpu.get_barrier_semaphore()
    for peer in group:
        pl.semaphore_signal(barrier, inc=1, device_id=(peer, x), device_id_type=MESH)
    for peer in x_peers:
        pl.semaphore_signal(barrier, inc=1, device_id=(t, peer), device_id_type=MESH)

    def rows(start, count):
        return pl.ds(pl.multiple_of(start, 8), count)

    def remote(src, dst, recv, where):
        copy = pltpu.make_async_remote_copy(
            src_ref=src, dst_ref=dst, send_sem=sent, recv_sem=recv, device_id=where, device_id_type=MESH
        )
        copy.start()
        return copy

    def absorb(ref, sem):
        pltpu.make_async_copy(ref, ref, sem).wait()

    def local(src, dst, sem):
        copy = pltpu.make_async_copy(src, dst, sem)
        copy.start()
        return copy

    for slot, plane in enumerate(PLANES):
        local(source.at[0, plane, rows(120 * k, 136), :], own.at[slot, rows(8 - 8 * k, 136), :], l_sem)
    shift_load = local(shift_hbm, shift_ref, h_sem)
    for slot, plane in enumerate(PLANES):
        local(potential.at[plane, rows(120 * k, 136), :], pot.at[slot, rows(8 - 8 * k, 136), :], p_sem)
    rest_load = local(potential.at[:, rows(128 - 128 * k, 128), :], pot_other, q_sem)
    for slot in range(4):
        for ref in (own, other, pot):
            ref[slot, rows(136 * k, 8), :] = jnp.zeros((8, 256), F32)

    pl.semaphore_wait(barrier, 10)

    first_rows = 64 - 64 * b + 32 - 32 * p
    remote(source.at[0, PLANES[0], rows(128 * k + first_rows, 32), :], raw.at[0], r_raw, (near, x))
    remote(source.at[0, PLANES[0], rows(128 - 128 * k + first_rows, 32), :], raw.at[1], r_raw, (near + 1 - 2 * k, x))
    for slot in (1, 0, 2, 3):
        remote(
            source.at[0, PLANES[slot], rows(120 - 120 * k, 136), :], other.at[slot, rows(8 * k, 136), :],
            r0.at[0 if slot == 1 else 1], (partner, x),
        )

    def to_side(src, halo, end, sem):
        @pl.when(x < 3 if end == 0 else x > 0)
        def _():
            remote(src, halo.at[end], sem.at[end], (t, x + 1 - 2 * end))

    def from_sides(halo, sem):
        for end in range(2):
            pl.when(x > 0 if end == 0 else x < 3)(lambda end=end: absorb(halo.at[end], sem.at[end]))

    for end in range(2):
        @pl.when(x == 3 * end)
        def _():
            hd[end] = jnp.zeros((128, 256), F32)
            hv[end] = jnp.zeros((64, 256), F32)
            hu[end] = jnp.zeros((2, 32, 256), F32)
            pot_side[end] = jnp.zeros((128, 256), F32)

    to_side(potential.at[0, rows(128 * k, 128), :], pot_side, 1, rxp)
    to_side(potential.at[3, rows(128 * k, 128), :], pot_side, 0, rxp)

    def to_near(index, slots, q, start=0, count=32):
        at = 32 * q + start
        firsts[index] = remote(
            s_buf.at[slots, rows(72 - 64 * b + at, count), :], nb.at[slots, rows(at, count), :],
            r1.at[min(index, 6) if index < 8 else 0], (near, x),
        )

    firsts = {}
    absorb(own.at[:, 0:136, :], l_sem)
    absorb(other.at[1, 0:136, :], r0.at[0])
    s_buf[1] = (own[1] + other[1]) * ROOT
    to_near(1, 1, 1 - p)
    absorb(other.at[0:3, 0:136, :], r0.at[1])
    for slot in (0, 2, 3):
        s_buf[slot] = (own[slot] + other[slot]) * ROOT
    for h in range(2):
        for i in range(4):
            for at, row in ((0, 7), (4, 40), (8, 39), (12, 72)):
                strip[h, at + i : at + i + 1, :] = s_buf[i, row + 64 * h : row + 64 * h + 1, :]
    strip_1 = remote(strip.at[1 - b], nstrip, rt, (near, x))
    to_near(2, 2, 1 - p)
    to_near(3, 3, 1 - p)

    sign = (1 - 2 * k).astype(F32)
    near_sign = (1 - 2 * b).astype(F32)
    far_sign = (1 - 2 * p).astype(F32)
    scale = ROOT * sign
    edge_low, edge_high = ones_where(x == 0), ones_where(x == 3)
    shift_load.wait()
    shift_0 = shift_ref[0]
    absorb(pot.at[:, 0:136, :], p_sem)
    for slot in range(4):
        rd[slot] = OMEGA / (6.0 + pot[slot] + shift_0)
        fd[slot] = (own[slot] - other[slot]) * scale * rd[slot]


    to_side(fd.at[0, 8:136, :], hd, 1, rxd)
    to_side(fd.at[1, 8:136, :], hd, 0, rxd)

    for slot in range(4):
        rv[slot] = OMEGA / (6.0 + pot[slot, rows(64 * b, 80), :] + shift_ref[1])
        here = 6.0 + pot[slot, rows(64 * b + 32 * p, 48), :]
        ru[0, slot] = OMEGA / (here + shift_ref[3])
        ru[1, slot] = OMEGA / (here + shift_ref[2])

    z_at, z_block = iota((256, 128), 0), iota((256, 128), 1)
    lane_block = ones_where(z_at // 8 == z_block % 32)
    row, col = iota((32, 128), 0), iota((32, 128), 1)
    rest_load.wait()
    pot_sum = (pot[0, 8:136, :] + pot[1, 8:136, :]) + (pot[2, 8:136, :] + pot[3, 8:136, :])
    pot_rest = (pot_other[0] + pot_other[1]) + (pot_other[2] + pot_other[3])
    pot_all[0] = dot(ones_where(col // 8 + 16 * k == row), dot(pot_sum, lane_block)) + dot(
        ones_where(col // 8 + 16 - 16 * k == row), dot(pot_rest, lane_block)
    )
    for m, peer in enumerate(x_peers):
        remote(pot_all.at[0], pot_all.at[m + 1], rp, (t, peer))
    block = ones_where(z_at // 8 == z_block)
    around = ones_where((z_at + 7) // 8 == z_block + 1) + ones_where((z_at + 1) // 8 == z_block)
    blocks[0] = block
    blocks[1] = jnp.where(z_block < 32, 2.0 * block + around, 0.0)

    row, col = iota((32, 64), 0), iota((32, 64), 1)
    sender, r = col // 8, col % 8
    sender_c = sender // 2
    sender_b, sender_p = sender_c % 2, sender_c // 2
    sender_at = 16 * (sender % 2) + 8 * sender_b - 1 + r
    pick[0] = ones_where((r < 6) & (sender_at + 4 * sender_p == row))
    pick[1] = ones_where((sender_p == p) & (sender_at == row))
    pick[2] = ones_where((sender_p == p) & (r < 2) & (sender_at + 8 == row))
    row, col = iota((32, 24), 0), iota((32, 24), 1)
    pick_d[0] = ones_where((col < 18) & (16 * k - 1 + col == row))
    pick_d[1] = ones_where((col < 18) & (16 * (1 - k) - 1 + col == row))

    def level_1(slot, q, start=0, count=32):
        inside = 32 * q + start
        here = s_buf[slot, rows(8 + 64 * b + inside, count), :]
        there = nb[slot, rows(inside, count), :]
        at = rows(8 + inside, count)
        u_buf[slot, at, :] = (here + there) * ROOT
        detail = (here - there) * (ROOT * near_sign)
        fv[slot, at, :] = detail * rv[slot, at, :]
        at = rows(inside, count)
        x_uv[at, :] = detail if slot == 0 else x_uv[at, :] + detail

    seconds = {}

    def to_far(index, slots, start=0, count=32):
        seconds[index] = remote(
            u_buf.at[slots, rows(40 - 32 * p + start, count), :], nu.at[slots, start : start + count, :],
            r2.at[index - index // 3], (far, x),
        )

    def passed_on(slot):
        if slot == 0:
            absorb(raw, r_raw)
            nb[0, rows(32 - 32 * p, 32), :] = (raw[0] + raw[1]) * ROOT
        else:
            firsts[slot].wait_recv()
        level_1(slot, 1 - p)
        to_far(slot, slot, 0, 32 if slot < 2 else 24)

    def level_2(slot, start=0, count=32):
        here = u_buf[slot, rows(8 + 32 * p + start, count), :]
        there = nu[slot, start : start + count, :]
        low, high = (here + there) * ROOT, (here - there) * (ROOT * far_sign)
        at = slice(8 + start, 8 + start + count)
        fu[0, slot, at, :] = low * ru[0, slot, at, :]
        fu[1, slot, at, :] = high * ru[1, slot, at, :]
        for first, field in ((64 + start, low), (96 + start, high)):
            at = slice(first, first + count)
            x_uv[at, :] = field if slot == 0 else x_uv[at, :] + field

    inner_slots = slice(2, 4)
    for slot in range(4):
        passed_on(slot)
        if slot < 2:
            to_near(4 + slot, slot, p)
        if slot == 0:
            strip_1.wait_recv()
            ustrip[...] = (strip[b] + nstrip[...]) * ROOT
            strip_2 = remote(ustrip.at[rows(8 - 8 * p, 8), :], nustrip, ru_sem, (far, x))
    to_near(6, 2, p, 0, 24)
    to_near(7, 3, p, 0, 24)
    to_far(4, inner_slots, 24, 8)
    to_near(8, inner_slots, p, 24, 8)
    details = (strip[b] - nstrip[...]) * (ROOT * near_sign)
    for slot in range(4):
        fv[slot, 7:8, :] = details[slot : slot + 1] * rv[slot, 7:8, :]
        fv[slot, 72:73, :] = details[12 + slot : 13 + slot] * rv[slot, 72:73, :]
        if slot > 1:
            fv[slot, 39:40, :] = details[8 + slot : 9 + slot] * rv[slot, 39:40, :]
    from_sides(pot_side, rxp)
    kept = [ones_where(x > 0), ones_where(x < 3)]

    def beside_weights(weight, start, count, shift, out):
        side = []
        for end in range(2):
            field = 6.0 + pot_side[end, rows(start, count), :] + shift
            side.append((OMEGA * kept[end]) / field)
        inner = [weight[SLOT[plane], 8 : 8 + count, :] for plane in range(4)]
        out[SLOT[0]] = side[0] + inner[1]
        out[SLOT[1]] = inner[0] + inner[2]
        out[SLOT[2]] = inner[1] + inner[3]
        out[SLOT[3]] = inner[2] + side[1]

    beside_weights(rv, 64 * b, 64, shift_ref[1], wv)
    for j, level in ((0, 3), (1, 2)):
        beside_weights(ru.at[j], 64 * b + 32 * p, 32, shift_ref[level], wu.at[j])

    for slot, end in ((0, 1), (1, 0)):
        firsts[4 + slot].wait_recv()
        level_1(slot, p)
        seconds[slot].wait_recv()
        level_2(slot)
        to_side(fu.at[:, slot, 8:40, :], hu, end, rxu)
        to_side(fv.at[slot, 8:72, :], hv, end, rxv)

    def second_pass(f, weight, low_rim, high_rim, at, count, order, done):
        center = rows(at + 8, count)
        total, outer = None, None
        for plane in order:
            slot = SLOT[plane]
            mid, beside = beside_yz(f[slot, rows(at, count + 16), :])
            low = f[SLOT[plane - 1], center, :] if plane > 0 else low_rim()
            high = f[SLOT[plane + 1], center, :] if plane < 3 else high_rim()
            second = 1.2 * mid + weight[slot, center, :] * (beside + (low + high))
            done(slot, second)
            q = second - OMEGA * mid
            total = q if total is None else total + q
            if plane in (0, 3):
                rim = q * (edge_low if plane == 0 else edge_high)
                outer = rim if outer is None else outer + rim
        return total, outer

    from_sides(hd, rxd)

    def odd_rows(step, _):
        at = 32 * step
        here = rows(at, 32)

        def done(slot, second):
            sd[slot, here, :] = second

        summed, outer = second_pass(
            fd, rd, lambda: hd[0, here, :], lambda: hd[1, here, :], at, 32, range(4), done
        )
        center = rows(at + 8, 32)
        waves = (own[0, center, :] - other[0, center, :]) + (own[1, center, :] - other[1, center, :])
        waves = waves + (own[2, center, :] - other[2, center, :]) + (own[3, center, :] - other[3, center, :])
        t_d[here, :] = summed
        x_d[here, :] = (0.04 * scale) * waves - outer
        return 0

    lax.fori_loop(0, 4, odd_rows, 0)
    y_at, y_row = iota((24, 128), 1), iota((24, 128), 0)
    inner = ones_where(y_at // 8 + 1 == y_row)
    beside = ones_where((y_at + 7) // 8 == y_row) + ones_where((y_at + 1) // 8 + 1 == y_row)
    sums = dot(inner, dot(x_d[...], blocks[0]) + dot(t_d[...], blocks[1])) + dot(beside, dot(t_d[...], blocks[0]))
    d_sums[...] = pltpu.roll(sums, 96, 1)
    for m, peer in enumerate(x_peers):
        remote(d_sums, d_x.at[m], rdx, (t, peer))

    strip_2.wait_recv()
    here = ustrip[rows(8 * p, 8), :]
    low, high = (here + nustrip[...]) * ROOT, (here - nustrip[...]) * (ROOT * far_sign)
    for slot in range(4):
        for j, rim in enumerate((low, high)):
            fu[j, slot, 7:8, :] = rim[slot : slot + 1] * ru[j, slot, 7:8, :]
            fu[j, slot, 40:41, :] = rim[4 + slot : 5 + slot] * ru[j, slot, 40:41, :]
    absorb(nu.at[2:4, 0:24, :], r2.at[2])
    absorb(nb.at[2:4, 0:24, :], r1.at[6])
    for slot in (2, 3):
        level_1(slot, p, 0, 24)
        level_2(slot, 0, 24)

    def own_planes(f, weight, sides, base, at, count, planes):
        here, center = rows(at, count), rows(at + 8, count)
        total, outer = None, None
        for plane in planes:
            slot = SLOT[plane]
            mid, beside = beside_yz(f[slot, rows(at, count + 16), :])
            within = weight[slot, center, :] * beside
            base[slot, here, :] = 1.2 * mid + within
            within = 0.4 * mid + within
            q = within + mid * sides[slot, here, :]
            total = q if total is None else total + q
            if plane in (0, 3):
                next_in = f[SLOT[1 if plane == 0 else 2], center, :]
                rim = (within + weight[slot, center, :] * next_in) * (edge_low if plane == 0 else edge_high)
                outer = rim if outer is None else outer + rim
        return total, outer

    def with_sides(f, weight, base, halo, at, count, plane):
        here, center = rows(at, count), rows(at + 8, count)
        low = f[SLOT[plane - 1], center, :] if plane > 0 else halo(0)
        high = f[SLOT[plane + 1], center, :] if plane < 3 else halo(1)
        return base[SLOT[plane], here, :] + weight[SLOT[plane], center, :] * (low + high)

    def near_planes(planes, start, count):
        def body(step, _):
            here = rows(32 * step + start, count)
            summed, outer = own_planes(fv, rv, wv, base_v, 32 * step + start, count, planes)
            if outer is None:
                t_uv[here, :] = summed
            else:
                t_uv[here, :] += summed
                x_uv[here, :] = 0.04 * x_uv[here, :] - outer
            return 0

        lax.fori_loop(0, 2, body, 0)

    def near_rows(planes, start, count):
        def body(step, _):
            here = rows(32 * step + start, count)
            for plane in planes:
                sv[SLOT[plane], here, :] = with_sides(
                    fv, rv, base_v, lambda end: hv[end, here, :], 32 * step + start, count, plane
                )
            return 0

        lax.fori_loop(0, 2, body, 0)

    def far_planes(planes, start, count):
        for j in range(2):
            at = slice(64 + 32 * j + start, 64 + 32 * j + start + count)
            summed, outer = own_planes(fu.at[j], ru.at[j], wu.at[j], base_u.at[j], start, count, planes)
            if outer is None:
                t_uv[at, :] = summed
            else:
                t_uv[at, :] += summed
                x_uv[at, :] = 0.04 * x_uv[at, :] - outer

    def far_rows(plane, start=0, count=32):
        here = slice(start, start + count)
        made = [
            with_sides(fu.at[j], ru.at[j], base_u.at[j], lambda end, j=j: hu[end, j, here, :], start, count, plane)
            for j in range(2)
        ]
        slot = SLOT[plane]
        low, high = made[0] * ROOT, made[1] * (ROOT * far_sign)
        give[slot, here, :] = low - high
        ub_own[slot, here, :] = low + high
        remote(give.at[slot, here, :], ub.at[slot, here, :], rb2.at[slot], (far, x))

    def join(slot, q, ref, start=0, count=32):
        at = 32 * q + start
        low = ref[slot, start : start + count, :] * ROOT
        high = sv[slot, rows(at, count), :] * (ROOT * near_sign)
        gives[slot, rows(at, count), :] = low - high
        bk[slot, rows(64 * b + at, count), :] = low + high
        remote(
            gives.at[slot, rows(at, count), :], bk.at[slot, rows(64 * b + at, count), :], rb1.at[4 if slot == 1 and ref is ub else slot], (near, x)
        )

    def rest(slot):
        absorb(ub.at[slot], rb2.at[slot])
        join(slot, 1 - p, ub)

    def inner_rows(start):
        far_planes((1, 2), start, 16)
        far_rows(1, start, 16)
        far_rows(2, start, 16)
        near_planes((1, 2), start, 16)
        near_rows((1, 2), start, 16)
        join(2, p, ub_own, start, 16)
        join(3, p, ub_own, start, 16)

    inner_rows(0)
    seconds[4].wait_recv()
    firsts[8].wait_recv()
    for slot in (2, 3):
        level_1(slot, p, 24, 8)
        level_2(slot, 24, 8)
    inner_rows(16)
    far_planes((0, 3), 0, 32)
    near_planes((0, 3), 0, 32)

    y_at, y_row = iota((32, 128), 1), iota((32, 128), 0)
    start = jnp.where(y_at < 64, 0, 16 + 8 * ((y_at - 64) // 32))
    y_in = jnp.where(y_at < 64, y_at, y_at % 32)
    inner = ones_where(start + y_in // 8 + 1 == y_row)
    beside = ones_where(start + (y_in + 7) // 8 == y_row) + ones_where(start + (y_in + 1) // 8 + 1 == y_row)
    sums = dot(inner, dot(x_uv[...], blocks[0]) + dot(t_uv[...], blocks[1])) + dot(beside, dot(t_uv[...], blocks[0]))
    uv_sums[...] = (sums[16:24] + pltpu.roll(sums[24:32], 32, 1)) + (
        pltpu.roll(sums[0:8], 64, 1) + pltpu.roll(sums[8:16], 96, 1)
    )
    for m, peer in enumerate(x_peers):
        remote(uv_sums, uv_x.at[m], rc, (t, peer))
    from_sides(hu, rxu)
    far_rows(0)
    far_rows(3)
    from_sides(hv, rxv)
    near_rows((0, 3), 0, 32)
    join(0, p, ub_own)
    join(1, p, ub_own)
    rest(2)
    absorb(uv_x, rc)
    uv_total[...] = (uv_sums[...] + uv_x[0]) + (uv_x[1] + uv_x[2])
    for peer in group:
        remote(uv_total, tr.at[e], rg, (peer, x))
    tr[e] = uv_total[...]
    rest(3)
    absorb(d_x, rdx)
    absorb(pot_all.at[1:4], rp)
    d_total[...] = (d_sums[...] + d_x[0]) + (d_x[1] + d_x[2])
    d_swap = remote(d_total, d_other, rdp, (partner, x))

    def finish(slot, start, count=64):
        here = rows(start, count)
        even, odd = bk[slot, here, :], sd[slot, here, :] * sign
        yours[slot, here, :] = (even - odd) * ROOT
        there = out.at[0, PLANES[slot], rows(128 * k + start, count), :]
        remote(yours.at[slot, here, :], there, ro, (partner, x))
        mine[slot, here, :] = (even + odd) * ROOT
        local(mine.at[slot, here, :], there, lo)

    rest(0)
    rest(1)
    for slot in (2, 3, 0, 1):
        finish(slot, 64 * b)

    def finish_far(slot):
        absorb(gives.at[slot], rb1.at[slot])
        finish(slot, 64 - 64 * b)

    for slot in (2, 3, 0):
        finish_far(slot)
    for q, index in ((p, 1), (1 - p, 4)):
        absorb(gives.at[1, 0:32, :], rb1.at[index])
        finish(1, 64 - 64 * b + 32 * q, 32)
    absorb(tr.at[0:7], rg)
    d_swap.wait_recv()

    lane = iota((32, 128), 1)
    coef = lane // 32
    gathered = tr[...].reshape(64, 128)
    rem_v = dot(pick[1], gathered) + pltpu.roll(dot(pick[2], gathered), 96, 1)
    rem_d = dot(pick_d[0], d_total[...]) + dot(pick_d[1], d_other[...])
    rem = jnp.where(coef < 2, dot(pick[0], gathered), jnp.where(coef == 2, rem_v, rem_d))
    shift = jnp.where(
        coef == 0, shift_ref[3], jnp.where(coef == 1, shift_ref[2], jnp.where(coef == 2, shift_ref[1], shift_0))
    )
    coarse_pot = (pot_all[0] + pot_all[1]) + (pot_all[2] + pot_all[3])
    diag = coarse_pot + shift * 1024.0 + 640.0
    one = rem / diag
    row = iota((32, 128), 0)
    up = jnp.where(row == 0, 0.0, pltpu.roll(one, 1, 0))
    down = jnp.where(row == 31, 0.0, pltpu.roll(one, 31, 0))
    left = jnp.where(lane % 32 == 0, 0.0, pltpu.roll(one, 1, 1))
    right = jnp.where(lane % 32 == 31, 0.0, pltpu.roll(one, 127, 1))
    applied = diag * one - 128.0 * ((up + down) + (left + right))
    fix = one + (rem - applied) / diag
    weight = jnp.where(
        coef == 0, 0.5 * ROOT, jnp.where(coef == 1, 0.5 * ROOT * far_sign, jnp.where(coef == 2, 0.5 * near_sign, scale))
    )
    widen = ones_where(iota((128, 256), 0) % 32 == iota((128, 256), 1) // 8)
    fix_all[...] = dot(fix * weight, widen)
    fix_store = local(fix_all, fix_out, f_sem)

    outer = (x == 0) | (x == 3)
    pl.when(outer)(lambda: absorb(all_sent.at[0:2400, :], sent))
    pl.when(jnp.logical_not(outer))(lambda: absorb(all_sent, sent))
    absorb(yours, ro)
    absorb(mine, lo)
    fix_store.wait()


def shards(source, potential, level_shift):
    dma = pltpu.SemaphoreType.DMA
    vmem = lambda *shape: pltpu.VMEM(shape, F32)
    scratch = dict(
        shift_ref=pltpu.SMEM((4,), F32),
        own=vmem(4, 144, 256), other=vmem(4, 144, 256), pot=vmem(4, 144, 256), pot_other=vmem(4, 128, 256), s_buf=vmem(4, 144, 256),
        rd=vmem(4, 144, 256), fd=vmem(4, 144, 256), sd=vmem(4, 128, 256), strip=vmem(2, 16, 256),
        nb=vmem(4, 64, 256), raw=vmem(2, 32, 256), nstrip=vmem(16, 256), u_buf=vmem(4, 80, 256), fv=vmem(4, 80, 256), rv=vmem(4, 80, 256),
        sv=vmem(4, 64, 256), ustrip=vmem(16, 256), nu=vmem(4, 32, 256), nustrip=vmem(8, 256),
        fu=vmem(2, 4, 48, 256), ru=vmem(2, 4, 48, 256),
        pot_side=vmem(2, 128, 256), wv=vmem(4, 64, 256), wu=vmem(2, 4, 32, 256), base_v=vmem(4, 64, 256), base_u=vmem(2, 4, 32, 256),
        hd=vmem(2, 128, 256), hv=vmem(2, 64, 256), hu=vmem(2, 2, 32, 256),
        ub=vmem(4, 32, 256), ub_own=vmem(4, 32, 256), give=vmem(4, 32, 256), bk=vmem(4, 128, 256), gives=vmem(4, 64, 256),
        t_d=vmem(128, 256), x_d=vmem(128, 256), t_uv=vmem(128, 256), x_uv=vmem(128, 256),
        pot_all=vmem(4, 32, 128), d_sums=vmem(24, 128), d_x=vmem(3, 24, 128), d_total=vmem(24, 128),
        d_other=vmem(24, 128), uv_sums=vmem(8, 128), uv_x=vmem(3, 8, 128), uv_total=vmem(8, 128),
        tr=vmem(8, 8, 128), blocks=vmem(2, 256, 128), pick=vmem(3, 32, 64), pick_d=vmem(2, 32, 24),
        fix_all=vmem(32, 256), mine=vmem(4, 128, 256), yours=vmem(4, 128, 256),
        all_sent=vmem(2784, 256),
        h_sem=dma(()), l_sem=dma(()), p_sem=dma(()), q_sem=dma(()), f_sem=dma(()), sent=dma(()), r_raw=dma(()), r0=dma((2,)), r1=dma((7,)),
        r2=dma((4,)), rt=dma(()), ru_sem=dma(()), rxp=dma((2,)), rxd=dma((2,)), rxv=dma((2,)), rxu=dma((2,)), rp=dma(()), rdx=dma(()), rdp=dma(()), rc=dma(()),
        rg=dma(()), rb2=dma((4,)), rb1=dma((5,)), ro=dma(()), lo=dma(()),
    )
    raw, fix = pl.pallas_call(
        kernel,
        out_shape=(jax.ShapeDtypeStruct(source.shape, F32), jax.ShapeDtypeStruct((32, 256), F32)),
        in_specs=[
            pl.BlockSpec(memory_space=pltpu.HBM),
            pl.BlockSpec(memory_space=pltpu.HBM),
            pl.BlockSpec(memory_space=pltpu.HBM),
        ],
        out_specs=(pl.BlockSpec(memory_space=pl.ANY), pl.BlockSpec(memory_space=pl.ANY)),
        scratch_shapes=list(scratch.values()),
        compiler_params=pltpu.CompilerParams(
            collective_id=0, has_side_effects=True, vmem_limit_bytes=40 * 2**20
        ),
        name="space_time_apply",
    )(*(pltpu.with_memory_space_constraint(a, pltpu.HBM) for a in (level_shift, source, potential)))
    return (raw.reshape(4, 32, 8, 256) + fix[None, :, None, :]).reshape(source.shape)


def solution(mesh):
    in_specs = (P("tm", "plane", None, None), P("plane", None, None), P())
    out_specs = P("tm", "plane", None, None)
    return jax.shard_map(shards, mesh=mesh, in_specs=in_specs, out_specs=out_specs, check_vma=False)
```

```python
import math

import jax
import jax.numpy as jnp
from jax import lax
from jax.experimental import pallas as pl
from jax.experimental.pallas import tpu as pltpu
from jax.sharding import PartitionSpec as P

F32 = jnp.float32
MESH = pl.DeviceIdType.MESH
ROOT = 1.0 / math.sqrt(2.0)
OMEGA = 0.8
PLANES = (0, 3, 1, 2)
SLOT = {plane: slot for slot, plane in enumerate(PLANES)}


def dot(a, b):
    return jnp.dot(a, b, precision=lax.Precision.HIGHEST, preferred_element_type=F32)


def iota(shape, dim):
    return lax.broadcasted_iota(jnp.int32, shape, dim)


def ones_where(mask):
    return jnp.where(mask, 1.0, 0.0).astype(F32)


def beside_yz(ext):
    rows = ext.shape[0] - 16
    mid = ext[8 : 8 + rows]
    up = pltpu.roll(ext, 1, 0)[8 : 8 + rows]
    down = pltpu.roll(ext, rows + 15, 0)[8 : 8 + rows]
    col = iota(mid.shape, 1)
    left = jnp.where(col == 0, 0.0, pltpu.roll(mid, 1, 1))
    right = jnp.where(col == 255, 0.0, pltpu.roll(mid, 255, 1))
    return mid, (up + down) + (left + right)


def kernel(
    shift_hbm, source, potential, out, fix_out,
    shift_ref, own, other, pot, pot_other, s_buf, rd, fd, sd, strip, nb, raw, nstrip, u_buf, fv, rv, sv, ustrip, nu, nustrip, fu, ru,
    pot_side, wv, wu, base_v, base_u, hd, hv, hu, ub, ub_own, give, bk, gives, t_d, x_d, t_uv, x_uv, pot_all, d_sums, d_x, d_total, d_other, uv_sums, uv_x, uv_total,
    tr, blocks, pick, pick_d, fix_all, mine, yours,
    all_sent, h_sem, l_sem, p_sem, q_sem, f_sem, sent, r_raw, r0, r1, r2, rt, ru_sem, rxp, rxd, rxv, rxu, rp, rdx, rdp, rc, rg, rb2, rb1, ro, lo,
):
    t, x = lax.axis_index("tm"), lax.axis_index("plane")
    e = t % 8
    k, c = e % 2, e // 2
    b, p = c % 2, c // 2
    partner = t + 1 - 2 * k
    near = t + 2 - 4 * b
    far = t + 4 - 8 * p
    x_peers = [(x + m) % 4 for m in (1, 2, 3)]
    group = [t - e + (e + m) % 8 for m in range(1, 8)]

    barrier = pltpu.get_barrier_semaphore()
    for peer in (far, near, near + 1 - 2 * k, partner):
        pl.semaphore_signal(barrier, inc=1, device_id=(peer, x), device_id_type=MESH)
    for peer in x_peers:
        pl.semaphore_signal(barrier, inc=1, device_id=(t, peer), device_id_type=MESH)

    def rows(start, count):
        return pl.ds(pl.multiple_of(start, 8), count)

    def remote(src, dst, recv, where):
        copy = pltpu.make_async_remote_copy(
            src_ref=src, dst_ref=dst, send_sem=sent, recv_sem=recv, device_id=where, device_id_type=MESH
        )
        copy.start()
        return copy

    def absorb(ref, sem):
        pltpu.make_async_copy(ref, ref, sem).wait()

    def local(src, dst, sem):
        copy = pltpu.make_async_copy(src, dst, sem)
        copy.start()
        return copy

    for slot, plane in enumerate(PLANES):
        local(source.at[0, plane, rows(120 * k, 136), :], own.at[slot, rows(8 - 8 * k, 136), :], l_sem)
    shift_load = local(shift_hbm, shift_ref, h_sem)
    for slot, plane in enumerate(PLANES):
        local(potential.at[plane, rows(120 * k, 136), :], pot.at[slot, rows(8 - 8 * k, 136), :], p_sem)
    rest_load = local(potential.at[:, rows(128 - 128 * k, 128), :], pot_other, q_sem)
    for slot in range(4):
        for ref in (own, other, pot):
            ref[slot, rows(136 * k, 8), :] = jnp.zeros((8, 256), F32)

    pl.semaphore_wait(barrier, 7)

    first_rows = 64 - 64 * b + 32 - 32 * p
    remote(source.at[0, PLANES[0], rows(128 * k + first_rows, 32), :], raw.at[0], r_raw, (near, x))
    remote(source.at[0, PLANES[0], rows(128 - 128 * k + first_rows, 32), :], raw.at[1], r_raw, (near + 1 - 2 * k, x))
    for slot in (1, 0, 2, 3):
        remote(
            source.at[0, PLANES[slot], rows(120 - 120 * k, 136), :], other.at[slot, rows(8 * k, 136), :],
            r0.at[0 if slot == 1 else 1], (partner, x),
        )

    def to_side(src, halo, end, sem):
        @pl.when(x < 3 if end == 0 else x > 0)
        def _():
            remote(src, halo.at[end], sem.at[end], (t, x + 1 - 2 * end))

    def from_sides(halo, sem):
        for end in range(2):
            pl.when(x > 0 if end == 0 else x < 3)(lambda end=end: absorb(halo.at[end], sem.at[end]))

    for end in range(2):
        @pl.when(x == 3 * end)
        def _():
            hd[end] = jnp.zeros((128, 256), F32)
            hv[end] = jnp.zeros((64, 256), F32)
            hu[end] = jnp.zeros((2, 32, 256), F32)
            pot_side[end] = jnp.zeros((128, 256), F32)

    to_side(potential.at[0, rows(128 * k, 128), :], pot_side, 1, rxp)
    to_side(potential.at[3, rows(128 * k, 128), :], pot_side, 0, rxp)

    def to_near(index, slots, q, start=0, count=32):
        at = 32 * q + start
        firsts[index] = remote(
            s_buf.at[slots, rows(72 - 64 * b + at, count), :], nb.at[slots, rows(at, count), :],
            r1.at[min(index, 6) if index < 8 else 0], (near, x),
        )

    firsts = {}
    absorb(own.at[:, 0:136, :], l_sem)
    absorb(other.at[1, 0:136, :], r0.at[0])
    s_buf[1] = (own[1] + other[1]) * ROOT
    to_near(1, 1, 1 - p)
    absorb(other.at[0:3, 0:136, :], r0.at[1])
    for slot in (0, 2, 3):
        s_buf[slot] = (own[slot] + other[slot]) * ROOT
    for h in range(2):
        for i in range(4):
            for at, row in ((0, 7), (4, 40), (8, 39), (12, 72)):
                strip[h, at + i : at + i + 1, :] = s_buf[i, row + 64 * h : row + 64 * h + 1, :]
    strip_1 = remote(strip.at[1 - b], nstrip, rt, (near, x))
    to_near(2, 2, 1 - p)
    to_near(3, 3, 1 - p)

    sign = (1 - 2 * k).astype(F32)
    near_sign = (1 - 2 * b).astype(F32)
    far_sign = (1 - 2 * p).astype(F32)
    scale = ROOT * sign
    edge_low, edge_high = ones_where(x == 0), ones_where(x == 3)
    shift_load.wait()
    shift_0 = shift_ref[0]
    absorb(pot.at[:, 0:136, :], p_sem)
    for slot in range(4):
        rd[slot] = OMEGA / (6.0 + pot[slot] + shift_0)
        fd[slot] = (own[slot] - other[slot]) * scale * rd[slot]


    to_side(fd.at[0, 8:136, :], hd, 1, rxd)
    to_side(fd.at[1, 8:136, :], hd, 0, rxd)

    for slot in range(4):
        rv[slot] = OMEGA / (6.0 + pot[slot, rows(64 * b, 80), :] + shift_ref[1])
        here = 6.0 + pot[slot, rows(64 * b + 32 * p, 48), :]
        ru[0, slot] = OMEGA / (here + shift_ref[3])
        ru[1, slot] = OMEGA / (here + shift_ref[2])

    z_at, z_block = iota((256, 128), 0), iota((256, 128), 1)
    lane_block = ones_where(z_at // 8 == z_block % 32)
    row, col = iota((32, 128), 0), iota((32, 128), 1)
    rest_load.wait()
    pot_sum = (pot[0, 8:136, :] + pot[1, 8:136, :]) + (pot[2, 8:136, :] + pot[3, 8:136, :])
    pot_rest = (pot_other[0] + pot_other[1]) + (pot_other[2] + pot_other[3])
    pot_all[0] = dot(ones_where(col // 8 + 16 * k == row), dot(pot_sum, lane_block)) + dot(
        ones_where(col // 8 + 16 - 16 * k == row), dot(pot_rest, lane_block)
    )
    for m, peer in enumerate(x_peers):
        remote(pot_all.at[0], pot_all.at[m + 1], rp, (t, peer))
    block = ones_where(z_at // 8 == z_block)
    around = ones_where((z_at + 7) // 8 == z_block + 1) + ones_where((z_at + 1) // 8 == z_block)
    blocks[0] = block
    blocks[1] = jnp.where(z_block < 32, 2.0 * block + around, 0.0)

    row, col = iota((32, 64), 0), iota((32, 64), 1)
    sender, r = col // 8, col % 8
    sender_c = sender // 2
    sender_b, sender_p = sender_c % 2, sender_c // 2
    sender_at = 16 * (sender % 2) + 8 * sender_b - 1 + r
    pick[0] = ones_where((r < 6) & (sender_at + 4 * sender_p == row))
    pick[1] = ones_where((sender_p == p) & (sender_at == row))
    pick[2] = ones_where((sender_p == p) & (r < 2) & (sender_at + 8 == row))
    row, col = iota((32, 24), 0), iota((32, 24), 1)
    pick_d[0] = ones_where((col < 18) & (16 * k - 1 + col == row))
    pick_d[1] = ones_where((col < 18) & (16 * (1 - k) - 1 + col == row))

    def level_1(slot, q, start=0, count=32):
        inside = 32 * q + start
        here = s_buf[slot, rows(8 + 64 * b + inside, count), :]
        there = nb[slot, rows(inside, count), :]
        at = rows(8 + inside, count)
        u_buf[slot, at, :] = (here + there) * ROOT
        detail = (here - there) * (ROOT * near_sign)
        fv[slot, at, :] = detail * rv[slot, at, :]
        at = rows(inside, count)
        x_uv[at, :] = detail if slot == 0 else x_uv[at, :] + detail

    seconds = {}

    def to_far(index, slots, start=0, count=32):
        seconds[index] = remote(
            u_buf.at[slots, rows(40 - 32 * p + start, count), :], nu.at[slots, start : start + count, :],
            r2.at[index - index // 3], (far, x),
        )

    def passed_on(slot):
        if slot == 0:
            absorb(raw, r_raw)
            nb[0, rows(32 - 32 * p, 32), :] = (raw[0] + raw[1]) * ROOT
        else:
            firsts[slot].wait_recv()
        level_1(slot, 1 - p)
        to_far(slot, slot, 0, 32 if slot < 2 else 24)

    def level_2(slot, start=0, count=32):
        here = u_buf[slot, rows(8 + 32 * p + start, count), :]
        there = nu[slot, start : start + count, :]
        low, high = (here + there) * ROOT, (here - there) * (ROOT * far_sign)
        at = slice(8 + start, 8 + start + count)
        fu[0, slot, at, :] = low * ru[0, slot, at, :]
        fu[1, slot, at, :] = high * ru[1, slot, at, :]
        for first, field in ((64 + start, low), (96 + start, high)):
            at = slice(first, first + count)
            x_uv[at, :] = field if slot == 0 else x_uv[at, :] + field

    inner_slots = slice(2, 4)
    for slot in range(4):
        passed_on(slot)
        if slot < 2:
            to_near(4 + slot, slot, p)
        if slot == 0:
            strip_1.wait_recv()
            ustrip[...] = (strip[b] + nstrip[...]) * ROOT
            strip_2 = remote(ustrip.at[rows(8 - 8 * p, 8), :], nustrip, ru_sem, (far, x))
    to_near(6, 2, p, 0, 24)
    to_near(7, 3, p, 0, 24)
    to_far(4, inner_slots, 24, 8)
    to_near(8, inner_slots, p, 24, 8)
    details = (strip[b] - nstrip[...]) * (ROOT * near_sign)
    for slot in range(4):
        fv[slot, 7:8, :] = details[slot : slot + 1] * rv[slot, 7:8, :]
        fv[slot, 72:73, :] = details[12 + slot : 13 + slot] * rv[slot, 72:73, :]
        if slot > 1:
            fv[slot, 39:40, :] = details[8 + slot : 9 + slot] * rv[slot, 39:40, :]
    from_sides(pot_side, rxp)
    kept = [ones_where(x > 0), ones_where(x < 3)]

    def beside_weights(weight, start, count, shift, out):
        side = []
        for end in range(2):
            field = 6.0 + pot_side[end, rows(start, count), :] + shift
            side.append((OMEGA * kept[end]) / field)
        inner = [weight[SLOT[plane], 8 : 8 + count, :] for plane in range(4)]
        out[SLOT[0]] = side[0] + inner[1]
        out[SLOT[1]] = inner[0] + inner[2]
        out[SLOT[2]] = inner[1] + inner[3]
        out[SLOT[3]] = inner[2] + side[1]

    beside_weights(rv, 64 * b, 64, shift_ref[1], wv)
    for j, level in ((0, 3), (1, 2)):
        beside_weights(ru.at[j], 64 * b + 32 * p, 32, shift_ref[level], wu.at[j])

    for slot, end in ((0, 1), (1, 0)):
        firsts[4 + slot].wait_recv()
        level_1(slot, p)
        seconds[slot].wait_recv()
        level_2(slot)
        to_side(fu.at[:, slot, 8:40, :], hu, end, rxu)
        to_side(fv.at[slot, 8:72, :], hv, end, rxv)

    def second_pass(f, weight, low_rim, high_rim, at, count, order, done):
        center = rows(at + 8, count)
        total, outer = None, None
        for plane in order:
            slot = SLOT[plane]
            mid, beside = beside_yz(f[slot, rows(at, count + 16), :])
            low = f[SLOT[plane - 1], center, :] if plane > 0 else low_rim()
            high = f[SLOT[plane + 1], center, :] if plane < 3 else high_rim()
            second = 1.2 * mid + weight[slot, center, :] * (beside + (low + high))
            done(slot, second)
            q = second - OMEGA * mid
            total = q if total is None else total + q
            if plane in (0, 3):
                rim = q * (edge_low if plane == 0 else edge_high)
                outer = rim if outer is None else outer + rim
        return total, outer

    from_sides(hd, rxd)

    def odd_rows(step, _):
        at = 32 * step
        here = rows(at, 32)

        def done(slot, second):
            sd[slot, here, :] = second

        summed, outer = second_pass(
            fd, rd, lambda: hd[0, here, :], lambda: hd[1, here, :], at, 32, range(4), done
        )
        center = rows(at + 8, 32)
        waves = (own[0, center, :] - other[0, center, :]) + (own[1, center, :] - other[1, center, :])
        waves = waves + (own[2, center, :] - other[2, center, :]) + (own[3, center, :] - other[3, center, :])
        t_d[here, :] = summed
        x_d[here, :] = (0.04 * scale) * waves - outer
        return 0

    lax.fori_loop(0, 4, odd_rows, 0)
    y_at, y_row = iota((24, 128), 1), iota((24, 128), 0)
    inner = ones_where(y_at // 8 + 1 == y_row)
    beside = ones_where((y_at + 7) // 8 == y_row) + ones_where((y_at + 1) // 8 + 1 == y_row)
    sums = dot(inner, dot(x_d[...], blocks[0]) + dot(t_d[...], blocks[1])) + dot(beside, dot(t_d[...], blocks[0]))
    d_sums[...] = pltpu.roll(sums, 96, 1)
    for m, peer in enumerate(x_peers):
        remote(d_sums, d_x.at[m], rdx, (t, peer))

    strip_2.wait_recv()
    here = ustrip[rows(8 * p, 8), :]
    low, high = (here + nustrip[...]) * ROOT, (here - nustrip[...]) * (ROOT * far_sign)
    for slot in range(4):
        for j, rim in enumerate((low, high)):
            fu[j, slot, 7:8, :] = rim[slot : slot + 1] * ru[j, slot, 7:8, :]
            fu[j, slot, 40:41, :] = rim[4 + slot : 5 + slot] * ru[j, slot, 40:41, :]
    absorb(nu.at[2:4, 0:24, :], r2.at[2])
    absorb(nb.at[2:4, 0:24, :], r1.at[6])
    for slot in (2, 3):
        level_1(slot, p, 0, 24)
        level_2(slot, 0, 24)

    def own_planes(f, weight, sides, base, at, count, planes):
        here, center = rows(at, count), rows(at + 8, count)
        total, outer = None, None
        for plane in planes:
            slot = SLOT[plane]
            mid, beside = beside_yz(f[slot, rows(at, count + 16), :])
            within = weight[slot, center, :] * beside
            base[slot, here, :] = 1.2 * mid + within
            within = 0.4 * mid + within
            q = within + mid * sides[slot, here, :]
            total = q if total is None else total + q
            if plane in (0, 3):
                next_in = f[SLOT[1 if plane == 0 else 2], center, :]
                rim = (within + weight[slot, center, :] * next_in) * (edge_low if plane == 0 else edge_high)
                outer = rim if outer is None else outer + rim
        return total, outer

    def with_sides(f, weight, base, halo, at, count, plane):
        here, center = rows(at, count), rows(at + 8, count)
        low = f[SLOT[plane - 1], center, :] if plane > 0 else halo(0)
        high = f[SLOT[plane + 1], center, :] if plane < 3 else halo(1)
        return base[SLOT[plane], here, :] + weight[SLOT[plane], center, :] * (low + high)

    def near_planes(planes, start, count):
        def body(step, _):
            here = rows(32 * step + start, count)
            summed, outer = own_planes(fv, rv, wv, base_v, 32 * step + start, count, planes)
            if outer is None:
                t_uv[here, :] = summed
            else:
                t_uv[here, :] += summed
                x_uv[here, :] = 0.04 * x_uv[here, :] - outer
            return 0

        lax.fori_loop(0, 2, body, 0)

    def near_rows(planes, start, count):
        def body(step, _):
            here = rows(32 * step + start, count)
            for plane in planes:
                sv[SLOT[plane], here, :] = with_sides(
                    fv, rv, base_v, lambda end: hv[end, here, :], 32 * step + start, count, plane
                )
            return 0

        lax.fori_loop(0, 2, body, 0)

    def far_planes(planes, start, count):
        for j in range(2):
            at = slice(64 + 32 * j + start, 64 + 32 * j + start + count)
            summed, outer = own_planes(fu.at[j], ru.at[j], wu.at[j], base_u.at[j], start, count, planes)
            if outer is None:
                t_uv[at, :] = summed
            else:
                t_uv[at, :] += summed
                x_uv[at, :] = 0.04 * x_uv[at, :] - outer

    def far_rows(plane, start=0, count=32):
        here = slice(start, start + count)
        made = [
            with_sides(fu.at[j], ru.at[j], base_u.at[j], lambda end, j=j: hu[end, j, here, :], start, count, plane)
            for j in range(2)
        ]
        slot = SLOT[plane]
        low, high = made[0] * ROOT, made[1] * (ROOT * far_sign)
        give[slot, here, :] = low - high
        ub_own[slot, here, :] = low + high
        remote(give.at[slot, here, :], ub.at[slot, here, :], rb2.at[slot], (far, x))

    def join(slot, q, ref, start=0, count=32):
        at = 32 * q + start
        low = ref[slot, start : start + count, :] * ROOT
        high = sv[slot, rows(at, count), :] * (ROOT * near_sign)
        gives[slot, rows(at, count), :] = low - high
        bk[slot, rows(64 * b + at, count), :] = low + high
        remote(
            gives.at[slot, rows(at, count), :], bk.at[slot, rows(64 * b + at, count), :], rb1.at[4 if slot == 1 and ref is ub else slot], (near, x)
        )

    def rest(slot):
        absorb(ub.at[slot], rb2.at[slot])
        join(slot, 1 - p, ub)

    def inner_rows(start):
        far_planes((1, 2), start, 16)
        far_rows(1, start, 16)
        far_rows(2, start, 16)
        near_planes((1, 2), start, 16)
        near_rows((1, 2), start, 16)
        join(2, p, ub_own, start, 16)
        join(3, p, ub_own, start, 16)

    inner_rows(0)
    seconds[4].wait_recv()
    firsts[8].wait_recv()
    for slot in (2, 3):
        level_1(slot, p, 24, 8)
        level_2(slot, 24, 8)
    inner_rows(16)
    far_planes((0, 3), 0, 32)
    near_planes((0, 3), 0, 32)

    y_at, y_row = iota((32, 128), 1), iota((32, 128), 0)
    start = jnp.where(y_at < 64, 0, 16 + 8 * ((y_at - 64) // 32))
    y_in = jnp.where(y_at < 64, y_at, y_at % 32)
    inner = ones_where(start + y_in // 8 + 1 == y_row)
    beside = ones_where(start + (y_in + 7) // 8 == y_row) + ones_where(start + (y_in + 1) // 8 + 1 == y_row)
    sums = dot(inner, dot(x_uv[...], blocks[0]) + dot(t_uv[...], blocks[1])) + dot(beside, dot(t_uv[...], blocks[0]))
    uv_sums[...] = (sums[16:24] + pltpu.roll(sums[24:32], 32, 1)) + (
        pltpu.roll(sums[0:8], 64, 1) + pltpu.roll(sums[8:16], 96, 1)
    )
    for m, peer in enumerate(x_peers):
        remote(uv_sums, uv_x.at[m], rc, (t, peer))
    from_sides(hu, rxu)
    far_rows(0)
    far_rows(3)
    from_sides(hv, rxv)
    near_rows((0, 3), 0, 32)
    join(0, p, ub_own)
    join(1, p, ub_own)
    rest(2)
    absorb(uv_x, rc)
    uv_total[...] = (uv_sums[...] + uv_x[0]) + (uv_x[1] + uv_x[2])
    for peer in group:
        remote(uv_total, tr.at[e], rg, (peer, x))
    tr[e] = uv_total[...]
    rest(3)
    absorb(d_x, rdx)
    absorb(pot_all.at[1:4], rp)
    d_total[...] = (d_sums[...] + d_x[0]) + (d_x[1] + d_x[2])
    d_swap = remote(d_total, d_other, rdp, (partner, x))

    def finish(slot, start, count=64):
        here = rows(start, count)
        even, odd = bk[slot, here, :], sd[slot, here, :] * sign
        yours[slot, here, :] = (even - odd) * ROOT
        there = out.at[0, PLANES[slot], rows(128 * k + start, count), :]
        remote(yours.at[slot, here, :], there, ro, (partner, x))
        mine[slot, here, :] = (even + odd) * ROOT
        local(mine.at[slot, here, :], there, lo)

    rest(0)
    rest(1)
    for slot in (2, 3, 0, 1):
        finish(slot, 64 * b)

    def finish_far(slot):
        absorb(gives.at[slot], rb1.at[slot])
        finish(slot, 64 - 64 * b)

    for slot in (2, 3, 0):
        finish_far(slot)
    for q, index in ((p, 1), (1 - p, 4)):
        absorb(gives.at[1, 0:32, :], rb1.at[index])
        finish(1, 64 - 64 * b + 32 * q, 32)
    absorb(tr.at[0:7], rg)
    d_swap.wait_recv()

    lane = iota((32, 128), 1)
    coef = lane // 32
    gathered = tr[...].reshape(64, 128)
    rem_v = dot(pick[1], gathered) + pltpu.roll(dot(pick[2], gathered), 96, 1)
    rem_d = dot(pick_d[0], d_total[...]) + dot(pick_d[1], d_other[...])
    rem = jnp.where(coef < 2, dot(pick[0], gathered), jnp.where(coef == 2, rem_v, rem_d))
    shift = jnp.where(
        coef == 0, shift_ref[3], jnp.where(coef == 1, shift_ref[2], jnp.where(coef == 2, shift_ref[1], shift_0))
    )
    coarse_pot = (pot_all[0] + pot_all[1]) + (pot_all[2] + pot_all[3])
    diag = coarse_pot + shift * 1024.0 + 640.0
    one = rem / diag
    row = iota((32, 128), 0)
    up = jnp.where(row == 0, 0.0, pltpu.roll(one, 1, 0))
    down = jnp.where(row == 31, 0.0, pltpu.roll(one, 31, 0))
    left = jnp.where(lane % 32 == 0, 0.0, pltpu.roll(one, 1, 1))
    right = jnp.where(lane % 32 == 31, 0.0, pltpu.roll(one, 127, 1))
    applied = diag * one - 128.0 * ((up + down) + (left + right))
    fix = one + (rem - applied) / diag
    weight = jnp.where(
        coef == 0, 0.5 * ROOT, jnp.where(coef == 1, 0.5 * ROOT * far_sign, jnp.where(coef == 2, 0.5 * near_sign, scale))
    )
    widen = ones_where(iota((128, 256), 0) % 32 == iota((128, 256), 1) // 8)
    fix_all[...] = dot(fix * weight, widen)
    fix_store = local(fix_all, fix_out, f_sem)

    outer = (x == 0) | (x == 3)
    pl.when(outer)(lambda: absorb(all_sent.at[0:2400, :], sent))
    pl.when(jnp.logical_not(outer))(lambda: absorb(all_sent, sent))
    absorb(yours, ro)
    absorb(mine, lo)
    fix_store.wait()


def shards(source, potential, level_shift):
    dma = pltpu.SemaphoreType.DMA
    vmem = lambda *shape: pltpu.VMEM(shape, F32)
    scratch = dict(
        shift_ref=pltpu.SMEM((4,), F32),
        own=vmem(4, 144, 256), other=vmem(4, 144, 256), pot=vmem(4, 144, 256), pot_other=vmem(4, 128, 256), s_buf=vmem(4, 144, 256),
        rd=vmem(4, 144, 256), fd=vmem(4, 144, 256), sd=vmem(4, 128, 256), strip=vmem(2, 16, 256),
        nb=vmem(4, 64, 256), raw=vmem(2, 32, 256), nstrip=vmem(16, 256), u_buf=vmem(4, 80, 256), fv=vmem(4, 80, 256), rv=vmem(4, 80, 256),
        sv=vmem(4, 64, 256), ustrip=vmem(16, 256), nu=vmem(4, 32, 256), nustrip=vmem(8, 256),
        fu=vmem(2, 4, 48, 256), ru=vmem(2, 4, 48, 256),
        pot_side=vmem(2, 128, 256), wv=vmem(4, 64, 256), wu=vmem(2, 4, 32, 256), base_v=vmem(4, 64, 256), base_u=vmem(2, 4, 32, 256),
        hd=vmem(2, 128, 256), hv=vmem(2, 64, 256), hu=vmem(2, 2, 32, 256),
        ub=vmem(4, 32, 256), ub_own=vmem(4, 32, 256), give=vmem(4, 32, 256), bk=vmem(4, 128, 256), gives=vmem(4, 64, 256),
        t_d=vmem(128, 256), x_d=vmem(128, 256), t_uv=vmem(128, 256), x_uv=vmem(128, 256),
        pot_all=vmem(4, 32, 128), d_sums=vmem(24, 128), d_x=vmem(3, 24, 128), d_total=vmem(24, 128),
        d_other=vmem(24, 128), uv_sums=vmem(8, 128), uv_x=vmem(3, 8, 128), uv_total=vmem(8, 128),
        tr=vmem(8, 8, 128), blocks=vmem(2, 256, 128), pick=vmem(3, 32, 64), pick_d=vmem(2, 32, 24),
        fix_all=vmem(32, 256), mine=vmem(4, 128, 256), yours=vmem(4, 128, 256),
        all_sent=vmem(2784, 256),
        h_sem=dma(()), l_sem=dma(()), p_sem=dma(()), q_sem=dma(()), f_sem=dma(()), sent=dma(()), r_raw=dma(()), r0=dma((2,)), r1=dma((7,)),
        r2=dma((4,)), rt=dma(()), ru_sem=dma(()), rxp=dma((2,)), rxd=dma((2,)), rxv=dma((2,)), rxu=dma((2,)), rp=dma(()), rdx=dma(()), rdp=dma(()), rc=dma(()),
        rg=dma(()), rb2=dma((4,)), rb1=dma((5,)), ro=dma(()), lo=dma(()),
    )
    raw, fix = pl.pallas_call(
        kernel,
        out_shape=(jax.ShapeDtypeStruct(source.shape, F32), jax.ShapeDtypeStruct((32, 256), F32)),
        in_specs=[
            pl.BlockSpec(memory_space=pltpu.HBM),
            pl.BlockSpec(memory_space=pltpu.HBM),
            pl.BlockSpec(memory_space=pltpu.HBM),
        ],
        out_specs=(pl.BlockSpec(memory_space=pl.ANY), pl.BlockSpec(memory_space=pl.ANY)),
        scratch_shapes=list(scratch.values()),
        compiler_params=pltpu.CompilerParams(
            collective_id=0, has_side_effects=True, vmem_limit_bytes=40 * 2**20
        ),
        name="space_time_apply",
    )(*(pltpu.with_memory_space_constraint(a, pltpu.HBM) for a in (level_shift, source, potential)))
    return (raw.reshape(4, 32, 8, 256) + fix[None, :, None, :]).reshape(source.shape)


def solution(mesh):
    in_specs = (P("tm", "plane", None, None), P("plane", None, None), P())
    out_specs = P("tm", "plane", None, None)
    return jax.shard_map(shards, mesh=mesh, in_specs=in_specs, out_specs=out_specs, check_vma=False)
```

```python
import math

import jax
import jax.numpy as jnp
from jax import lax
from jax.experimental import pallas as pl
from jax.experimental.pallas import tpu as pltpu
from jax.sharding import PartitionSpec as P

F32 = jnp.float32
MESH = pl.DeviceIdType.MESH
ROOT = 1.0 / math.sqrt(2.0)
OMEGA = 0.8
PLANES = (0, 3, 1, 2)
SLOT = {plane: slot for slot, plane in enumerate(PLANES)}


def dot(a, b):
    return jnp.dot(a, b, precision=lax.Precision.HIGHEST, preferred_element_type=F32)


def iota(shape, dim):
    return lax.broadcasted_iota(jnp.int32, shape, dim)


def ones_where(mask):
    return jnp.where(mask, 1.0, 0.0).astype(F32)


def beside_yz(ext):
    rows = ext.shape[0] - 16
    mid = ext[8 : 8 + rows]
    up = pltpu.roll(ext, 1, 0)[8 : 8 + rows]
    down = pltpu.roll(ext, rows + 15, 0)[8 : 8 + rows]
    col = iota(mid.shape, 1)
    left = jnp.where(col == 0, 0.0, pltpu.roll(mid, 1, 1))
    right = jnp.where(col == 255, 0.0, pltpu.roll(mid, 255, 1))
    return mid, (up + down) + (left + right)


def kernel(
    shift_hbm, source, potential, out, fix_out,
    shift_ref, own, other, pot, pot_other, s_buf, rd, fd, sd, strip, nb, raw, nstrip, u_buf, fv, rv, sv, ustrip, nu, nustrip, fu, ru,
    pot_side, wv, wu, base_v, base_u, hd, hv, hu, ub, ub_own, give, bk, gives, t_d, x_d, t_uv, x_uv, pot_all, d_sums, d_x, d_total, d_other, uv_sums, uv_x, uv_total,
    tr, blocks, pick, pick_d, fix_all, mine, yours,
    all_sent, h_sem, l_sem, p_sem, sent, ends, r_raw, r0, r1, r2, rt, ru_sem, rxp, rxd, rxv, rxu, rp, rdx, rdp, rc, rg, rb2, rb1,
):
    t, x = lax.axis_index("tm"), lax.axis_index("plane")
    e = t % 8
    k, c = e % 2, e // 2
    b, p = c % 2, c // 2
    partner = t + 1 - 2 * k
    near = t + 2 - 4 * b
    far = t + 4 - 8 * p
    x_peers = [(x + m) % 4 for m in (1, 2, 3)]
    group = [t - e + (e + m) % 8 for m in range(1, 8)]

    barrier = pltpu.get_barrier_semaphore()
    for peer in (far, near, near + 1 - 2 * k, partner):
        pl.semaphore_signal(barrier, inc=1, device_id=(peer, x), device_id_type=MESH)
    for peer in x_peers:
        pl.semaphore_signal(barrier, inc=1, device_id=(t, peer), device_id_type=MESH)

    def rows(start, count):
        return pl.ds(pl.multiple_of(start, 8), count)

    def remote(src, dst, recv, where):
        copy = pltpu.make_async_remote_copy(
            src_ref=src, dst_ref=dst, send_sem=sent, recv_sem=recv, device_id=where, device_id_type=MESH
        )
        copy.start()
        return copy

    def absorb(ref, sem):
        pltpu.make_async_copy(ref, ref, sem).wait()

    def local(src, dst, sem):
        copy = pltpu.make_async_copy(src, dst, sem)
        copy.start()
        return copy

    for slot, plane in enumerate(PLANES):
        local(source.at[0, plane, rows(120 * k, 136), :], own.at[slot, rows(8 - 8 * k, 136), :], l_sem)
    shift_load = local(shift_hbm, shift_ref, h_sem)
    for slot, plane in enumerate(PLANES):
        local(potential.at[plane, rows(120 * k, 136), :], pot.at[slot, rows(8 - 8 * k, 136), :], p_sem)
    local(potential.at[:, rows(128 - 128 * k, 128), :], pot_other, p_sem)
    for slot in range(4):
        for ref in (own, other, pot):
            ref[slot, rows(136 * k, 8), :] = jnp.zeros((8, 256), F32)

    pl.semaphore_wait(barrier, 7)

    first_rows = 64 - 64 * b + 32 - 32 * p
    remote(source.at[0, PLANES[0], rows(128 * k + first_rows, 32), :], raw.at[0], r_raw, (near, x))
    remote(source.at[0, PLANES[0], rows(128 - 128 * k + first_rows, 32), :], raw.at[1], r_raw, (near + 1 - 2 * k, x))
    for slot in (1, 0, 2, 3):
        remote(
            source.at[0, PLANES[slot], rows(120 - 120 * k, 136), :], other.at[slot, rows(8 * k, 136), :],
            r0.at[0 if slot == 1 else 1], (partner, x),
        )

    def to_side(src, halo, end, sem):
        @pl.when(x < 3 if end == 0 else x > 0)
        def _():
            remote(src, halo.at[end], sem.at[end], (t, x + 1 - 2 * end))

    def from_sides(halo, sem):
        for end in range(2):
            pl.when(x > 0 if end == 0 else x < 3)(lambda end=end: absorb(halo.at[end], sem.at[end]))

    for end in range(2):
        @pl.when(x == 3 * end)
        def _():
            hd[end] = jnp.zeros((128, 256), F32)
            hv[end] = jnp.zeros((64, 256), F32)
            hu[end] = jnp.zeros((2, 32, 256), F32)
            pot_side[end] = jnp.zeros((128, 256), F32)

    to_side(potential.at[0, rows(128 * k, 128), :], pot_side, 1, rxp)
    to_side(potential.at[3, rows(128 * k, 128), :], pot_side, 0, rxp)

    def to_near(index, slots, q, start=0, count=32):
        at = 32 * q + start
        firsts[index] = remote(
            s_buf.at[slots, rows(72 - 64 * b + at, count), :], nb.at[slots, rows(at, count), :],
            r1.at[min(index, 6) if index < 8 else 0], (near, x),
        )

    firsts = {}
    absorb(own.at[:, 0:136, :], l_sem)
    absorb(other.at[1, 0:136, :], r0.at[0])
    s_buf[1] = (own[1] + other[1]) * ROOT
    to_near(1, 1, 1 - p)
    absorb(other.at[0:3, 0:136, :], r0.at[1])
    for slot in (0, 2, 3):
        s_buf[slot] = (own[slot] + other[slot]) * ROOT
    for h in range(2):
        for i in range(4):
            for at, row in ((0, 7), (4, 40), (8, 39), (12, 72)):
                strip[h, at + i : at + i + 1, :] = s_buf[i, row + 64 * h : row + 64 * h + 1, :]
    strip_1 = remote(strip.at[1 - b], nstrip, rt, (near, x))
    to_near(2, 2, 1 - p)
    to_near(3, 3, 1 - p)

    sign = (1 - 2 * k).astype(F32)
    near_sign = (1 - 2 * b).astype(F32)
    far_sign = (1 - 2 * p).astype(F32)
    scale = ROOT * sign
    edge_low, edge_high = ones_where(x == 0), ones_where(x == 3)
    shift_load.wait()
    shift_0 = shift_ref[0]
    absorb(all_sent.at[0:1056, :], p_sem)
    for slot in range(4):
        rd[slot] = OMEGA / (6.0 + pot[slot] + shift_0)
        fd[slot] = (own[slot] - other[slot]) * scale * rd[slot]


    to_side(fd.at[0, 8:136, :], hd, 1, rxd)
    to_side(fd.at[1, 8:136, :], hd, 0, rxd)

    for slot in range(4):
        rv[slot] = OMEGA / (6.0 + pot[slot, rows(64 * b, 80), :] + shift_ref[1])
        here = 6.0 + pot[slot, rows(64 * b + 32 * p, 48), :]
        ru[0, slot] = OMEGA / (here + shift_ref[3])
        ru[1, slot] = OMEGA / (here + shift_ref[2])

    z_at, z_block = iota((256, 128), 0), iota((256, 128), 1)
    lane_block = ones_where(z_at // 8 == z_block % 32)
    row, col = iota((32, 128), 0), iota((32, 128), 1)
    pot_sum = (pot[0, 8:136, :] + pot[1, 8:136, :]) + (pot[2, 8:136, :] + pot[3, 8:136, :])
    pot_rest = (pot_other[0] + pot_other[1]) + (pot_other[2] + pot_other[3])
    pot_all[0] = dot(ones_where(col // 8 + 16 * k == row), dot(pot_sum, lane_block)) + dot(
        ones_where(col // 8 + 16 - 16 * k == row), dot(pot_rest, lane_block)
    )
    for m, peer in enumerate(x_peers):
        remote(pot_all.at[0], pot_all.at[m + 1], rp, (t, peer))
    block = ones_where(z_at // 8 == z_block)
    around = ones_where((z_at + 7) // 8 == z_block + 1) + ones_where((z_at + 1) // 8 == z_block)
    blocks[0] = block
    blocks[1] = jnp.where(z_block < 32, 2.0 * block + around, 0.0)

    row, col = iota((32, 64), 0), iota((32, 64), 1)
    sender, r = col // 8, col % 8
    sender_c = sender // 2
    sender_b, sender_p = sender_c % 2, sender_c // 2
    sender_at = 16 * (sender % 2) + 8 * sender_b - 1 + r
    pick[0] = ones_where((r < 6) & (sender_at + 4 * sender_p == row))
    pick[1] = ones_where((sender_p == p) & (sender_at == row))
    pick[2] = ones_where((sender_p == p) & (r < 2) & (sender_at + 8 == row))
    row, col = iota((32, 24), 0), iota((32, 24), 1)
    pick_d[0] = ones_where((col < 18) & (16 * k - 1 + col == row))
    pick_d[1] = ones_where((col < 18) & (16 * (1 - k) - 1 + col == row))

    def level_1(slot, q, start=0, count=32):
        inside = 32 * q + start
        here = s_buf[slot, rows(8 + 64 * b + inside, count), :]
        there = nb[slot, rows(inside, count), :]
        at = rows(8 + inside, count)
        u_buf[slot, at, :] = (here + there) * ROOT
        detail = (here - there) * (ROOT * near_sign)
        fv[slot, at, :] = detail * rv[slot, at, :]
        at = rows(inside, count)
        x_uv[at, :] = detail if slot == 0 else x_uv[at, :] + detail

    seconds = {}

    def to_far(index, slots, start=0, count=32):
        seconds[index] = remote(
            u_buf.at[slots, rows(40 - 32 * p + start, count), :], nu.at[slots, start : start + count, :],
            r2.at[index - index // 3], (far, x),
        )

    def passed_on(slot):
        if slot == 0:
            absorb(raw, r_raw)
            nb[0, rows(32 - 32 * p, 32), :] = (raw[0] + raw[1]) * ROOT
        else:
            firsts[slot].wait_recv()
        level_1(slot, 1 - p)
        to_far(slot, slot, 0, 32 if slot < 2 else 24)

    def level_2(slot, start=0, count=32):
        here = u_buf[slot, rows(8 + 32 * p + start, count), :]
        there = nu[slot, start : start + count, :]
        low, high = (here + there) * ROOT, (here - there) * (ROOT * far_sign)
        at = slice(8 + start, 8 + start + count)
        fu[0, slot, at, :] = low * ru[0, slot, at, :]
        fu[1, slot, at, :] = high * ru[1, slot, at, :]
        for first, field in ((64 + start, low), (96 + start, high)):
            at = slice(first, first + count)
            x_uv[at, :] = field if slot == 0 else x_uv[at, :] + field

    inner_slots = slice(2, 4)
    for slot in range(4):
        passed_on(slot)
        if slot < 2:
            to_near(4 + slot, slot, p)
        if slot == 0:
            strip_1.wait_recv()
            ustrip[...] = (strip[b] + nstrip[...]) * ROOT
            strip_2 = remote(ustrip.at[rows(8 - 8 * p, 8), :], nustrip, ru_sem, (far, x))
    to_near(6, 2, p, 0, 24)
    to_near(7, 3, p, 0, 24)
    to_far(4, inner_slots, 24, 8)
    to_near(8, inner_slots, p, 24, 8)
    details = (strip[b] - nstrip[...]) * (ROOT * near_sign)
    for slot in range(4):
        fv[slot, 7:8, :] = details[slot : slot + 1] * rv[slot, 7:8, :]
        fv[slot, 72:73, :] = details[12 + slot : 13 + slot] * rv[slot, 72:73, :]
        if slot > 1:
            fv[slot, 39:40, :] = details[8 + slot : 9 + slot] * rv[slot, 39:40, :]
    from_sides(pot_side, rxp)
    kept = [ones_where(x > 0), ones_where(x < 3)]

    def beside_weights(weight, start, count, shift, out):
        side = []
        for end in range(2):
            field = 6.0 + pot_side[end, rows(start, count), :] + shift
            side.append((OMEGA * kept[end]) / field)
        inner = [weight[SLOT[plane], 8 : 8 + count, :] for plane in range(4)]
        out[SLOT[0]] = side[0] + inner[1]
        out[SLOT[1]] = inner[0] + inner[2]
        out[SLOT[2]] = inner[1] + inner[3]
        out[SLOT[3]] = inner[2] + side[1]

    beside_weights(rv, 64 * b, 64, shift_ref[1], wv)
    for j, level in ((0, 3), (1, 2)):
        beside_weights(ru.at[j], 64 * b + 32 * p, 32, shift_ref[level], wu.at[j])

    for slot, end in ((0, 1), (1, 0)):
        firsts[4 + slot].wait_recv()
        level_1(slot, p)
        seconds[slot].wait_recv()
        level_2(slot)
        to_side(fu.at[:, slot, 8:40, :], hu, end, rxu)
        to_side(fv.at[slot, 8:72, :], hv, end, rxv)

    def second_pass(f, weight, low_rim, high_rim, at, count, order, done):
        center = rows(at + 8, count)
        total, outer = None, None
        for plane in order:
            slot = SLOT[plane]
            mid, beside = beside_yz(f[slot, rows(at, count + 16), :])
            low = f[SLOT[plane - 1], center, :] if plane > 0 else low_rim()
            high = f[SLOT[plane + 1], center, :] if plane < 3 else high_rim()
            second = 1.2 * mid + weight[slot, center, :] * (beside + (low + high))
            done(slot, second)
            q = second - OMEGA * mid
            total = q if total is None else total + q
            if plane in (0, 3):
                rim = q * (edge_low if plane == 0 else edge_high)
                outer = rim if outer is None else outer + rim
        return total, outer

    from_sides(hd, rxd)

    def odd_rows(step, _):
        at = 32 * step
        here = rows(at, 32)

        def done(slot, second):
            sd[slot, here, :] = second

        summed, outer = second_pass(
            fd, rd, lambda: hd[0, here, :], lambda: hd[1, here, :], at, 32, range(4), done
        )
        center = rows(at + 8, 32)
        waves = (own[0, center, :] - other[0, center, :]) + (own[1, center, :] - other[1, center, :])
        waves = waves + (own[2, center, :] - other[2, center, :]) + (own[3, center, :] - other[3, center, :])
        t_d[here, :] = summed
        x_d[here, :] = (0.04 * scale) * waves - outer
        return 0

    lax.fori_loop(0, 4, odd_rows, 0)
    y_at, y_row = iota((24, 128), 1), iota((24, 128), 0)
    inner = ones_where(y_at // 8 + 1 == y_row)
    beside = ones_where((y_at + 7) // 8 == y_row) + ones_where((y_at + 1) // 8 + 1 == y_row)
    sums = dot(inner, dot(x_d[...], blocks[0]) + dot(t_d[...], blocks[1])) + dot(beside, dot(t_d[...], blocks[0]))
    d_sums[...] = pltpu.roll(sums, 96, 1)
    for m, peer in enumerate(x_peers):
        remote(d_sums, d_x.at[m], rdx, (t, peer))

    strip_2.wait_recv()
    here = ustrip[rows(8 * p, 8), :]
    low, high = (here + nustrip[...]) * ROOT, (here - nustrip[...]) * (ROOT * far_sign)
    for slot in range(4):
        for j, rim in enumerate((low, high)):
            fu[j, slot, 7:8, :] = rim[slot : slot + 1] * ru[j, slot, 7:8, :]
            fu[j, slot, 40:41, :] = rim[4 + slot : 5 + slot] * ru[j, slot, 40:41, :]
    absorb(nu.at[2:4, 0:24, :], r2.at[2])
    absorb(nb.at[2:4, 0:24, :], r1.at[6])
    for slot in (2, 3):
        level_1(slot, p, 0, 24)
        level_2(slot, 0, 24)

    def own_planes(f, weight, sides, base, at, count, planes):
        here, center = rows(at, count), rows(at + 8, count)
        total, outer = None, None
        for plane in planes:
            slot = SLOT[plane]
            mid, beside = beside_yz(f[slot, rows(at, count + 16), :])
            within = weight[slot, center, :] * beside
            base[slot, here, :] = 1.2 * mid + within
            within = 0.4 * mid + within
            q = within + mid * sides[slot, here, :]
            total = q if total is None else total + q
            if plane in (0, 3):
                next_in = f[SLOT[1 if plane == 0 else 2], center, :]
                rim = (within + weight[slot, center, :] * next_in) * (edge_low if plane == 0 else edge_high)
                outer = rim if outer is None else outer + rim
        return total, outer

    def with_sides(f, weight, base, halo, at, count, plane):
        here, center = rows(at, count), rows(at + 8, count)
        low = f[SLOT[plane - 1], center, :] if plane > 0 else halo(0)
        high = f[SLOT[plane + 1], center, :] if plane < 3 else halo(1)
        return base[SLOT[plane], here, :] + weight[SLOT[plane], center, :] * (low + high)

    def near_planes(planes, start, count):
        def body(step, _):
            here = rows(32 * step + start, count)
            summed, outer = own_planes(fv, rv, wv, base_v, 32 * step + start, count, planes)
            if outer is None:
                t_uv[here, :] = summed
            else:
                t_uv[here, :] += summed
                x_uv[here, :] = 0.04 * x_uv[here, :] - outer
            return 0

        lax.fori_loop(0, 2, body, 0)

    def near_rows(planes, start, count):
        def body(step, _):
            here = rows(32 * step + start, count)
            for plane in planes:
                sv[SLOT[plane], here, :] = with_sides(
                    fv, rv, base_v, lambda end: hv[end, here, :], 32 * step + start, count, plane
                )
            return 0

        lax.fori_loop(0, 2, body, 0)

    def far_planes(planes, start, count):
        for j in range(2):
            at = slice(64 + 32 * j + start, 64 + 32 * j + start + count)
            summed, outer = own_planes(fu.at[j], ru.at[j], wu.at[j], base_u.at[j], start, count, planes)
            if outer is None:
                t_uv[at, :] = summed
            else:
                t_uv[at, :] += summed
                x_uv[at, :] = 0.04 * x_uv[at, :] - outer

    def far_rows(plane, start=0, count=32):
        here = slice(start, start + count)
        made = [
            with_sides(fu.at[j], ru.at[j], base_u.at[j], lambda end, j=j: hu[end, j, here, :], start, count, plane)
            for j in range(2)
        ]
        slot = SLOT[plane]
        low, high = made[0] * ROOT, made[1] * (ROOT * far_sign)
        give[slot, here, :] = low - high
        ub_own[slot, here, :] = low + high
        remote(give.at[slot, here, :], ub.at[slot, here, :], rb2.at[slot], (far, x))

    def join(slot, q, ref, start=0, count=32):
        at = 32 * q + start
        low = ref[slot, start : start + count, :] * ROOT
        high = sv[slot, rows(at, count), :] * (ROOT * near_sign)
        gives[slot, rows(at, count), :] = low - high
        bk[slot, rows(64 * b + at, count), :] = low + high
        remote(
            gives.at[slot, rows(at, count), :], bk.at[slot, rows(64 * b + at, count), :], rb1.at[4 if slot == 1 and ref is ub else slot], (near, x)
        )

    def rest(slot):
        absorb(ub.at[slot], rb2.at[slot])
        join(slot, 1 - p, ub)

    def inner_rows(start):
        far_planes((1, 2), start, 16)
        far_rows(1, start, 16)
        far_rows(2, start, 16)
        near_planes((1, 2), start, 16)
        near_rows((1, 2), start, 16)
        join(2, p, ub_own, start, 16)
        join(3, p, ub_own, start, 16)

    inner_rows(0)
    seconds[4].wait_recv()
    firsts[8].wait_recv()
    for slot in (2, 3):
        level_1(slot, p, 24, 8)
        level_2(slot, 24, 8)
    inner_rows(16)
    far_planes((0, 3), 0, 32)
    near_planes((0, 3), 0, 32)

    y_at, y_row = iota((32, 128), 1), iota((32, 128), 0)
    start = jnp.where(y_at < 64, 0, 16 + 8 * ((y_at - 64) // 32))
    y_in = jnp.where(y_at < 64, y_at, y_at % 32)
    inner = ones_where(start + y_in // 8 + 1 == y_row)
    beside = ones_where(start + (y_in + 7) // 8 == y_row) + ones_where(start + (y_in + 1) // 8 + 1 == y_row)
    sums = dot(inner, dot(x_uv[...], blocks[0]) + dot(t_uv[...], blocks[1])) + dot(beside, dot(t_uv[...], blocks[0]))
    uv_sums[...] = (sums[16:24] + pltpu.roll(sums[24:32], 32, 1)) + (
        pltpu.roll(sums[0:8], 64, 1) + pltpu.roll(sums[8:16], 96, 1)
    )
    for m, peer in enumerate(x_peers):
        remote(uv_sums, uv_x.at[m], rc, (t, peer))
    from_sides(hu, rxu)
    far_rows(0)
    far_rows(3)
    from_sides(hv, rxv)
    near_rows((0, 3), 0, 32)
    join(0, p, ub_own)
    join(1, p, ub_own)
    rest(2)
    absorb(uv_x, rc)
    uv_total[...] = (uv_sums[...] + uv_x[0]) + (uv_x[1] + uv_x[2])
    for peer in group:
        remote(uv_total, tr.at[e], rg, (peer, x))
    tr[e] = uv_total[...]
    rest(3)
    absorb(d_x, rdx)
    absorb(pot_all.at[1:4], rp)
    d_total[...] = (d_sums[...] + d_x[0]) + (d_x[1] + d_x[2])
    d_swap = remote(d_total, d_other, rdp, (partner, x))

    def finish(slot, start, count=64):
        here = rows(start, count)
        even, odd = bk[slot, here, :], sd[slot, here, :] * sign
        yours[slot, here, :] = (even - odd) * ROOT
        there = out.at[0, PLANES[slot], rows(128 * k + start, count), :]
        remote(yours.at[slot, here, :], there, ends, (partner, x))
        mine[slot, here, :] = (even + odd) * ROOT
        local(mine.at[slot, here, :], there, sent)

    rest(0)
    rest(1)
    for slot in (2, 3, 0, 1):
        finish(slot, 64 * b)

    def finish_far(slot):
        absorb(gives.at[slot], rb1.at[slot])
        finish(slot, 64 - 64 * b)

    for slot in (2, 3, 0):
        finish_far(slot)
    for q, index in ((p, 1), (1 - p, 4)):
        absorb(gives.at[1, 0:32, :], rb1.at[index])
        finish(1, 64 - 64 * b + 32 * q, 32)
    absorb(tr.at[0:7], rg)
    d_swap.wait_recv()

    lane = iota((32, 128), 1)
    coef = lane // 32
    gathered = tr[...].reshape(64, 128)
    rem_v = dot(pick[1], gathered) + pltpu.roll(dot(pick[2], gathered), 96, 1)
    rem_d = dot(pick_d[0], d_total[...]) + dot(pick_d[1], d_other[...])
    rem = jnp.where(coef < 2, dot(pick[0], gathered), jnp.where(coef == 2, rem_v, rem_d))
    shift = jnp.where(
        coef == 0, shift_ref[3], jnp.where(coef == 1, shift_ref[2], jnp.where(coef == 2, shift_ref[1], shift_0))
    )
    coarse_pot = (pot_all[0] + pot_all[1]) + (pot_all[2] + pot_all[3])
    diag = coarse_pot + shift * 1024.0 + 640.0
    one = rem / diag
    row = iota((32, 128), 0)
    up = jnp.where(row == 0, 0.0, pltpu.roll(one, 1, 0))
    down = jnp.where(row == 31, 0.0, pltpu.roll(one, 31, 0))
    left = jnp.where(lane % 32 == 0, 0.0, pltpu.roll(one, 1, 1))
    right = jnp.where(lane % 32 == 31, 0.0, pltpu.roll(one, 127, 1))
    applied = diag * one - 128.0 * ((up + down) + (left + right))
    fix = one + (rem - applied) / diag
    weight = jnp.where(
        coef == 0, 0.5 * ROOT, jnp.where(coef == 1, 0.5 * ROOT * far_sign, jnp.where(coef == 2, 0.5 * near_sign, scale))
    )
    widen = ones_where(iota((128, 256), 0) % 32 == iota((128, 256), 1) // 8)
    fix_all[...] = dot(fix * weight, widen)
    local(fix_all, fix_out, sent)

    outer = (x == 0) | (x == 3)
    pl.when(outer)(lambda: absorb(all_sent.at[0:2944, :], sent))
    pl.when(jnp.logical_not(outer))(lambda: absorb(all_sent, sent))
    absorb(yours, ends)


def add_fix(raw, fix, out, buffer, sems):
    copies = []
    for plane in range(4):
        for i in range(32):
            at = slice(8 * i, 8 * i + 8)
            buffer[plane, at, :] = raw[0, plane, at, :] + fix[i : i + 1, :]
        copy = pltpu.make_async_copy(buffer.at[plane], out.at[0, plane], sems.at[plane])
        copy.start()
        copies.append(copy)
    for copy in copies:
        copy.wait()


def shards(source, potential, level_shift):
    dma = pltpu.SemaphoreType.DMA
    vmem = lambda *shape: pltpu.VMEM(shape, F32)
    scratch = dict(
        shift_ref=pltpu.SMEM((4,), F32),
        own=vmem(4, 144, 256), other=vmem(4, 144, 256), pot=vmem(4, 144, 256), pot_other=vmem(4, 128, 256), s_buf=vmem(4, 144, 256),
        rd=vmem(4, 144, 256), fd=vmem(4, 144, 256), sd=vmem(4, 128, 256), strip=vmem(2, 16, 256),
        nb=vmem(4, 64, 256), raw=vmem(2, 32, 256), nstrip=vmem(16, 256), u_buf=vmem(4, 80, 256), fv=vmem(4, 80, 256), rv=vmem(4, 80, 256),
        sv=vmem(4, 64, 256), ustrip=vmem(16, 256), nu=vmem(4, 32, 256), nustrip=vmem(8, 256),
        fu=vmem(2, 4, 48, 256), ru=vmem(2, 4, 48, 256),
        pot_side=vmem(2, 128, 256), wv=vmem(4, 64, 256), wu=vmem(2, 4, 32, 256), base_v=vmem(4, 64, 256), base_u=vmem(2, 4, 32, 256),
        hd=vmem(2, 128, 256), hv=vmem(2, 64, 256), hu=vmem(2, 2, 32, 256),
        ub=vmem(4, 32, 256), ub_own=vmem(4, 32, 256), give=vmem(4, 32, 256), bk=vmem(4, 128, 256), gives=vmem(4, 64, 256),
        t_d=vmem(128, 256), x_d=vmem(128, 256), t_uv=vmem(128, 256), x_uv=vmem(128, 256),
        pot_all=vmem(4, 32, 128), d_sums=vmem(24, 128), d_x=vmem(3, 24, 128), d_total=vmem(24, 128),
        d_other=vmem(24, 128), uv_sums=vmem(8, 128), uv_x=vmem(3, 8, 128), uv_total=vmem(8, 128),
        tr=vmem(8, 8, 128), blocks=vmem(2, 256, 128), pick=vmem(3, 32, 64), pick_d=vmem(2, 32, 24),
        fix_all=vmem(32, 256), mine=vmem(4, 128, 256), yours=vmem(4, 128, 256),
        all_sent=vmem(3328, 256),
        h_sem=dma(()), l_sem=dma(()), p_sem=dma(()), sent=dma(()), ends=dma(()), r_raw=dma(()), r0=dma((2,)), r1=dma((7,)),
        r2=dma((4,)), rt=dma(()), ru_sem=dma(()), rxp=dma((2,)), rxd=dma((2,)), rxv=dma((2,)), rxu=dma((2,)), rp=dma(()), rdx=dma(()), rdp=dma(()), rc=dma(()),
        rg=dma(()), rb2=dma((4,)), rb1=dma((5,)),
    )
    raw, fix = pl.pallas_call(
        kernel,
        out_shape=(jax.ShapeDtypeStruct(source.shape, F32), jax.ShapeDtypeStruct((32, 256), F32)),
        in_specs=[
            pl.BlockSpec(memory_space=pltpu.HBM),
            pl.BlockSpec(memory_space=pltpu.HBM),
            pl.BlockSpec(memory_space=pltpu.HBM),
        ],
        out_specs=(pl.BlockSpec(memory_space=pl.ANY), pl.BlockSpec(memory_space=pl.ANY)),
        scratch_shapes=list(scratch.values()),
        compiler_params=pltpu.CompilerParams(
            collective_id=0, has_side_effects=True, vmem_limit_bytes=40 * 2**20
        ),
        name="space_time_apply",
    )(*(pltpu.with_memory_space_constraint(a, pltpu.HBM) for a in (level_shift, source, potential)))
    return pl.pallas_call(
        add_fix,
        out_shape=jax.ShapeDtypeStruct(source.shape, F32),
        in_specs=[pl.BlockSpec(memory_space=pltpu.VMEM)] * 2,
        out_specs=pl.BlockSpec(memory_space=pltpu.HBM),
        scratch_shapes=[pltpu.VMEM((4, 256, 256), F32), dma((4,))],
        name="add_fix",
    )(*(pltpu.with_memory_space_constraint(a, pltpu.VMEM) for a in (raw, fix)))


def solution(mesh):
    in_specs = (P("tm", "plane", None, None), P("plane", None, None), P())
    out_specs = P("tm", "plane", None, None)
    return jax.shard_map(shards, mesh=mesh, in_specs=in_specs, out_specs=out_specs, check_vma=False)
```

```python
import math

import jax
import jax.numpy as jnp
from jax import lax
from jax.experimental import pallas as pl
from jax.experimental.pallas import tpu as pltpu
from jax.sharding import PartitionSpec as P

F32 = jnp.float32
MESH = pl.DeviceIdType.MESH
ROOT = 1.0 / math.sqrt(2.0)
OMEGA = 0.8
PLANES = (0, 3, 1, 2)
SLOT = {plane: slot for slot, plane in enumerate(PLANES)}


def dot(a, b):
    return jnp.dot(a, b, precision=lax.Precision.HIGHEST, preferred_element_type=F32)


def iota(shape, dim):
    return lax.broadcasted_iota(jnp.int32, shape, dim)


def ones_where(mask):
    return jnp.where(mask, 1.0, 0.0).astype(F32)


def beside_yz(ext):
    rows = ext.shape[0] - 16
    mid = ext[8 : 8 + rows]
    up = pltpu.roll(ext, 1, 0)[8 : 8 + rows]
    down = pltpu.roll(ext, rows + 15, 0)[8 : 8 + rows]
    col = iota(mid.shape, 1)
    left = jnp.where(col == 0, 0.0, pltpu.roll(mid, 1, 1))
    right = jnp.where(col == 255, 0.0, pltpu.roll(mid, 255, 1))
    return mid, (up + down) + (left + right)


def kernel(
    shift_hbm, source, potential, out, fix_out,
    shift_ref, own, other, pot, pot_other, s_buf, rd, fd, sd, strip, nb, raw, nstrip, u_buf, fv, rv, sv, ustrip, nu, nustrip, fu, ru,
    pot_side, wv, wu, base_v, base_u, hd, hv, hu, ub, ub_own, give, bk, gives, t_d, x_d, t_uv, x_uv, pot_all, d_sums, d_x, d_total, d_other, uv_sums, uv_x, uv_total,
    tr, blocks, pick, pick_d, fix_all, mine, yours,
    all_sent, h_sem, l_sem, p_sem, sent, ends, r_raw, r0, r1, r2, rt, ru_sem, rxp, rxd, rxv, rxu, rp, rdx, rdp, rc, rg, rb2, rb1,
):
    t, x = lax.axis_index("tm"), lax.axis_index("plane")
    e = t % 8
    k, c = e % 2, e // 2
    b, p = c % 2, c // 2
    partner = t + 1 - 2 * k
    near = t + 2 - 4 * b
    far = t + 4 - 8 * p
    x_peers = [(x + m) % 4 for m in (1, 2, 3)]
    group = [t - e + (e + m) % 8 for m in range(1, 8)]

    barrier = pltpu.get_barrier_semaphore()
    for peer in (far, near, near + 1 - 2 * k, partner):
        pl.semaphore_signal(barrier, inc=1, device_id=(peer, x), device_id_type=MESH)
    for peer in x_peers:
        pl.semaphore_signal(barrier, inc=1, device_id=(t, peer), device_id_type=MESH)

    def rows(start, count):
        return pl.ds(pl.multiple_of(start, 8), count)

    def remote(src, dst, recv, where):
        copy = pltpu.make_async_remote_copy(
            src_ref=src, dst_ref=dst, send_sem=sent, recv_sem=recv, device_id=where, device_id_type=MESH
        )
        copy.start()
        return copy

    def absorb(ref, sem):
        pltpu.make_async_copy(ref, ref, sem).wait()

    def local(src, dst, sem):
        copy = pltpu.make_async_copy(src, dst, sem)
        copy.start()
        return copy

    for slot, plane in enumerate(PLANES):
        local(source.at[0, plane, rows(120 * k, 136), :], own.at[slot, rows(8 - 8 * k, 136), :], l_sem)
    shift_load = local(shift_hbm, shift_ref, h_sem)
    for slot, plane in enumerate(PLANES):
        local(potential.at[plane, rows(120 * k, 136), :], pot.at[slot, rows(8 - 8 * k, 136), :], p_sem)
    local(potential.at[:, rows(128 - 128 * k, 128), :], pot_other, p_sem)
    for slot in range(4):
        for ref in (own, other, pot):
            ref[slot, rows(136 * k, 8), :] = jnp.zeros((8, 256), F32)

    pl.semaphore_wait(barrier, 7)

    first_rows = 64 - 64 * b + 32 - 32 * p
    remote(source.at[0, PLANES[0], rows(128 * k + first_rows, 32), :], raw.at[0], r_raw, (near, x))
    remote(source.at[0, PLANES[0], rows(128 - 128 * k + first_rows, 32), :], raw.at[1], r_raw, (near + 1 - 2 * k, x))
    for slot in (1, 0, 2, 3):
        remote(
            source.at[0, PLANES[slot], rows(120 - 120 * k, 136), :], other.at[slot, rows(8 * k, 136), :],
            r0.at[0 if slot == 1 else 1], (partner, x),
        )

    def to_side(src, halo, end, sem):
        @pl.when(x < 3 if end == 0 else x > 0)
        def _():
            remote(src, halo.at[end], sem.at[end], (t, x + 1 - 2 * end))

    def from_sides(halo, sem):
        for end in range(2):
            pl.when(x > 0 if end == 0 else x < 3)(lambda end=end: absorb(halo.at[end], sem.at[end]))

    for end in range(2):
        @pl.when(x == 3 * end)
        def _():
            hd[end] = jnp.zeros((128, 256), F32)
            hv[end] = jnp.zeros((64, 256), F32)
            hu[end] = jnp.zeros((2, 32, 256), F32)
            pot_side[end] = jnp.zeros((128, 256), F32)

    to_side(potential.at[0, rows(128 * k, 128), :], pot_side, 1, rxp)
    to_side(potential.at[3, rows(128 * k, 128), :], pot_side, 0, rxp)

    def to_near(index, slots, q, start=0, count=32):
        at = 32 * q + start
        firsts[index] = remote(
            s_buf.at[slots, rows(72 - 64 * b + at, count), :], nb.at[slots, rows(at, count), :],
            r1.at[min(index, 6) if index < 8 else 0], (near, x),
        )

    firsts = {}
    absorb(own.at[:, 0:136, :], l_sem)
    absorb(other.at[1, 0:136, :], r0.at[0])
    s_buf[1] = (own[1] + other[1]) * ROOT
    to_near(1, 1, 1 - p)
    absorb(other.at[0:3, 0:136, :], r0.at[1])
    for slot in (0, 2, 3):
        s_buf[slot] = (own[slot] + other[slot]) * ROOT
    for h in range(2):
        for i in range(4):
            for at, row in ((0, 7), (4, 40), (8, 39), (12, 72)):
                strip[h, at + i : at + i + 1, :] = s_buf[i, row + 64 * h : row + 64 * h + 1, :]
    strip_1 = remote(strip.at[1 - b], nstrip, rt, (near, x))
    to_near(2, 2, 1 - p)
    to_near(3, 3, 1 - p)

    sign = (1 - 2 * k).astype(F32)
    near_sign = (1 - 2 * b).astype(F32)
    far_sign = (1 - 2 * p).astype(F32)
    scale = ROOT * sign
    edge_low, edge_high = ones_where(x == 0), ones_where(x == 3)
    shift_load.wait()
    shift_0 = shift_ref[0]
    absorb(all_sent.at[0:1056, :], p_sem)
    for slot in range(4):
        rd[slot] = OMEGA / (6.0 + pot[slot] + shift_0)
        fd[slot] = (own[slot] - other[slot]) * scale * rd[slot]


    to_side(fd.at[0, 8:136, :], hd, 1, rxd)
    to_side(fd.at[1, 8:136, :], hd, 0, rxd)

    for slot in range(4):
        rv[slot] = OMEGA / (6.0 + pot[slot, rows(64 * b, 80), :] + shift_ref[1])
        here = 6.0 + pot[slot, rows(64 * b + 32 * p, 48), :]
        ru[0, slot] = OMEGA / (here + shift_ref[3])
        ru[1, slot] = OMEGA / (here + shift_ref[2])

    z_at, z_block = iota((256, 128), 0), iota((256, 128), 1)
    lane_block = ones_where(z_at // 8 == z_block % 32)
    row, col = iota((32, 128), 0), iota((32, 128), 1)
    pot_sum = (pot[0, 8:136, :] + pot[1, 8:136, :]) + (pot[2, 8:136, :] + pot[3, 8:136, :])
    pot_rest = (pot_other[0] + pot_other[1]) + (pot_other[2] + pot_other[3])
    pot_all[0] = dot(ones_where(col // 8 + 16 * k == row), dot(pot_sum, lane_block)) + dot(
        ones_where(col // 8 + 16 - 16 * k == row), dot(pot_rest, lane_block)
    )
    for m, peer in enumerate(x_peers):
        remote(pot_all.at[0], pot_all.at[m + 1], rp, (t, peer))
    block = ones_where(z_at // 8 == z_block)
    around = ones_where((z_at + 7) // 8 == z_block + 1) + ones_where((z_at + 1) // 8 == z_block)
    blocks[0] = block
    blocks[1] = jnp.where(z_block < 32, 2.0 * block + around, 0.0)

    row, col = iota((32, 64), 0), iota((32, 64), 1)
    sender, r = col // 8, col % 8
    sender_c = sender // 2
    sender_b, sender_p = sender_c % 2, sender_c // 2
    sender_at = 16 * (sender % 2) + 8 * sender_b - 1 + r
    pick[0] = ones_where((r < 6) & (sender_at + 4 * sender_p == row))
    pick[1] = ones_where((sender_p == p) & (sender_at == row))
    pick[2] = ones_where((sender_p == p) & (r < 2) & (sender_at + 8 == row))
    row, col = iota((32, 24), 0), iota((32, 24), 1)
    pick_d[0] = ones_where((col < 18) & (16 * k - 1 + col == row))
    pick_d[1] = ones_where((col < 18) & (16 * (1 - k) - 1 + col == row))

    def level_1(slot, q, start=0, count=32):
        inside = 32 * q + start
        here = s_buf[slot, rows(8 + 64 * b + inside, count), :]
        there = nb[slot, rows(inside, count), :]
        at = rows(8 + inside, count)
        u_buf[slot, at, :] = (here + there) * ROOT
        detail = (here - there) * (ROOT * near_sign)
        fv[slot, at, :] = detail * rv[slot, at, :]
        at = rows(inside, count)
        x_uv[at, :] = detail if slot == 0 else x_uv[at, :] + detail

    seconds = {}

    def to_far(index, slots, start=0, count=32):
        seconds[index] = remote(
            u_buf.at[slots, rows(40 - 32 * p + start, count), :], nu.at[slots, start : start + count, :],
            r2.at[index - index // 3], (far, x),
        )

    def passed_on(slot):
        if slot == 0:
            absorb(raw, r_raw)
            nb[0, rows(32 - 32 * p, 32), :] = (raw[0] + raw[1]) * ROOT
        else:
            firsts[slot].wait_recv()
        level_1(slot, 1 - p)
        to_far(slot, slot, 0, 32 if slot < 2 else 24)

    def level_2(slot, start=0, count=32):
        here = u_buf[slot, rows(8 + 32 * p + start, count), :]
        there = nu[slot, start : start + count, :]
        low, high = (here + there) * ROOT, (here - there) * (ROOT * far_sign)
        at = slice(8 + start, 8 + start + count)
        fu[0, slot, at, :] = low * ru[0, slot, at, :]
        fu[1, slot, at, :] = high * ru[1, slot, at, :]
        for first, field in ((64 + start, low), (96 + start, high)):
            at = slice(first, first + count)
            x_uv[at, :] = field if slot == 0 else x_uv[at, :] + field

    inner_slots = slice(2, 4)
    for slot in range(4):
        passed_on(slot)
        if slot < 2:
            to_near(4 + slot, slot, p)
        if slot == 0:
            strip_1.wait_recv()
            ustrip[...] = (strip[b] + nstrip[...]) * ROOT
            strip_2 = remote(ustrip.at[rows(8 - 8 * p, 8), :], nustrip, ru_sem, (far, x))
    to_near(6, 2, p, 0, 24)
    to_near(7, 3, p, 0, 24)
    to_far(4, inner_slots, 24, 8)
    to_near(8, inner_slots, p, 24, 8)
    details = (strip[b] - nstrip[...]) * (ROOT * near_sign)
    for slot in range(4):
        fv[slot, 7:8, :] = details[slot : slot + 1] * rv[slot, 7:8, :]
        fv[slot, 72:73, :] = details[12 + slot : 13 + slot] * rv[slot, 72:73, :]
        if slot > 1:
            fv[slot, 39:40, :] = details[8 + slot : 9 + slot] * rv[slot, 39:40, :]
    from_sides(pot_side, rxp)
    kept = [ones_where(x > 0), ones_where(x < 3)]

    def beside_weights(weight, start, count, shift, out):
        side = []
        for end in range(2):
            field = 6.0 + pot_side[end, rows(start, count), :] + shift
            side.append((OMEGA * kept[end]) / field)
        inner = [weight[SLOT[plane], 8 : 8 + count, :] for plane in range(4)]
        out[SLOT[0]] = side[0] + inner[1]
        out[SLOT[1]] = inner[0] + inner[2]
        out[SLOT[2]] = inner[1] + inner[3]
        out[SLOT[3]] = inner[2] + side[1]

    beside_weights(rv, 64 * b, 64, shift_ref[1], wv)
    for j, level in ((0, 3), (1, 2)):
        beside_weights(ru.at[j], 64 * b + 32 * p, 32, shift_ref[level], wu.at[j])

    for slot, end in ((0, 1), (1, 0)):
        firsts[4 + slot].wait_recv()
        level_1(slot, p)
        seconds[slot].wait_recv()
        level_2(slot)
        to_side(fu.at[:, slot, 8:40, :], hu, end, rxu)
        to_side(fv.at[slot, 8:72, :], hv, end, rxv)

    def second_pass(f, weight, low_rim, high_rim, at, count, order, done):
        center = rows(at + 8, count)
        total, outer = None, None
        for plane in order:
            slot = SLOT[plane]
            mid, beside = beside_yz(f[slot, rows(at, count + 16), :])
            low = f[SLOT[plane - 1], center, :] if plane > 0 else low_rim()
            high = f[SLOT[plane + 1], center, :] if plane < 3 else high_rim()
            second = 1.2 * mid + weight[slot, center, :] * (beside + (low + high))
            done(slot, second)
            q = second - OMEGA * mid
            total = q if total is None else total + q
            if plane in (0, 3):
                rim = q * (edge_low if plane == 0 else edge_high)
                outer = rim if outer is None else outer + rim
        return total, outer

    from_sides(hd, rxd)

    def odd_rows(step, _):
        at = 32 * step
        here = rows(at, 32)

        def done(slot, second):
            sd[slot, here, :] = second

        summed, outer = second_pass(
            fd, rd, lambda: hd[0, here, :], lambda: hd[1, here, :], at, 32, range(4), done
        )
        center = rows(at + 8, 32)
        waves = (own[0, center, :] - other[0, center, :]) + (own[1, center, :] - other[1, center, :])
        waves = waves + (own[2, center, :] - other[2, center, :]) + (own[3, center, :] - other[3, center, :])
        t_d[here, :] = summed
        x_d[here, :] = (0.04 * scale) * waves - outer
        return 0

    lax.fori_loop(0, 4, odd_rows, 0)
    y_at, y_row = iota((24, 128), 1), iota((24, 128), 0)
    inner = ones_where(y_at // 8 + 1 == y_row)
    beside = ones_where((y_at + 7) // 8 == y_row) + ones_where((y_at + 1) // 8 + 1 == y_row)
    sums = dot(inner, dot(x_d[...], blocks[0]) + dot(t_d[...], blocks[1])) + dot(beside, dot(t_d[...], blocks[0]))
    d_sums[...] = pltpu.roll(sums, 96, 1)
    for m, peer in enumerate(x_peers):
        remote(d_sums, d_x.at[m], rdx, (t, peer))

    strip_2.wait_recv()
    here = ustrip[rows(8 * p, 8), :]
    low, high = (here + nustrip[...]) * ROOT, (here - nustrip[...]) * (ROOT * far_sign)
    for slot in range(4):
        for j, rim in enumerate((low, high)):
            fu[j, slot, 7:8, :] = rim[slot : slot + 1] * ru[j, slot, 7:8, :]
            fu[j, slot, 40:41, :] = rim[4 + slot : 5 + slot] * ru[j, slot, 40:41, :]
    absorb(nu.at[2:4, 0:24, :], r2.at[2])
    absorb(nb.at[2:4, 0:24, :], r1.at[6])
    for slot in (2, 3):
        level_1(slot, p, 0, 24)
        level_2(slot, 0, 24)

    def own_planes(f, weight, sides, base, at, count, planes):
        here, center = rows(at, count), rows(at + 8, count)
        total, outer = None, None
        for plane in planes:
            slot = SLOT[plane]
            mid, beside = beside_yz(f[slot, rows(at, count + 16), :])
            within = weight[slot, center, :] * beside
            base[slot, here, :] = 1.2 * mid + within
            within = 0.4 * mid + within
            q = within + mid * sides[slot, here, :]
            total = q if total is None else total + q
            if plane in (0, 3):
                next_in = f[SLOT[1 if plane == 0 else 2], center, :]
                rim = (within + weight[slot, center, :] * next_in) * (edge_low if plane == 0 else edge_high)
                outer = rim if outer is None else outer + rim
        return total, outer

    def with_sides(f, weight, base, halo, at, count, plane):
        here, center = rows(at, count), rows(at + 8, count)
        low = f[SLOT[plane - 1], center, :] if plane > 0 else halo(0)
        high = f[SLOT[plane + 1], center, :] if plane < 3 else halo(1)
        return base[SLOT[plane], here, :] + weight[SLOT[plane], center, :] * (low + high)

    def near_planes(planes, start, count):
        def body(step, _):
            here = rows(32 * step + start, count)
            summed, outer = own_planes(fv, rv, wv, base_v, 32 * step + start, count, planes)
            if outer is None:
                t_uv[here, :] = summed
            else:
                t_uv[here, :] += summed
                x_uv[here, :] = 0.04 * x_uv[here, :] - outer
            return 0

        lax.fori_loop(0, 2, body, 0)

    def near_rows(planes, start, count):
        def body(step, _):
            here = rows(32 * step + start, count)
            for plane in planes:
                sv[SLOT[plane], here, :] = with_sides(
                    fv, rv, base_v, lambda end: hv[end, here, :], 32 * step + start, count, plane
                )
            return 0

        lax.fori_loop(0, 2, body, 0)

    def far_planes(planes, start, count):
        for j in range(2):
            at = slice(64 + 32 * j + start, 64 + 32 * j + start + count)
            summed, outer = own_planes(fu.at[j], ru.at[j], wu.at[j], base_u.at[j], start, count, planes)
            if outer is None:
                t_uv[at, :] = summed
            else:
                t_uv[at, :] += summed
                x_uv[at, :] = 0.04 * x_uv[at, :] - outer

    def far_rows(plane, start=0, count=32):
        here = slice(start, start + count)
        made = [
            with_sides(fu.at[j], ru.at[j], base_u.at[j], lambda end, j=j: hu[end, j, here, :], start, count, plane)
            for j in range(2)
        ]
        slot = SLOT[plane]
        low, high = made[0] * ROOT, made[1] * (ROOT * far_sign)
        give[slot, here, :] = low - high
        ub_own[slot, here, :] = low + high
        remote(give.at[slot, here, :], ub.at[slot, here, :], rb2.at[slot], (far, x))

    def join(slot, q, ref, start=0, count=32):
        at = 32 * q + start
        low = ref[slot, start : start + count, :] * ROOT
        high = sv[slot, rows(at, count), :] * (ROOT * near_sign)
        gives[slot, rows(at, count), :] = low - high
        bk[slot, rows(64 * b + at, count), :] = low + high
        remote(
            gives.at[slot, rows(at, count), :], bk.at[slot, rows(64 * b + at, count), :], rb1.at[4 if slot == 1 and ref is ub else slot], (near, x)
        )

    def rest(slot):
        absorb(ub.at[slot], rb2.at[slot])
        join(slot, 1 - p, ub)

    def inner_rows(start):
        far_planes((1, 2), start, 16)
        far_rows(1, start, 16)
        far_rows(2, start, 16)
        near_planes((1, 2), start, 16)
        near_rows((1, 2), start, 16)
        join(2, p, ub_own, start, 16)
        join(3, p, ub_own, start, 16)

    inner_rows(0)
    seconds[4].wait_recv()
    firsts[8].wait_recv()
    for slot in (2, 3):
        level_1(slot, p, 24, 8)
        level_2(slot, 24, 8)
    inner_rows(16)
    far_planes((0, 3), 0, 32)
    near_planes((0, 3), 0, 32)
    from_sides(hu, rxu)
    far_rows(0)
    far_rows(3)

    y_at, y_row = iota((32, 128), 1), iota((32, 128), 0)
    start = jnp.where(y_at < 64, 0, 16 + 8 * ((y_at - 64) // 32))
    y_in = jnp.where(y_at < 64, y_at, y_at % 32)
    inner = ones_where(start + y_in // 8 + 1 == y_row)
    beside = ones_where(start + (y_in + 7) // 8 == y_row) + ones_where(start + (y_in + 1) // 8 + 1 == y_row)
    sums = dot(inner, dot(x_uv[...], blocks[0]) + dot(t_uv[...], blocks[1])) + dot(beside, dot(t_uv[...], blocks[0]))
    uv_sums[...] = (sums[16:24] + pltpu.roll(sums[24:32], 32, 1)) + (
        pltpu.roll(sums[0:8], 64, 1) + pltpu.roll(sums[8:16], 96, 1)
    )
    for m, peer in enumerate(x_peers):
        remote(uv_sums, uv_x.at[m], rc, (t, peer))
    from_sides(hv, rxv)
    near_rows((0, 3), 0, 32)
    join(0, p, ub_own)
    join(1, p, ub_own)
    rest(2)
    absorb(uv_x, rc)
    uv_total[...] = (uv_sums[...] + uv_x[0]) + (uv_x[1] + uv_x[2])
    for peer in group:
        remote(uv_total, tr.at[e], rg, (peer, x))
    tr[e] = uv_total[...]
    rest(3)
    absorb(d_x, rdx)
    absorb(pot_all.at[1:4], rp)
    d_total[...] = (d_sums[...] + d_x[0]) + (d_x[1] + d_x[2])
    d_swap = remote(d_total, d_other, rdp, (partner, x))

    def finish(slot, start, count=64):
        here = rows(start, count)
        even, odd = bk[slot, here, :], sd[slot, here, :] * sign
        yours[slot, here, :] = (even - odd) * ROOT
        there = out.at[0, PLANES[slot], rows(128 * k + start, count), :]
        remote(yours.at[slot, here, :], there, ends, (partner, x))
        mine[slot, here, :] = (even + odd) * ROOT
        local(mine.at[slot, here, :], there, sent)

    rest(0)
    rest(1)
    for slot in (2, 3, 0, 1):
        finish(slot, 64 * b)

    def finish_far(slot):
        absorb(gives.at[slot], rb1.at[slot])
        finish(slot, 64 - 64 * b)

    for slot in (2, 3, 0):
        finish_far(slot)
    for q, index in ((p, 1), (1 - p, 4)):
        absorb(gives.at[1, 0:32, :], rb1.at[index])
        finish(1, 64 - 64 * b + 32 * q, 32)
    absorb(tr.at[0:7], rg)
    d_swap.wait_recv()

    lane = iota((32, 128), 1)
    coef = lane // 32
    gathered = tr[...].reshape(64, 128)
    rem_v = dot(pick[1], gathered) + pltpu.roll(dot(pick[2], gathered), 96, 1)
    rem_d = dot(pick_d[0], d_total[...]) + dot(pick_d[1], d_other[...])
    rem = jnp.where(coef < 2, dot(pick[0], gathered), jnp.where(coef == 2, rem_v, rem_d))
    shift = jnp.where(
        coef == 0, shift_ref[3], jnp.where(coef == 1, shift_ref[2], jnp.where(coef == 2, shift_ref[1], shift_0))
    )
    coarse_pot = (pot_all[0] + pot_all[1]) + (pot_all[2] + pot_all[3])
    diag = coarse_pot + shift * 1024.0 + 640.0
    one = rem / diag
    row = iota((32, 128), 0)
    up = jnp.where(row == 0, 0.0, pltpu.roll(one, 1, 0))
    down = jnp.where(row == 31, 0.0, pltpu.roll(one, 31, 0))
    left = jnp.where(lane % 32 == 0, 0.0, pltpu.roll(one, 1, 1))
    right = jnp.where(lane % 32 == 31, 0.0, pltpu.roll(one, 127, 1))
    applied = diag * one - 128.0 * ((up + down) + (left + right))
    fix = one + (rem - applied) / diag
    weight = jnp.where(
        coef == 0, 0.5 * ROOT, jnp.where(coef == 1, 0.5 * ROOT * far_sign, jnp.where(coef == 2, 0.5 * near_sign, scale))
    )
    widen = ones_where(iota((128, 256), 0) % 32 == iota((128, 256), 1) // 8)
    fix_all[...] = dot(fix * weight, widen)
    local(fix_all, fix_out, sent)

    outer = (x == 0) | (x == 3)
    pl.when(outer)(lambda: absorb(all_sent.at[0:2944, :], sent))
    pl.when(jnp.logical_not(outer))(lambda: absorb(all_sent, sent))
    absorb(yours, ends)


def add_fix(raw, fix, out, buffer, sems):
    copies = []
    for plane in range(4):
        for i in range(32):
            at = slice(8 * i, 8 * i + 8)
            buffer[plane, at, :] = raw[0, plane, at, :] + fix[i : i + 1, :]
        copy = pltpu.make_async_copy(buffer.at[plane], out.at[0, plane], sems.at[plane])
        copy.start()
        copies.append(copy)
    for copy in copies:
        copy.wait()


def shards(source, potential, level_shift):
    dma = pltpu.SemaphoreType.DMA
    vmem = lambda *shape: pltpu.VMEM(shape, F32)
    scratch = dict(
        shift_ref=pltpu.SMEM((4,), F32),
        own=vmem(4, 144, 256), other=vmem(4, 144, 256), pot=vmem(4, 144, 256), pot_other=vmem(4, 128, 256), s_buf=vmem(4, 144, 256),
        rd=vmem(4, 144, 256), fd=vmem(4, 144, 256), sd=vmem(4, 128, 256), strip=vmem(2, 16, 256),
        nb=vmem(4, 64, 256), raw=vmem(2, 32, 256), nstrip=vmem(16, 256), u_buf=vmem(4, 80, 256), fv=vmem(4, 80, 256), rv=vmem(4, 80, 256),
        sv=vmem(4, 64, 256), ustrip=vmem(16, 256), nu=vmem(4, 32, 256), nustrip=vmem(8, 256),
        fu=vmem(2, 4, 48, 256), ru=vmem(2, 4, 48, 256),
        pot_side=vmem(2, 128, 256), wv=vmem(4, 64, 256), wu=vmem(2, 4, 32, 256), base_v=vmem(4, 64, 256), base_u=vmem(2, 4, 32, 256),
        hd=vmem(2, 128, 256), hv=vmem(2, 64, 256), hu=vmem(2, 2, 32, 256),
        ub=vmem(4, 32, 256), ub_own=vmem(4, 32, 256), give=vmem(4, 32, 256), bk=vmem(4, 128, 256), gives=vmem(4, 64, 256),
        t_d=vmem(128, 256), x_d=vmem(128, 256), t_uv=vmem(128, 256), x_uv=vmem(128, 256),
        pot_all=vmem(4, 32, 128), d_sums=vmem(24, 128), d_x=vmem(3, 24, 128), d_total=vmem(24, 128),
        d_other=vmem(24, 128), uv_sums=vmem(8, 128), uv_x=vmem(3, 8, 128), uv_total=vmem(8, 128),
        tr=vmem(8, 8, 128), blocks=vmem(2, 256, 128), pick=vmem(3, 32, 64), pick_d=vmem(2, 32, 24),
        fix_all=vmem(32, 256), mine=vmem(4, 128, 256), yours=vmem(4, 128, 256),
        all_sent=vmem(3328, 256),
        h_sem=dma(()), l_sem=dma(()), p_sem=dma(()), sent=dma(()), ends=dma(()), r_raw=dma(()), r0=dma((2,)), r1=dma((7,)),
        r2=dma((4,)), rt=dma(()), ru_sem=dma(()), rxp=dma((2,)), rxd=dma((2,)), rxv=dma((2,)), rxu=dma((2,)), rp=dma(()), rdx=dma(()), rdp=dma(()), rc=dma(()),
        rg=dma(()), rb2=dma((4,)), rb1=dma((5,)),
    )
    raw, fix = pl.pallas_call(
        kernel,
        out_shape=(jax.ShapeDtypeStruct(source.shape, F32), jax.ShapeDtypeStruct((32, 256), F32)),
        in_specs=[
            pl.BlockSpec(memory_space=pltpu.HBM),
            pl.BlockSpec(memory_space=pltpu.HBM),
            pl.BlockSpec(memory_space=pltpu.HBM),
        ],
        out_specs=(pl.BlockSpec(memory_space=pl.ANY), pl.BlockSpec(memory_space=pl.ANY)),
        scratch_shapes=list(scratch.values()),
        compiler_params=pltpu.CompilerParams(
            collective_id=0, has_side_effects=True, vmem_limit_bytes=40 * 2**20
        ),
        name="space_time_apply",
    )(*(pltpu.with_memory_space_constraint(a, pltpu.HBM) for a in (level_shift, source, potential)))
    return pl.pallas_call(
        add_fix,
        out_shape=jax.ShapeDtypeStruct(source.shape, F32),
        in_specs=[pl.BlockSpec(memory_space=pltpu.VMEM)] * 2,
        out_specs=pl.BlockSpec(memory_space=pltpu.HBM),
        scratch_shapes=[pltpu.VMEM((4, 256, 256), F32), dma((4,))],
        name="add_fix",
    )(*(pltpu.with_memory_space_constraint(a, pltpu.VMEM) for a in (raw, fix)))


def solution(mesh):
    in_specs = (P("tm", "plane", None, None), P("plane", None, None), P())
    out_specs = P("tm", "plane", None, None)
    return jax.shard_map(shards, mesh=mesh, in_specs=in_specs, out_specs=out_specs, check_vma=False)
```

```python
import math

import jax
import jax.numpy as jnp
from jax import lax
from jax.experimental import pallas as pl
from jax.experimental.pallas import tpu as pltpu
from jax.sharding import PartitionSpec as P

F32 = jnp.float32
MESH = pl.DeviceIdType.MESH
ROOT = 1.0 / math.sqrt(2.0)
OMEGA = 0.8
PLANES = (0, 3, 1, 2)
SLOT = {plane: slot for slot, plane in enumerate(PLANES)}


def dot(a, b):
    return jnp.dot(a, b, precision=lax.Precision.HIGHEST, preferred_element_type=F32)


def iota(shape, dim):
    return lax.broadcasted_iota(jnp.int32, shape, dim)


def ones_where(mask):
    return jnp.where(mask, 1.0, 0.0).astype(F32)


def beside_yz(ext):
    rows = ext.shape[0] - 16
    mid = ext[8 : 8 + rows]
    up = pltpu.roll(ext, 1, 0)[8 : 8 + rows]
    down = pltpu.roll(ext, rows + 15, 0)[8 : 8 + rows]
    col = iota(mid.shape, 1)
    left = jnp.where(col == 0, 0.0, pltpu.roll(mid, 1, 1))
    right = jnp.where(col == 255, 0.0, pltpu.roll(mid, 255, 1))
    return mid, (up + down) + (left + right)


def kernel(
    shift_hbm, source, potential, out, fix_out,
    shift_ref, own, other, pot, pot_other, s_buf, rd, fd, sd, strip, nb, raw, nstrip, u_buf, fv, rv, sv, ustrip, nu, nustrip, fu, ru,
    pot_side, wv, wu, base_v, base_u, hd, hv, hu, ub, ub_own, give, bk, gives, t_d, x_d, t_uv, x_uv, pot_all, d_sums, d_x, d_total, d_other, uv_sums, uv_x, uv_total,
    tr, blocks, pick, pick_d, fix_all, mine, yours,
    all_sent, h_sem, l_sem, p_sem, sent, ends, r_raw, r0, r1, r2, rt, ru_sem, rxp, rxd, rxv, rxu, rp, rdx, rdp, rc, rg, rb2, rb1,
):
    t, x = lax.axis_index("tm"), lax.axis_index("plane")
    e = t % 8
    k, c = e % 2, e // 2
    b, p = c % 2, c // 2
    partner = t + 1 - 2 * k
    near = t + 2 - 4 * b
    far = t + 4 - 8 * p
    x_peers = [(x + m) % 4 for m in (1, 2, 3)]
    group = [t - e + (e + m) % 8 for m in range(1, 8)]

    barrier = pltpu.get_barrier_semaphore()
    for peer in (far, near, near + 1 - 2 * k, partner):
        pl.semaphore_signal(barrier, inc=1, device_id=(peer, x), device_id_type=MESH)
    for peer in x_peers:
        pl.semaphore_signal(barrier, inc=1, device_id=(t, peer), device_id_type=MESH)

    def rows(start, count):
        return pl.ds(pl.multiple_of(start, 8), count)

    def remote(src, dst, recv, where):
        copy = pltpu.make_async_remote_copy(
            src_ref=src, dst_ref=dst, send_sem=sent, recv_sem=recv, device_id=where, device_id_type=MESH
        )
        copy.start()
        return copy

    def absorb(ref, sem):
        pltpu.make_async_copy(ref, ref, sem).wait()

    def local(src, dst, sem):
        copy = pltpu.make_async_copy(src, dst, sem)
        copy.start()
        return copy

    for slot, plane in enumerate(PLANES):
        local(source.at[0, plane, rows(120 * k, 136), :], own.at[slot, rows(8 - 8 * k, 136), :], l_sem)
    shift_load = local(shift_hbm, shift_ref, h_sem)
    for slot, plane in enumerate(PLANES):
        local(potential.at[plane, rows(120 * k, 136), :], pot.at[slot, rows(8 - 8 * k, 136), :], p_sem)
    local(potential.at[:, rows(128 - 128 * k, 128), :], pot_other, p_sem)
    for slot in range(4):
        for ref in (own, other, pot):
            ref[slot, rows(136 * k, 8), :] = jnp.zeros((8, 256), F32)

    pl.semaphore_wait(barrier, 7)

    first_rows = 64 - 64 * b + 32 - 32 * p
    remote(source.at[0, PLANES[0], rows(128 * k + first_rows, 32), :], raw.at[0], r_raw, (near, x))
    remote(source.at[0, PLANES[0], rows(128 - 128 * k + first_rows, 32), :], raw.at[1], r_raw, (near + 1 - 2 * k, x))
    for slot in (1, 0, 2, 3):
        remote(
            source.at[0, PLANES[slot], rows(120 - 120 * k, 136), :], other.at[slot, rows(8 * k, 136), :],
            r0.at[0 if slot == 1 else 1], (partner, x),
        )

    def to_side(src, halo, end, sem):
        @pl.when(x < 3 if end == 0 else x > 0)
        def _():
            remote(src, halo.at[end], sem.at[end], (t, x + 1 - 2 * end))

    def from_sides(halo, sem):
        for end in range(2):
            pl.when(x > 0 if end == 0 else x < 3)(lambda end=end: absorb(halo.at[end], sem.at[end]))

    for end in range(2):
        @pl.when(x == 3 * end)
        def _():
            hd[end] = jnp.zeros((128, 256), F32)
            hv[end] = jnp.zeros((64, 256), F32)
            hu[end] = jnp.zeros((2, 32, 256), F32)
            pot_side[end] = jnp.zeros((128, 256), F32)

    to_side(potential.at[0, rows(128 * k, 128), :], pot_side, 1, rxp)
    to_side(potential.at[3, rows(128 * k, 128), :], pot_side, 0, rxp)

    def to_near(index, slots, q, start=0, count=32):
        at = 32 * q + start
        firsts[index] = remote(
            s_buf.at[slots, rows(72 - 64 * b + at, count), :], nb.at[slots, rows(at, count), :],
            r1.at[min(index, 6) if index < 8 else 0], (near, x),
        )

    firsts = {}
    absorb(own.at[:, 0:136, :], l_sem)
    absorb(other.at[1, 0:136, :], r0.at[0])
    s_buf[1] = (own[1] + other[1]) * ROOT
    to_near(1, 1, 1 - p)
    absorb(other.at[0:3, 0:136, :], r0.at[1])
    for slot in (0, 2, 3):
        s_buf[slot] = (own[slot] + other[slot]) * ROOT
    for h in range(2):
        for i in range(4):
            for at, row in ((0, 7), (4, 40), (8, 39), (12, 72)):
                strip[h, at + i : at + i + 1, :] = s_buf[i, row + 64 * h : row + 64 * h + 1, :]
    strip_1 = remote(strip.at[1 - b], nstrip, rt, (near, x))
    to_near(2, 2, 1 - p)
    to_near(3, 3, 1 - p)

    sign = (1 - 2 * k).astype(F32)
    near_sign = (1 - 2 * b).astype(F32)
    far_sign = (1 - 2 * p).astype(F32)
    scale = ROOT * sign
    edge_low, edge_high = ones_where(x == 0), ones_where(x == 3)
    shift_load.wait()
    shift_0 = shift_ref[0]
    absorb(all_sent.at[0:1056, :], p_sem)
    for slot in range(4):
        rd[slot] = OMEGA / (6.0 + pot[slot] + shift_0)
        fd[slot] = (own[slot] - other[slot]) * scale * rd[slot]


    to_side(fd.at[0, 8:136, :], hd, 1, rxd)
    to_side(fd.at[1, 8:136, :], hd, 0, rxd)

    for slot in range(4):
        rv[slot] = OMEGA / (6.0 + pot[slot, rows(64 * b, 80), :] + shift_ref[1])
        here = 6.0 + pot[slot, rows(64 * b + 32 * p, 48), :]
        ru[0, slot] = OMEGA / (here + shift_ref[3])
        ru[1, slot] = OMEGA / (here + shift_ref[2])

    z_at, z_block = iota((256, 128), 0), iota((256, 128), 1)
    lane_block = ones_where(z_at // 8 == z_block % 32)
    row, col = iota((32, 128), 0), iota((32, 128), 1)
    pot_sum = (pot[0, 8:136, :] + pot[1, 8:136, :]) + (pot[2, 8:136, :] + pot[3, 8:136, :])
    pot_rest = (pot_other[0] + pot_other[1]) + (pot_other[2] + pot_other[3])
    pot_all[0] = dot(ones_where(col // 8 + 16 * k == row), dot(pot_sum, lane_block)) + dot(
        ones_where(col // 8 + 16 - 16 * k == row), dot(pot_rest, lane_block)
    )
    for m, peer in enumerate(x_peers):
        remote(pot_all.at[0], pot_all.at[m + 1], rp, (t, peer))
    block = ones_where(z_at // 8 == z_block)
    around = ones_where((z_at + 7) // 8 == z_block + 1) + ones_where((z_at + 1) // 8 == z_block)
    blocks[0] = block
    blocks[1] = jnp.where(z_block < 32, 2.0 * block + around, 0.0)

    row, col = iota((32, 64), 0), iota((32, 64), 1)
    sender, r = col // 8, col % 8
    sender_c = sender // 2
    sender_b, sender_p = sender_c % 2, sender_c // 2
    sender_at = 16 * (sender % 2) + 8 * sender_b - 1 + r
    pick[0] = ones_where((r < 6) & (sender_at + 4 * sender_p == row))
    pick[1] = ones_where((sender_p == p) & (sender_at == row))
    pick[2] = ones_where((sender_p == p) & (r < 2) & (sender_at + 8 == row))
    row, col = iota((32, 24), 0), iota((32, 24), 1)
    pick_d[0] = ones_where((col < 18) & (16 * k - 1 + col == row))
    pick_d[1] = ones_where((col < 18) & (16 * (1 - k) - 1 + col == row))

    def level_1(slot, q, start=0, count=32):
        inside = 32 * q + start
        here = s_buf[slot, rows(8 + 64 * b + inside, count), :]
        there = nb[slot, rows(inside, count), :]
        at = rows(8 + inside, count)
        u_buf[slot, at, :] = (here + there) * ROOT
        detail = (here - there) * (ROOT * near_sign)
        fv[slot, at, :] = detail * rv[slot, at, :]
        at = rows(inside, count)
        x_uv[at, :] = detail if slot == 0 else x_uv[at, :] + detail

    seconds = {}

    def to_far(index, slots, start=0, count=32):
        seconds[index] = remote(
            u_buf.at[slots, rows(40 - 32 * p + start, count), :], nu.at[slots, start : start + count, :],
            r2.at[index - index // 3], (far, x),
        )

    def passed_on(slot):
        if slot == 0:
            absorb(raw, r_raw)
            nb[0, rows(32 - 32 * p, 32), :] = (raw[0] + raw[1]) * ROOT
        else:
            firsts[slot].wait_recv()
        level_1(slot, 1 - p)
        to_far(slot, slot, 0, 32 if slot < 2 else 24)

    def level_2(slot, start=0, count=32):
        here = u_buf[slot, rows(8 + 32 * p + start, count), :]
        there = nu[slot, start : start + count, :]
        low, high = (here + there) * ROOT, (here - there) * (ROOT * far_sign)
        at = slice(8 + start, 8 + start + count)
        fu[0, slot, at, :] = low * ru[0, slot, at, :]
        fu[1, slot, at, :] = high * ru[1, slot, at, :]
        for first, field in ((64 + start, low), (96 + start, high)):
            at = slice(first, first + count)
            x_uv[at, :] = field if slot == 0 else x_uv[at, :] + field

    inner_slots = slice(2, 4)
    for slot in range(4):
        passed_on(slot)
        if slot < 2:
            to_near(4 + slot, slot, p)
        if slot == 0:
            strip_1.wait_recv()
            ustrip[...] = (strip[b] + nstrip[...]) * ROOT
            strip_2 = remote(ustrip.at[rows(8 - 8 * p, 8), :], nustrip, ru_sem, (far, x))
    to_near(6, 2, p, 0, 24)
    to_near(7, 3, p, 0, 24)
    to_far(4, inner_slots, 24, 8)
    to_near(8, inner_slots, p, 24, 8)
    details = (strip[b] - nstrip[...]) * (ROOT * near_sign)
    for slot in range(4):
        fv[slot, 7:8, :] = details[slot : slot + 1] * rv[slot, 7:8, :]
        fv[slot, 72:73, :] = details[12 + slot : 13 + slot] * rv[slot, 72:73, :]
        if slot > 1:
            fv[slot, 39:40, :] = details[8 + slot : 9 + slot] * rv[slot, 39:40, :]
    from_sides(pot_side, rxp)
    kept = [ones_where(x > 0), ones_where(x < 3)]

    def beside_weights(weight, start, count, shift, out):
        side = []
        for end in range(2):
            field = 6.0 + pot_side[end, rows(start, count), :] + shift
            side.append((OMEGA * kept[end]) / field)
        inner = [weight[SLOT[plane], 8 : 8 + count, :] for plane in range(4)]
        out[SLOT[0]] = side[0] + inner[1]
        out[SLOT[1]] = inner[0] + inner[2]
        out[SLOT[2]] = inner[1] + inner[3]
        out[SLOT[3]] = inner[2] + side[1]

    beside_weights(rv, 64 * b, 64, shift_ref[1], wv)
    for j, level in ((0, 3), (1, 2)):
        beside_weights(ru.at[j], 64 * b + 32 * p, 32, shift_ref[level], wu.at[j])

    for slot, end in ((0, 1), (1, 0)):
        firsts[4 + slot].wait_recv()
        level_1(slot, p)
        seconds[slot].wait_recv()
        level_2(slot)
        to_side(fu.at[:, slot, 8:40, :], hu, end, rxu)
        to_side(fv.at[slot, 8:72, :], hv, end, rxv)

    def second_pass(f, weight, low_rim, high_rim, at, count, order, done):
        center = rows(at + 8, count)
        total, outer = None, None
        for plane in order:
            slot = SLOT[plane]
            mid, beside = beside_yz(f[slot, rows(at, count + 16), :])
            low = f[SLOT[plane - 1], center, :] if plane > 0 else low_rim()
            high = f[SLOT[plane + 1], center, :] if plane < 3 else high_rim()
            second = 1.2 * mid + weight[slot, center, :] * (beside + (low + high))
            done(slot, second)
            q = second - OMEGA * mid
            total = q if total is None else total + q
            if plane in (0, 3):
                rim = q * (edge_low if plane == 0 else edge_high)
                outer = rim if outer is None else outer + rim
        return total, outer

    from_sides(hd, rxd)

    def odd_rows(step, _):
        at = 32 * step
        here = rows(at, 32)

        def done(slot, second):
            sd[slot, here, :] = second

        summed, outer = second_pass(
            fd, rd, lambda: hd[0, here, :], lambda: hd[1, here, :], at, 32, range(4), done
        )
        center = rows(at + 8, 32)
        waves = (own[0, center, :] - other[0, center, :]) + (own[1, center, :] - other[1, center, :])
        waves = waves + (own[2, center, :] - other[2, center, :]) + (own[3, center, :] - other[3, center, :])
        t_d[here, :] = summed
        x_d[here, :] = (0.04 * scale) * waves - outer
        return 0

    lax.fori_loop(0, 4, odd_rows, 0)

    strip_2.wait_recv()
    here = ustrip[rows(8 * p, 8), :]
    low, high = (here + nustrip[...]) * ROOT, (here - nustrip[...]) * (ROOT * far_sign)
    for slot in range(4):
        for j, rim in enumerate((low, high)):
            fu[j, slot, 7:8, :] = rim[slot : slot + 1] * ru[j, slot, 7:8, :]
            fu[j, slot, 40:41, :] = rim[4 + slot : 5 + slot] * ru[j, slot, 40:41, :]
    absorb(nu.at[2:4, 0:24, :], r2.at[2])
    absorb(nb.at[2:4, 0:24, :], r1.at[6])
    for slot in (2, 3):
        level_1(slot, p, 0, 24)
        level_2(slot, 0, 24)

    def own_planes(f, weight, sides, base, at, count, planes):
        here, center = rows(at, count), rows(at + 8, count)
        total, outer = None, None
        for plane in planes:
            slot = SLOT[plane]
            mid, beside = beside_yz(f[slot, rows(at, count + 16), :])
            within = weight[slot, center, :] * beside
            base[slot, here, :] = 1.2 * mid + within
            within = 0.4 * mid + within
            q = within + mid * sides[slot, here, :]
            total = q if total is None else total + q
            if plane in (0, 3):
                next_in = f[SLOT[1 if plane == 0 else 2], center, :]
                rim = (within + weight[slot, center, :] * next_in) * (edge_low if plane == 0 else edge_high)
                outer = rim if outer is None else outer + rim
        return total, outer

    def with_sides(f, weight, base, halo, at, count, plane):
        here, center = rows(at, count), rows(at + 8, count)
        low = f[SLOT[plane - 1], center, :] if plane > 0 else halo(0)
        high = f[SLOT[plane + 1], center, :] if plane < 3 else halo(1)
        return base[SLOT[plane], here, :] + weight[SLOT[plane], center, :] * (low + high)

    def near_planes(planes, start, count):
        def body(step, _):
            here = rows(32 * step + start, count)
            summed, outer = own_planes(fv, rv, wv, base_v, 32 * step + start, count, planes)
            if outer is None:
                t_uv[here, :] = summed
            else:
                t_uv[here, :] += summed
                x_uv[here, :] = 0.04 * x_uv[here, :] - outer
            return 0

        lax.fori_loop(0, 2, body, 0)

    def near_rows(planes, start, count):
        def body(step, _):
            here = rows(32 * step + start, count)
            for plane in planes:
                sv[SLOT[plane], here, :] = with_sides(
                    fv, rv, base_v, lambda end: hv[end, here, :], 32 * step + start, count, plane
                )
            return 0

        lax.fori_loop(0, 2, body, 0)

    def far_planes(planes, start, count):
        for j in range(2):
            at = slice(64 + 32 * j + start, 64 + 32 * j + start + count)
            summed, outer = own_planes(fu.at[j], ru.at[j], wu.at[j], base_u.at[j], start, count, planes)
            if outer is None:
                t_uv[at, :] = summed
            else:
                t_uv[at, :] += summed
                x_uv[at, :] = 0.04 * x_uv[at, :] - outer

    def far_rows(plane, start=0, count=32):
        here = slice(start, start + count)
        made = [
            with_sides(fu.at[j], ru.at[j], base_u.at[j], lambda end, j=j: hu[end, j, here, :], start, count, plane)
            for j in range(2)
        ]
        slot = SLOT[plane]
        low, high = made[0] * ROOT, made[1] * (ROOT * far_sign)
        give[slot, here, :] = low - high
        ub_own[slot, here, :] = low + high
        remote(give.at[slot, here, :], ub.at[slot, here, :], rb2.at[slot], (far, x))

    def join(slot, q, ref, start=0, count=32):
        at = 32 * q + start
        low = ref[slot, start : start + count, :] * ROOT
        high = sv[slot, rows(at, count), :] * (ROOT * near_sign)
        gives[slot, rows(at, count), :] = low - high
        bk[slot, rows(64 * b + at, count), :] = low + high
        remote(
            gives.at[slot, rows(at, count), :], bk.at[slot, rows(64 * b + at, count), :], rb1.at[4 if slot == 1 and ref is ub else slot], (near, x)
        )

    def rest(slot):
        absorb(ub.at[slot], rb2.at[slot])
        join(slot, 1 - p, ub)

    def inner_rows(start):
        far_planes((1, 2), start, 16)
        far_rows(1, start, 16)
        far_rows(2, start, 16)
        near_planes((1, 2), start, 16)
        near_rows((1, 2), start, 16)
        join(2, p, ub_own, start, 16)
        join(3, p, ub_own, start, 16)

    inner_rows(0)
    seconds[4].wait_recv()
    firsts[8].wait_recv()
    for slot in (2, 3):
        level_1(slot, p, 24, 8)
        level_2(slot, 24, 8)
    inner_rows(16)
    far_planes((0, 3), 0, 32)
    near_planes((0, 3), 0, 32)
    from_sides(hu, rxu)
    far_rows(0)
    far_rows(3)

    y_at, y_row = iota((32, 128), 1), iota((32, 128), 0)
    start = jnp.where(y_at < 64, 0, 16 + 8 * ((y_at - 64) // 32))
    y_in = jnp.where(y_at < 64, y_at, y_at % 32)
    inner = ones_where(start + y_in // 8 + 1 == y_row)
    beside = ones_where(start + (y_in + 7) // 8 == y_row) + ones_where(start + (y_in + 1) // 8 + 1 == y_row)
    sums = dot(inner, dot(x_uv[...], blocks[0]) + dot(t_uv[...], blocks[1])) + dot(beside, dot(t_uv[...], blocks[0]))
    uv_sums[...] = (sums[16:24] + pltpu.roll(sums[24:32], 32, 1)) + (
        pltpu.roll(sums[0:8], 64, 1) + pltpu.roll(sums[8:16], 96, 1)
    )
    for m, peer in enumerate(x_peers):
        remote(uv_sums, uv_x.at[m], rc, (t, peer))
    from_sides(hv, rxv)
    near_rows((0, 3), 0, 32)
    join(0, p, ub_own)
    join(1, p, ub_own)
    y_at, y_row = iota((24, 128), 1), iota((24, 128), 0)
    inner = ones_where(y_at // 8 + 1 == y_row)
    beside = ones_where((y_at + 7) // 8 == y_row) + ones_where((y_at + 1) // 8 + 1 == y_row)
    sums = dot(inner, dot(x_d[...], blocks[0]) + dot(t_d[...], blocks[1])) + dot(beside, dot(t_d[...], blocks[0]))
    d_sums[...] = pltpu.roll(sums, 96, 1)
    for m, peer in enumerate(x_peers):
        remote(d_sums, d_x.at[m], rdx, (t, peer))
    rest(2)
    absorb(uv_x, rc)
    uv_total[...] = (uv_sums[...] + uv_x[0]) + (uv_x[1] + uv_x[2])
    for peer in group:
        remote(uv_total, tr.at[e], rg, (peer, x))
    tr[e] = uv_total[...]
    rest(3)
    absorb(d_x, rdx)
    absorb(pot_all.at[1:4], rp)
    d_total[...] = (d_sums[...] + d_x[0]) + (d_x[1] + d_x[2])
    d_swap = remote(d_total, d_other, rdp, (partner, x))

    def finish(slot, start, count=64):
        here = rows(start, count)
        even, odd = bk[slot, here, :], sd[slot, here, :] * sign
        yours[slot, here, :] = (even - odd) * ROOT
        there = out.at[0, PLANES[slot], rows(128 * k + start, count), :]
        remote(yours.at[slot, here, :], there, ends, (partner, x))
        mine[slot, here, :] = (even + odd) * ROOT
        local(mine.at[slot, here, :], there, sent)

    rest(0)
    rest(1)
    for slot in (2, 3, 0, 1):
        finish(slot, 64 * b)

    def finish_far(slot):
        absorb(gives.at[slot], rb1.at[slot])
        finish(slot, 64 - 64 * b)

    for slot in (2, 3, 0):
        finish_far(slot)
    for q, index in ((p, 1), (1 - p, 4)):
        absorb(gives.at[1, 0:32, :], rb1.at[index])
        finish(1, 64 - 64 * b + 32 * q, 32)
    absorb(tr.at[0:7], rg)
    d_swap.wait_recv()

    lane = iota((32, 128), 1)
    coef = lane // 32
    gathered = tr[...].reshape(64, 128)
    rem_v = dot(pick[1], gathered) + pltpu.roll(dot(pick[2], gathered), 96, 1)
    rem_d = dot(pick_d[0], d_total[...]) + dot(pick_d[1], d_other[...])
    rem = jnp.where(coef < 2, dot(pick[0], gathered), jnp.where(coef == 2, rem_v, rem_d))
    shift = jnp.where(
        coef == 0, shift_ref[3], jnp.where(coef == 1, shift_ref[2], jnp.where(coef == 2, shift_ref[1], shift_0))
    )
    coarse_pot = (pot_all[0] + pot_all[1]) + (pot_all[2] + pot_all[3])
    diag = coarse_pot + shift * 1024.0 + 640.0
    one = rem / diag
    row = iota((32, 128), 0)
    up = jnp.where(row == 0, 0.0, pltpu.roll(one, 1, 0))
    down = jnp.where(row == 31, 0.0, pltpu.roll(one, 31, 0))
    left = jnp.where(lane % 32 == 0, 0.0, pltpu.roll(one, 1, 1))
    right = jnp.where(lane % 32 == 31, 0.0, pltpu.roll(one, 127, 1))
    applied = diag * one - 128.0 * ((up + down) + (left + right))
    fix = one + (rem - applied) / diag
    weight = jnp.where(
        coef == 0, 0.5 * ROOT, jnp.where(coef == 1, 0.5 * ROOT * far_sign, jnp.where(coef == 2, 0.5 * near_sign, scale))
    )
    widen = ones_where(iota((128, 256), 0) % 32 == iota((128, 256), 1) // 8)
    fix_all[...] = dot(fix * weight, widen)
    local(fix_all, fix_out, sent)

    outer = (x == 0) | (x == 3)
    pl.when(outer)(lambda: absorb(all_sent.at[0:2944, :], sent))
    pl.when(jnp.logical_not(outer))(lambda: absorb(all_sent, sent))
    absorb(yours, ends)


def add_fix(raw, fix, out, buffer, sems):
    copies = []
    for plane in range(4):
        for i in range(32):
            at = slice(8 * i, 8 * i + 8)
            buffer[plane, at, :] = raw[0, plane, at, :] + fix[i : i + 1, :]
        copy = pltpu.make_async_copy(buffer.at[plane], out.at[0, plane], sems.at[plane])
        copy.start()
        copies.append(copy)
    for copy in copies:
        copy.wait()


def shards(source, potential, level_shift):
    dma = pltpu.SemaphoreType.DMA
    vmem = lambda *shape: pltpu.VMEM(shape, F32)
    scratch = dict(
        shift_ref=pltpu.SMEM((4,), F32),
        own=vmem(4, 144, 256), other=vmem(4, 144, 256), pot=vmem(4, 144, 256), pot_other=vmem(4, 128, 256), s_buf=vmem(4, 144, 256),
        rd=vmem(4, 144, 256), fd=vmem(4, 144, 256), sd=vmem(4, 128, 256), strip=vmem(2, 16, 256),
        nb=vmem(4, 64, 256), raw=vmem(2, 32, 256), nstrip=vmem(16, 256), u_buf=vmem(4, 80, 256), fv=vmem(4, 80, 256), rv=vmem(4, 80, 256),
        sv=vmem(4, 64, 256), ustrip=vmem(16, 256), nu=vmem(4, 32, 256), nustrip=vmem(8, 256),
        fu=vmem(2, 4, 48, 256), ru=vmem(2, 4, 48, 256),
        pot_side=vmem(2, 128, 256), wv=vmem(4, 64, 256), wu=vmem(2, 4, 32, 256), base_v=vmem(4, 64, 256), base_u=vmem(2, 4, 32, 256),
        hd=vmem(2, 128, 256), hv=vmem(2, 64, 256), hu=vmem(2, 2, 32, 256),
        ub=vmem(4, 32, 256), ub_own=vmem(4, 32, 256), give=vmem(4, 32, 256), bk=vmem(4, 128, 256), gives=vmem(4, 64, 256),
        t_d=vmem(128, 256), x_d=vmem(128, 256), t_uv=vmem(128, 256), x_uv=vmem(128, 256),
        pot_all=vmem(4, 32, 128), d_sums=vmem(24, 128), d_x=vmem(3, 24, 128), d_total=vmem(24, 128),
        d_other=vmem(24, 128), uv_sums=vmem(8, 128), uv_x=vmem(3, 8, 128), uv_total=vmem(8, 128),
        tr=vmem(8, 8, 128), blocks=vmem(2, 256, 128), pick=vmem(3, 32, 64), pick_d=vmem(2, 32, 24),
        fix_all=vmem(32, 256), mine=vmem(4, 128, 256), yours=vmem(4, 128, 256),
        all_sent=vmem(3328, 256),
        h_sem=dma(()), l_sem=dma(()), p_sem=dma(()), sent=dma(()), ends=dma(()), r_raw=dma(()), r0=dma((2,)), r1=dma((7,)),
        r2=dma((4,)), rt=dma(()), ru_sem=dma(()), rxp=dma((2,)), rxd=dma((2,)), rxv=dma((2,)), rxu=dma((2,)), rp=dma(()), rdx=dma(()), rdp=dma(()), rc=dma(()),
        rg=dma(()), rb2=dma((4,)), rb1=dma((5,)),
    )
    raw, fix = pl.pallas_call(
        kernel,
        out_shape=(jax.ShapeDtypeStruct(source.shape, F32), jax.ShapeDtypeStruct((32, 256), F32)),
        in_specs=[
            pl.BlockSpec(memory_space=pltpu.HBM),
            pl.BlockSpec(memory_space=pltpu.HBM),
            pl.BlockSpec(memory_space=pltpu.HBM),
        ],
        out_specs=(pl.BlockSpec(memory_space=pl.ANY), pl.BlockSpec(memory_space=pl.ANY)),
        scratch_shapes=list(scratch.values()),
        compiler_params=pltpu.CompilerParams(
            collective_id=0, has_side_effects=True, vmem_limit_bytes=40 * 2**20
        ),
        name="space_time_apply",
    )(*(pltpu.with_memory_space_constraint(a, pltpu.HBM) for a in (level_shift, source, potential)))
    return pl.pallas_call(
        add_fix,
        out_shape=jax.ShapeDtypeStruct(source.shape, F32),
        in_specs=[pl.BlockSpec(memory_space=pltpu.VMEM)] * 2,
        out_specs=pl.BlockSpec(memory_space=pltpu.HBM),
        scratch_shapes=[pltpu.VMEM((4, 256, 256), F32), dma((4,))],
        name="add_fix",
    )(*(pltpu.with_memory_space_constraint(a, pltpu.VMEM) for a in (raw, fix)))


def solution(mesh):
    in_specs = (P("tm", "plane", None, None), P("plane", None, None), P())
    out_specs = P("tm", "plane", None, None)
    return jax.shard_map(shards, mesh=mesh, in_specs=in_specs, out_specs=out_specs, check_vma=False)
```
